256 devices in a mesh: layer: 32 (over x, y, core), dp: 8 (over z).
Axes of the slice: x: 4, y: 4, z: 8, core: 2. Of those that a mesh axis runs over, the one named last changes fastest.
Arguments:
- initial: float32 [512, 1024], P('dp'), may hold values from -6 to 6
- norm_gains: float32 [32, 1024], P('layer'), may hold values from 0.25 to 1.75
- first_weights: bfloat16 [32, 1024, 2048], P('layer'), may hold values from -0.1875 to 0.1875
- second_weights: bfloat16 [32, 2048, 1024], P('layer'), may hold values from -0.046875 to 0.046875
Outputs:
- layer_states: float32 [32, 512, 1024], P('layer', 'dp')
- residual_ratios: float32 [7], replicated
- coarse_defects_four: float32 [32, 512, 1024], P('layer', 'dp')
- coarse_defects_sixteen: float32 [32, 512, 1024], P('layer', 'dp')
The draws below stay inside these ranges and needn't reach their ends.
All inputs are finite; a program needn't handle non-finite values.
Results may differ from the reference program's by a relative error of at most 0.02.
Values sent between devices are 32-bit elements; how exact they have to be, the bound alone decides.
No kernel may reach another device: no remote copies, remote signals or barrier semaphores. Data moves between devices by JAX's collectives and lax.ppermute only.
A program may use at most 64 MiB of HBM per device.

```python
import jax
import jax.numpy as jnp
from jax import lax

D = 1024
FF = 2048
LAYERS = 32
TOKENS = 512


def steps_of(own_key, shape, cuts, least, high):
    level, own = 1.0, jax.random.fold_in(own_key, 6)
    for position, parts in cuts:
        steps = jnp.exp(jax.random.uniform(jax.random.fold_in(own, position), (parts,), jnp.float32, least / len(cuts), high / len(cuts)))
        level = level * jnp.repeat(steps, shape[position] // parts).reshape([-1 if axis == position else 1 for axis in range(len(shape))])
    return level


def noise(own_key, shape, scale, bound, cuts=(), kind=jnp.bfloat16):
    result = jax.random.normal(own_key, shape, jnp.float32) * scale
    if len(cuts) > 0:
        result = steps_of(own_key, shape, cuts, -0.22, 0.18) * result
    return jnp.clip(result, min=-bound, max=bound).astype(kind)


def setup_inputs(seed: int = 0) -> dict:
    key_of = jax.random.split(jax.random.key(seed), 5)
    initial = noise(key_of[0], (TOKENS, D), 1.0, 6.0, ((0, 8),), jnp.float32)
    norm_gains = jnp.clip(1.0 + 0.15 * jax.random.normal(key_of[1], (LAYERS, D), jnp.float32), 0.25, 1.75)
    first_weights = noise(key_of[2], (LAYERS, D, FF), D ** -0.5, 0.1875, ((0, 32),))
    second_weights = noise(key_of[3], (LAYERS, FF, D), (7 * FF) ** -0.5, 0.046875, ((0, 32),))
    return {"initial": initial, "norm_gains": norm_gains, "first_weights": first_weights, "second_weights": second_weights}


epsilon = 1e-06

def branch(row_block, weight_in, weight_out, gain_row):
    mean_square = lax.optimization_barrier(jnp.mean(row_block * row_block, axis=-1, keepdims=True))
    normed = (row_block * lax.rsqrt(mean_square + epsilon) * gain_row).astype(jnp.bfloat16)
    hidden = jax.nn.gelu(jnp.dot(normed, weight_in, preferred_element_type=jnp.float32), approximate=True).astype(jnp.bfloat16)
    return jnp.dot(hidden, weight_out, preferred_element_type=jnp.float32)

def reference(initial, norm_gains, first_weights, second_weights):
    layer_total = LAYERS
    history = [initial] * (layer_total + 1)

    def propagate(point, values, spacing):
        return values + spacing * branch(values, first_weights[point - 1], second_weights[point - 1], norm_gains[point - 1])

    def relaxation(spacing, residues, right_side):
        for residue in residues:
            for point in range(spacing, layer_total + 1, spacing):
                if point % (4 * spacing) == residue:
                    updated = propagate(point, history[point - spacing], spacing)
                    if right_side is not None:
                        updated = updated + right_side[point]
                    history[point] = updated

    def restrict(spacing, right_side):
        coarse = {}
        gap_sums = []
        step_sums = []
        for point in range(4 * spacing, layer_total + 1, 4 * spacing):
            before = history[point - spacing]
            update = branch(before, first_weights[point - 1], second_weights[point - 1], norm_gains[point - 1])
            fine_value = before + spacing * update
            if right_side is not None:
                fine_value = fine_value + right_side[point]
            coarse[point] = fine_value - propagate(point, history[point - 4 * spacing], 4 * spacing)
            gap = fine_value - history[point]
            gap_sums.append(jnp.sum(gap * gap))
            step_sums.append(jnp.sum(update * update))
        return (coarse, gap_sums, step_sums)

    def defects(spacing):
        rows = []
        for point in range(1, layer_total + 1):
            if point >= spacing:
                rows.append(history[point] - propagate(point, history[point - spacing], spacing))
            else:
                rows.append(jnp.zeros_like(initial))
        return jnp.stack(rows)
    relaxation(1, (1, 2, 3), None)
    relaxation(1, (0,), None)
    relaxation(1, (1, 2, 3), None)
    rhs_one, gap_sums, step_sums = restrict(1, None)
    relaxation(4, (4, 8, 12), rhs_one)
    rhs_two, unused_gaps, unused_steps = restrict(4, rhs_one)
    for point in range(16, layer_total + 1, 16):
        history[point] = propagate(point, history[point - 16], 16) + rhs_two[point]
    relaxation(4, (4, 8, 12), rhs_one)
    relaxation(1, (1, 2, 3), None)
    layer_states = jnp.stack(history[1:])
    residual_ratios = jnp.sqrt(jnp.stack(gap_sums[1:]) / (jnp.stack(step_sums[1:]) + epsilon))
    defects_four = defects(4)
    defects_sixteen = defects(16)
    return (layer_states, residual_ratios, defects_four, defects_sixteen)
```

```python
import functools

import jax
import jax.numpy as jnp
from jax import lax
from jax.experimental import pallas as pl
from jax.experimental.pallas import tpu as pltpu
from jax.sharding import PartitionSpec as P

epsilon = 1e-06
PORTIONS = 2
CHUNK = 1024

FINE, LEVEL, GAP_FOUR, GAP_SIXTEEN, RESTRICT, COARSEST = 1, 2, 3, 4, 5, 6
SPACING = {FINE: 1.0, LEVEL: 4.0, GAP_FOUR: 4.0, GAP_SIXTEEN: 16.0, RESTRICT: 1.0, COARSEST: 16.0}


def plan(layers):
    rounds = []

    def every(residue, shift, job, least=1):
        return [
            (n, n + shift, job)
            for n in range(least, layers - shift + 1)
            if n % 4 == residue
        ]

    rounds.append(every(1, 1, FINE))
    rounds.append(every(2, 1, FINE))
    rounds.append(every(3, 1, FINE))
    rounds.append(every(0, 1, FINE))
    rounds.append(every(0, 4, GAP_FOUR))
    rounds.append(every(1, 1, FINE) + [(16, 32, GAP_SIXTEEN)])
    rounds.append(every(2, 1, FINE))
    rounds.append(every(3, 1, RESTRICT))
    restricted = len(rounds) - 1
    rounds.append([(8, 12, LEVEL), (20, 24, LEVEL)])
    rounds.append([(12, 16, LEVEL), (24, 28, LEVEL)])
    rounds.append([(16, 20, LEVEL), (28, 32, LEVEL)])
    rounds.append([(20, 24, LEVEL), (16, 32, COARSEST)])
    rounds.append([(24, 28, LEVEL)])
    rounds.append([(24, 25, FINE)])
    rounds.append([(28, 29, FINE), (25, 26, FINE)])
    rounds.append([(29, 30, FINE), (26, 27, FINE), (28, 32, GAP_FOUR)])
    rounds.append([(27, 31, GAP_FOUR)])
    rounds.append([(30, 31, FINE)])

    final = {1: -1, 2: 0, 3: 1, 4: 2, 5: 3, 6: 5, 7: 6, 8: 7}
    final.update({12: 8, 16: 9, 20: 10, 24: 11, 28: 12, 32: 11, 25: 13, 26: 14, 27: 15, 29: 14, 30: 15, 31: 17})

    def place(source, target, job, not_before=0):
        index = max(final[source] + 1, not_before)
        while index < len(rounds):
            used = rounds[index]
            if all(a != source and b != target for a, b, unused in used):
                used.append((source, target, job))
                return index
            index += 1
        rounds.append([(source, target, job)])
        return index

    for anchor in (8, 12, 16, 20):
        for n in (anchor + 1, anchor + 2, anchor + 3):
            final[n] = place(n - 1, n, FINE, restricted + 1)
    wanted = []
    for n in range(5, layers + 1):
        if n % 4 != 0 and n != 31:
            wanted.append((final[n - 4], n - 4, n, GAP_FOUR))
    for n in range(17, layers):
        wanted.append((final[n - 16], n - 16, n, GAP_SIXTEEN))
    for unused, source, target, job in sorted(wanted):
        place(source, target, job, 4)
    return rounds, restricted


def branch(state, gain_ref, first_ref, second_ref):
    mean_square = jnp.mean(state * state, axis=-1, keepdims=True)
    normed = (state * lax.rsqrt(mean_square + epsilon) * gain_ref[...]).astype(jnp.bfloat16)
    total = None
    for start in range(0, first_ref.shape[1], CHUNK):
        hidden = jax.nn.gelu(
            jnp.dot(normed, first_ref[:, start : start + CHUNK], preferred_element_type=jnp.float32),
            approximate=True,
        ).astype(jnp.bfloat16)
        part = jnp.dot(hidden, second_ref[start : start + CHUNK, :], preferred_element_type=jnp.float32)
        total = part if total is None else total + part
    return total


WHOLE = pl.BlockSpec(memory_space=pltpu.VMEM)
ANYWHERE = pl.BlockSpec(memory_space=pl.ANY)


def settings(rows):
    return dict(
        compiler_params=pltpu.CompilerParams(vmem_limit_bytes=16 * 2**20),
        cost_estimate=pl.CostEstimate(flops=4 * rows * 1024 * 2048 * 4, bytes_accessed=2**20, transcendentals=0),
    )


def first_kernel(state_ref, gain_ref, first_ref, second_ref, dep_ref, current_ref, four_ref, sixteen_ref):
    state = state_ref[...]
    update = branch(state, gain_ref, first_ref, second_ref)
    current_ref[...] = state + update
    four_ref[...] = state + 4.0 * update
    sixteen_ref[...] = state + 16.0 * update


def first_round(state, layer, dep):
    shape = jax.ShapeDtypeStruct(state.shape, jnp.float32)
    return pl.pallas_call(
        first_kernel,
        out_shape=(shape, shape, shape),
        in_specs=[WHOLE] * 4 + [ANYWHERE],
        out_specs=(WHOLE, WHOLE, WHOLE),
        **settings(state.shape[0]),
    )(state, *layer, dep)


def round_kernel(jobs, names_in, names_out, *refs):
    given = dict(zip(names_in, refs))
    made = dict(zip(names_out, refs[len(names_in) :]))
    update_ref = refs[-1]
    place = lax.axis_index("layer")

    def among(points):
        mask = 0
        for n in points:
            mask |= 1 << (n - 1)
        if mask >= 2**31:
            mask -= 2**32
        return (lax.shift_right_logical(jnp.int32(mask), place.astype(jnp.int32)) & 1) == 1

    busy = among([n for points in jobs.values() for n in points])

    @pl.when(busy)
    def compute():
        update_ref[...] = branch(given["arrived"][...], given["gain"], given["first"], given["second"])

    changing = [n for job, points in jobs.items() if job not in (GAP_FOUR, GAP_SIXTEEN) for n in points]
    if changing:

        @pl.when(jnp.logical_not(among(changing)))
        def keep():
            made["current"][...] = given["current"][...]

    if RESTRICT in jobs:
        made["sums"][...] = jnp.zeros(made["sums"].shape, jnp.float32)

    for job, points in jobs.items():

        @pl.when(among(points))
        def finish(job=job):
            stepped = given["arrived"][...] + SPACING[job] * update_ref[...]
            if job == FINE:
                made["current"][...] = stepped
            if job == LEVEL:
                made["four"][...] = stepped
                made["current"][...] = stepped + given["coarse"][...]
            if job == GAP_FOUR:
                made["four"][...] = stepped
            if job == GAP_SIXTEEN:
                made["sixteen"][...] = stepped
            if job == COARSEST:
                made["current"][...] = given["current"][...] + (stepped - given["sixteen"][...])
                made["sixteen"][...] = stepped
            if job == RESTRICT:
                gap = stepped - given["current"][...]
                update = update_ref[...]
                made["current"][...] = stepped
                made["coarse"][...] = stepped - given["four"][...]
                shape = made["sums"].shape
                row = lax.broadcasted_iota(jnp.int32, shape, 0)
                here = lax.broadcasted_iota(jnp.int32, shape, 1) == (place + 1) // 4 - 2
                both = jnp.where(row == 0, jnp.sum(gap * gap), jnp.sum(update * update))
                made["sums"][...] = jnp.where(here & (row < 2), both, 0.0)


def run_round(arrived, state, layer, pairs, dep):
    jobs = {}
    for unused, target, job in pairs:
        jobs.setdefault(job, []).append(target)
    kinds = set(jobs)
    names_in = ["arrived", "gain", "first", "second", "dep"]
    values = [arrived, *layer, dep]
    names_out, aliases = [], {}
    block = jax.ShapeDtypeStruct(arrived.shape, jnp.float32)
    shapes = []
    if kinds - {GAP_FOUR, GAP_SIXTEEN}:
        names_in.append("current")
        values.append(state["current"])
        names_out.append("current")
        shapes.append(block)
    for name, readers, writers in (
        ("four", {RESTRICT}, {LEVEL, GAP_FOUR}),
        ("sixteen", {COARSEST}, {GAP_SIXTEEN, COARSEST}),
        ("coarse", {LEVEL}, {RESTRICT}),
    ):
        if kinds & writers:
            if name in state:
                aliases[len(names_in)] = len(names_out)
            names_out.append(name)
            shapes.append(block)
        if name in state and kinds & (readers | writers):
            names_in.append(name)
            values.append(state[name])
    if RESTRICT in kinds:
        names_out.append("sums")
        shapes.append(jax.ShapeDtypeStruct((8, 128), jnp.float32))
    made = pl.pallas_call(
        functools.partial(round_kernel, jobs, names_in, names_out),
        out_shape=tuple(shapes),
        in_specs=[ANYWHERE if name == "dep" else WHOLE for name in names_in],
        out_specs=(WHOLE,) * len(shapes),
        scratch_shapes=[pltpu.VMEM(arrived.shape, jnp.float32)],
        input_output_aliases=aliases,
        **settings(arrived.shape[0]),
    )(*values)
    result = dict(state)
    result.update(zip(names_out, made))
    return result, made[0]


def sum_kernel(held_ref, arrived_ref, dep_ref, result_ref):
    result_ref[...] = held_ref[...] + arrived_ref[...]


def add(held, arrived, dep):
    return pl.pallas_call(
        sum_kernel,
        out_shape=jax.ShapeDtypeStruct(held.shape, jnp.float32),
        in_specs=[WHOLE, WHOLE, ANYWHERE],
        out_specs=WHOLE,
    )(held, arrived, dep)


def local(initial, norm_gains, first_weights, second_weights):
    layers = lax.axis_size("layer")
    layer = (norm_gains, first_weights[0], second_weights[0])
    rounds, restricted = plan(layers)
    rows = initial.shape[0] // PORTIONS
    states = []
    dep = norm_gains
    for portion in range(PORTIONS):
        current, four, sixteen = first_round(initial[portion * rows : (portion + 1) * rows], layer, dep)
        states.append({"current": current, "four": four, "sixteen": sixteen})
        dep = current
    steps = [("dp", 1 << k) for k in range((lax.axis_size("dp") - 1).bit_length())]
    steps += [("layer", 1 << k) for k in range((layers - 1).bit_length())]
    sums = None
    for index, pairs in enumerate(rounds):
        route = [(a - 1, b - 1) for a, b, unused in pairs]
        for portion in range(PORTIONS):
            arrived = lax.ppermute(states[portion]["current"], "layer", route)
            states[portion], dep = run_round(arrived, states[portion], layer, pairs, dep)
        if index == restricted:
            sums = functools.reduce(jnp.add, [state["sums"] for state in states])
        elif sums is not None and steps:
            axis, distance = steps.pop(0)
            partner = [(i, i ^ distance) for i in range(lax.axis_size(axis))]
            sums = add(sums, lax.ppermute(sums, axis, partner), dep)
    assert not steps
    residual_ratios = jnp.sqrt(sums[0, :7] / (sums[1, :7] + epsilon))
    point = lax.axis_index("layer") + 1

    def joined(name):
        return jnp.concatenate([state[name] for state in states], axis=0)[None]

    layer_states = joined("current")
    defects_four = jnp.where(point >= 4, layer_states - joined("four"), 0.0)
    defects_sixteen = jnp.where(point >= 16, layer_states - joined("sixteen"), 0.0)
    return (layer_states, residual_ratios, defects_four, defects_sixteen)


def solution(mesh):
    placed = (P("dp", None), P("layer", None), P("layer", None, None), P("layer", None, None))
    return jax.shard_map(
        local,
        mesh=mesh,
        in_specs=placed,
        out_specs=(P("layer", "dp", None), P(), P("layer", "dp", None), P("layer", "dp", None)),
        check_vma=False,
    )
```

```python
import functools

import jax
import jax.numpy as jnp
from jax import lax
from jax.experimental import pallas as pl
from jax.experimental.pallas import tpu as pltpu
from jax.sharding import PartitionSpec as P

epsilon = 1e-06
PORTIONS = 2
CHUNK = 1024
LOADS = 4

FINE, LEVEL, GAP_FOUR, GAP_SIXTEEN, RESTRICT, COARSEST = 1, 2, 3, 4, 5, 6
SPACING = {FINE: 1.0, LEVEL: 4.0, GAP_FOUR: 4.0, GAP_SIXTEEN: 16.0, RESTRICT: 1.0, COARSEST: 16.0}


def plan(layers):
    rounds = []

    def every(residue, shift, job, least=1):
        return [
            (n, n + shift, job)
            for n in range(least, layers - shift + 1)
            if n % 4 == residue
        ]

    rounds.append(every(1, 1, FINE))
    rounds.append(every(2, 1, FINE))
    rounds.append(every(3, 1, FINE))
    rounds.append(every(0, 1, FINE))
    rounds.append(every(0, 4, GAP_FOUR))
    rounds.append(every(1, 1, FINE) + [(16, 32, GAP_SIXTEEN)])
    rounds.append(every(2, 1, FINE))
    rounds.append(every(3, 1, RESTRICT))
    restricted = len(rounds) - 1
    rounds.append([(8, 12, LEVEL), (20, 24, LEVEL)])
    rounds.append([(12, 16, LEVEL), (24, 28, LEVEL)])
    rounds.append([(16, 20, LEVEL), (28, 32, LEVEL)])
    rounds.append([(20, 24, LEVEL), (16, 32, COARSEST)])
    rounds.append([(24, 28, LEVEL)])
    rounds.append([(24, 25, FINE)])
    rounds.append([(28, 29, FINE), (25, 26, FINE)])
    rounds.append([(29, 30, FINE), (26, 27, FINE), (28, 32, GAP_FOUR)])
    rounds.append([(27, 31, GAP_FOUR)])
    rounds.append([(30, 31, FINE)])

    final = {1: -1, 2: 0, 3: 1, 4: 2, 5: 3, 6: 5, 7: 6, 8: 7}
    final.update({12: 8, 16: 9, 20: 10, 24: 11, 28: 12, 32: 11, 25: 13, 26: 14, 27: 15, 29: 14, 30: 15, 31: 17})

    def place(source, target, job, not_before=0):
        index = max(final[source] + 1, not_before)
        while index < len(rounds):
            used = rounds[index]
            if all(a != source and b != target for a, b, unused in used):
                used.append((source, target, job))
                return index
            index += 1
        rounds.append([(source, target, job)])
        return index

    for anchor in (8, 12, 16, 20):
        for n in (anchor + 1, anchor + 2, anchor + 3):
            final[n] = place(n - 1, n, FINE, restricted + 1)
    wanted = []
    for n in range(5, layers + 1):
        if n % 4 != 0 and n != 31:
            wanted.append((final[n - 4], n - 4, n, GAP_FOUR))
    for n in range(17, layers):
        wanted.append((final[n - 16], n - 16, n, GAP_SIXTEEN))
    for unused, source, target, job in sorted(wanted):
        place(source, target, job, 17 if target == 30 and source == 26 else 4)
    return rounds, restricted


def normalised(state, gain_ref):
    mean_square = jnp.mean(state * state, axis=-1, keepdims=True)
    return (state * lax.rsqrt(mean_square + epsilon) * gain_ref[...]).astype(jnp.bfloat16)


def chunk_of(normed, first_ref, second_ref, start, width):
    hidden = jax.nn.gelu(
        jnp.dot(normed, first_ref[:, start : start + width], preferred_element_type=jnp.float32),
        approximate=True,
    ).astype(jnp.bfloat16)
    return jnp.dot(hidden, second_ref[start : start + width, :], preferred_element_type=jnp.float32)


def branch(state, gain_ref, first_ref, second_ref):
    normed = normalised(state, gain_ref)
    total = None
    for start in range(0, first_ref.shape[1], CHUNK):
        part = chunk_of(normed, first_ref, second_ref, start, CHUNK)
        total = part if total is None else total + part
    return total


WHOLE = pl.BlockSpec(memory_space=pltpu.VMEM)
FAR = pl.BlockSpec(memory_space=pltpu.HBM)
TOKEN = jax.ShapeDtypeStruct((8, 128), jnp.float32)


def settings(rows, mebibytes=8):
    return dict(
        compiler_params=pltpu.CompilerParams(vmem_limit_bytes=mebibytes * 2**20),
        cost_estimate=pl.CostEstimate(flops=4 * rows * 1024 * 2048 * 4, bytes_accessed=2**20, transcendentals=0),
    )


def first_kernel(state_hbm, gain_hbm, first_hbm, second_hbm, token_ref, gain_ref, first_ref, second_ref, *refs):
    state_ref, sems = refs[-2:]
    small = [
        pltpu.make_async_copy(state_hbm, state_ref, sems.at[2 * LOADS]),
        pltpu.make_async_copy(gain_hbm, gain_ref, sems.at[2 * LOADS + 1]),
    ]
    for copy in small:
        copy.start()
    width = first_hbm.shape[1] // LOADS
    copies = []
    for k in range(LOADS):
        columns = pl.ds(k * width, width)
        copies.append(pltpu.make_async_copy(first_hbm.at[:, columns], first_ref.at[:, columns], sems.at[2 * k]))
        copies.append(pltpu.make_async_copy(second_hbm.at[columns, :], second_ref.at[columns, :], sems.at[2 * k + 1]))
    for copy in copies:
        copy.start()
    token_ref[...] = jnp.zeros(token_ref.shape, jnp.float32)
    for copy in small:
        copy.wait()
    state = state_ref[...]
    normed = normalised(state, gain_ref)
    update = None
    for k in range(LOADS):
        copies[2 * k].wait()
        copies[2 * k + 1].wait()
        part = chunk_of(normed, first_ref, second_ref, k * width, width)
        update = part if update is None else update + part
    rows = state.shape[0] // PORTIONS
    for portion in range(PORTIONS):
        mine = slice(portion * rows, (portion + 1) * rows)
        for k, spacing in enumerate((1.0, 4.0, 16.0)):
            refs[3 * portion + k][...] = state[mine] + spacing * update[mine]


def first_round(initial, gain, first, second):
    rows = initial.shape[0] // PORTIONS
    block = jax.ShapeDtypeStruct((rows, initial.shape[1]), jnp.float32)
    made = pl.pallas_call(
        first_kernel,
        out_shape=(
            TOKEN,
            jax.ShapeDtypeStruct(gain.shape, gain.dtype),
            jax.ShapeDtypeStruct(first.shape, first.dtype),
            jax.ShapeDtypeStruct(second.shape, second.dtype),
        )
        + (block,) * (3 * PORTIONS),
        in_specs=[FAR] * 4,
        out_specs=(WHOLE,) * (4 + 3 * PORTIONS),
        scratch_shapes=[pltpu.VMEM(initial.shape, jnp.float32), pltpu.SemaphoreType.DMA((2 * LOADS + 2,))],
        **settings(initial.shape[0], 43),
    )(initial, gain, first, second)
    states = [
        dict(zip(("current", "four", "sixteen"), made[4 + 3 * k : 7 + 3 * k])) for k in range(PORTIONS)
    ]
    return made[0], made[1:4], states


def round_kernel(jobs, names_in, names_out, *refs):
    given = dict(zip(names_in, refs))
    made = dict(zip(names_out, refs[len(names_in) :]))
    update_ref = refs[-1]
    place = lax.axis_index("layer").astype(jnp.int32)
    made["token"][...] = given["token"][...]

    def among(points):
        mask = 0
        for n in points:
            mask |= 1 << (n - 1)
        if mask >= 2**31:
            mask -= 2**32
        return (lax.shift_right_logical(jnp.int32(mask), place) & 1) == 1

    busy = among([n for points in jobs.values() for n in points])

    @pl.when(busy)
    def compute():
        update_ref[...] = branch(given["arrived"][...], given["gain"], given["first"], given["second"])

    for name, writers in WRITERS.items():
        if name in made and name in given:

            @pl.when(jnp.logical_not(among([n for job in writers for n in jobs.get(job, ())])))
            def keep(name=name):
                made[name][...] = given[name][...]

    if "partner" in given:
        made["sums"][...] = given["sums"][...] + given["partner"][...]
    elif "sums" in given:
        made["sums"][...] = given["sums"][...]
    elif "sums" in made:
        made["sums"][...] = jnp.zeros(made["sums"].shape, jnp.float32)

    for job, points in jobs.items():

        @pl.when(among(points))
        def finish(job=job):
            stepped = given["arrived"][...] + SPACING[job] * update_ref[...]
            if job == FINE:
                made["current"][...] = stepped
            if job == LEVEL:
                made["four"][...] = stepped
                made["current"][...] = stepped + given["coarse"][...]
            if job == GAP_FOUR:
                made["four"][...] = stepped
            if job == GAP_SIXTEEN:
                made["sixteen"][...] = stepped
            if job == COARSEST:
                made["current"][...] = given["current"][...] + (stepped - given["sixteen"][...])
                made["sixteen"][...] = stepped
            if job == RESTRICT:
                gap = stepped - given["current"][...]
                update = update_ref[...]
                made["current"][...] = stepped
                made["coarse"][...] = stepped - given["four"][...]
                shape = made["sums"].shape
                row = lax.broadcasted_iota(jnp.int32, shape, 0)
                here = lax.broadcasted_iota(jnp.int32, shape, 1) == (place + 1) // 4 - 2
                both = jnp.where(row == 0, jnp.sum(gap * gap), jnp.sum(update * update))
                made["sums"][...] += jnp.where(here & (row < 2), both, 0.0)


WRITERS = {
    "current": {FINE, LEVEL, RESTRICT, COARSEST},
    "four": {LEVEL, GAP_FOUR},
    "sixteen": {GAP_SIXTEEN, COARSEST},
    "coarse": {RESTRICT},
}
READERS = {
    "current": {FINE, LEVEL, RESTRICT, COARSEST},
    "four": {RESTRICT, LEVEL, GAP_FOUR},
    "sixteen": {GAP_SIXTEEN, COARSEST},
    "coarse": {LEVEL},
}


def run_round(arrived, state, layer, pairs, token, sums):
    jobs = {}
    for unused, target, job in pairs:
        jobs.setdefault(job, []).append(target)
    kinds = set(jobs)
    names_in = ["arrived", "gain", "first", "second", "token"]
    values = [arrived, *layer, token]
    names_out, shapes = ["token"], [TOKEN]
    block = jax.ShapeDtypeStruct(arrived.shape, jnp.float32)
    for name, writers in WRITERS.items():
        if name in state and kinds & READERS[name]:
            names_in.append(name)
            values.append(state[name])
        if kinds & writers:
            names_out.append(name)
            shapes.append(block)
    names_in += list(sums)
    values += list(sums.values())
    if RESTRICT in kinds or sums:
        names_out.append("sums")
        shapes.append(TOKEN)
    made = pl.pallas_call(
        functools.partial(round_kernel, jobs, names_in, names_out),
        out_shape=tuple(shapes),
        in_specs=[WHOLE] * len(names_in),
        out_specs=(WHOLE,) * len(shapes),
        scratch_shapes=[pltpu.VMEM(arrived.shape, jnp.float32)],
        **settings(arrived.shape[0]),
    )(*values)
    made = dict(zip(names_out, made))
    return made


def finish_kernel(sums_ref, token_ref, *refs):
    given = refs[: 3 * PORTIONS]
    outs = refs[3 * PORTIONS : 3 * PORTIONS + 3]
    ratios_ref, *scratch, sems = refs[3 * PORTIONS + 3 :]
    point = lax.axis_index("layer") + 1
    rows = given[0].shape[0]
    copies = []

    def send(source, target, portion):
        block = target.at[0, pl.ds(portion * rows, rows), :]
        copies.append(pltpu.make_async_copy(source, block, sems.at[len(copies)]))
        copies[-1].start()

    for portion in range(PORTIONS):
        send(given[3 * portion], outs[0], portion)
    for portion in range(PORTIONS):
        current, *coarser = given[3 * portion : 3 * portion + 3]
        mine = pl.ds(portion * rows, rows)
        for ref, made, least, out in zip(coarser, scratch, (4, 16), outs[1:]):
            made[mine, :] = jnp.where(point >= least, current[...] - ref[...], 0.0)
            send(made.at[mine, :], out, portion)
    sums = sums_ref[...]
    ratios_ref[...] = jnp.sqrt(sums[0:1] / (sums[1:2] + epsilon))
    for copy in copies:
        copy.wait()


def finish(states, sums, token):
    rows, width = states[0]["current"].shape
    whole = jax.ShapeDtypeStruct((1, rows * PORTIONS, width), jnp.float32)
    values = [state[name] for state in states for name in ("current", "four", "sixteen")]
    layer_states, defects_four, defects_sixteen, ratios = pl.pallas_call(
        finish_kernel,
        out_shape=(whole, whole, whole, jax.ShapeDtypeStruct((1, 128), jnp.float32)),
        in_specs=[WHOLE] * (2 + len(values)),
        out_specs=(FAR, FAR, FAR, WHOLE),
        scratch_shapes=[pltpu.VMEM((rows * PORTIONS, width), jnp.float32)] * 2
        + [pltpu.SemaphoreType.DMA((3 * PORTIONS,))],
        compiler_params=pltpu.CompilerParams(vmem_limit_bytes=8 * 2**20),
    )(sums, token, *values)
    return layer_states, ratios[0, :7], defects_four, defects_sixteen


def local(initial, norm_gains, first_weights, second_weights):
    layers = lax.axis_size("layer")
    rounds, restricted = plan(layers)
    token, layer, states = first_round(initial, norm_gains, first_weights[0], second_weights[0])
    steps = [("dp", 1 << k) for k in range((lax.axis_size("dp") - 1).bit_length())]
    steps += [("layer", 1 << k) for k in range((layers - 1).bit_length())]
    sums, partner = None, None
    for index, pairs in enumerate(rounds):
        route = [(a - 1, b - 1) for a, b, unused in pairs]
        for portion in range(PORTIONS):
            arrived = lax.ppermute(states[portion]["current"], "layer", route)
            adding = {}
            if sums is not None and index == restricted:
                adding = {"sums": sums}
            if partner is not None and portion == PORTIONS - 1:
                adding = {"sums": sums, "partner": partner}
            made = run_round(arrived, states[portion], layer, pairs, token, adding)
            token = made.pop("token")
            sums = made.pop("sums", sums)
            states[portion].update(made)
        if index >= restricted:
            partner = None
            if steps:
                axis, distance = steps.pop(0)
                partner = lax.ppermute(sums, axis, [(i, i ^ distance) for i in range(lax.axis_size(axis))])
    assert not steps and partner is None
    return finish(states, sums, token)


def solution(mesh):
    placed = (P("dp", None), P("layer", None), P("layer", None, None), P("layer", None, None))
    return jax.shard_map(
        local,
        mesh=mesh,
        in_specs=placed,
        out_specs=(P("layer", "dp", None), P(), P("layer", "dp", None), P("layer", "dp", None)),
        check_vma=False,
    )
```

```python
import functools

import jax
import jax.numpy as jnp
from jax import lax
from jax.experimental import pallas as pl
from jax.experimental.pallas import tpu as pltpu
from jax.sharding import PartitionSpec as P

epsilon = 1e-06
PORTIONS = 2
CHUNK = 1024
LOADS = 4

FINE, LEVEL, GAP_FOUR, GAP_SIXTEEN, RESTRICT, COARSEST = 1, 2, 3, 4, 5, 6
SPACING = {FINE: 1.0, LEVEL: 4.0, GAP_FOUR: 4.0, GAP_SIXTEEN: 16.0, RESTRICT: 1.0, COARSEST: 16.0}


def plan(layers):
    rounds = []

    def every(residue, shift, job, least=1):
        return [
            (n, n + shift, job)
            for n in range(least, layers - shift + 1)
            if n % 4 == residue
        ]

    rounds.append(every(1, 1, FINE))
    rounds.append(every(2, 1, FINE))
    rounds.append(every(3, 1, FINE))
    rounds.append(every(0, 1, FINE))
    rounds.append(every(0, 4, GAP_FOUR))
    rounds.append(every(1, 1, FINE) + [(16, 32, GAP_SIXTEEN)])
    rounds.append(every(2, 1, FINE))
    rounds.append(every(3, 1, RESTRICT))
    restricted = len(rounds) - 1
    rounds.append([(8, 12, LEVEL), (20, 24, LEVEL)])
    rounds.append([(12, 16, LEVEL), (24, 28, LEVEL)])
    rounds.append([(16, 20, LEVEL), (28, 32, LEVEL)])
    rounds.append([(20, 24, LEVEL), (16, 32, COARSEST)])
    rounds.append([(24, 28, LEVEL)])
    rounds.append([(24, 25, FINE)])
    rounds.append([(28, 29, FINE), (25, 26, FINE)])
    rounds.append([(29, 30, FINE), (26, 27, FINE), (28, 32, GAP_FOUR)])
    rounds.append([(27, 31, GAP_FOUR)])
    rounds.append([(30, 31, FINE)])

    final = {1: -1, 2: 0, 3: 1, 4: 2, 5: 3, 6: 5, 7: 6, 8: 7}
    final.update({12: 8, 16: 9, 20: 10, 24: 11, 28: 12, 32: 11, 25: 13, 26: 14, 27: 15, 29: 14, 30: 15, 31: 17})

    closed = {17}

    def place(source, target, job, not_before=0):
        index = max(final[source] + 1, not_before)
        while index < len(rounds):
            used = rounds[index]
            if index not in closed and all(a != source and b != target for a, b, unused in used):
                used.append((source, target, job))
                return index
            index += 1
        rounds.append([(source, target, job)])
        return index

    for anchor in (8, 12, 16, 20):
        for n in (anchor + 1, anchor + 2, anchor + 3):
            final[n] = place(n - 1, n, FINE, restricted + 1)
    wanted = []
    for n in range(5, layers + 1):
        if n % 4 != 0 and n != 31:
            wanted.append((final[n - 4], n - 4, n, GAP_FOUR))
    for n in range(17, layers):
        wanted.append((final[n - 16], n - 16, n, GAP_SIXTEEN))
    for unused, source, target, job in sorted(wanted):
        place(source, target, job, 4)
    routes = [[(a, b) for a, b, unused in pairs] for pairs in rounds]
    for index, like in ((0, 5), (1, 6), (2, 7), (17, 6)):
        assert set(routes[index]) <= set(routes[like])
        routes[index] = routes[like]
    return rounds, routes, restricted


def normalised(state, gain_ref):
    mean_square = jnp.mean(state * state, axis=-1, keepdims=True)
    return (state * lax.rsqrt(mean_square + epsilon) * gain_ref[...]).astype(jnp.bfloat16)


def chunk_of(normed, first_ref, second_ref, start, width):
    hidden = jax.nn.gelu(
        jnp.dot(normed, first_ref[:, start : start + width], preferred_element_type=jnp.float32),
        approximate=True,
    ).astype(jnp.bfloat16)
    return jnp.dot(hidden, second_ref[start : start + width, :], preferred_element_type=jnp.float32)


def branch(state, gain_ref, first_ref, second_ref):
    normed = normalised(state, gain_ref)
    total = None
    for start in range(0, first_ref.shape[1], CHUNK):
        part = chunk_of(normed, first_ref, second_ref, start, CHUNK)
        total = part if total is None else total + part
    return total


WHOLE = pl.BlockSpec(memory_space=pltpu.VMEM)
FAR = pl.BlockSpec(memory_space=pltpu.HBM)
TOKEN = jax.ShapeDtypeStruct((8, 128), jnp.float32)


def settings(rows, mebibytes=8):
    return dict(
        compiler_params=pltpu.CompilerParams(vmem_limit_bytes=mebibytes * 2**20),
        cost_estimate=pl.CostEstimate(flops=4 * rows * 1024 * 2048 * 4, bytes_accessed=2**20, transcendentals=0),
    )


def first_kernel(state_hbm, gain_hbm, first_hbm, second_hbm, token_ref, gain_ref, first_ref, second_ref, *refs):
    state_ref, sems = refs[-2:]
    small = [
        pltpu.make_async_copy(state_hbm, state_ref, sems.at[2 * LOADS]),
        pltpu.make_async_copy(gain_hbm, gain_ref, sems.at[2 * LOADS + 1]),
    ]
    for copy in small:
        copy.start()
    width = first_hbm.shape[1] // LOADS
    copies = []
    for k in range(LOADS):
        columns = pl.ds(k * width, width)
        copies.append(pltpu.make_async_copy(first_hbm.at[:, columns], first_ref.at[:, columns], sems.at[2 * k]))
        copies.append(pltpu.make_async_copy(second_hbm.at[columns, :], second_ref.at[columns, :], sems.at[2 * k + 1]))
    for copy in copies:
        copy.start()
    token_ref[...] = jnp.zeros(token_ref.shape, jnp.float32)
    for copy in small:
        copy.wait()
    state = state_ref[...]
    normed = normalised(state, gain_ref)
    update = None
    for k in range(LOADS):
        copies[2 * k].wait()
        copies[2 * k + 1].wait()
        part = chunk_of(normed, first_ref, second_ref, k * width, width)
        update = part if update is None else update + part
    rows = state.shape[0] // PORTIONS
    for portion in range(PORTIONS):
        mine = slice(portion * rows, (portion + 1) * rows)
        for k, spacing in enumerate((1.0, 4.0, 16.0)):
            refs[3 * portion + k][...] = state[mine] + spacing * update[mine]


def first_round(initial, gain, first, second):
    rows = initial.shape[0] // PORTIONS
    block = jax.ShapeDtypeStruct((rows, initial.shape[1]), jnp.float32)
    made = pl.pallas_call(
        first_kernel,
        out_shape=(
            TOKEN,
            jax.ShapeDtypeStruct(gain.shape, gain.dtype),
            jax.ShapeDtypeStruct(first.shape, first.dtype),
            jax.ShapeDtypeStruct(second.shape, second.dtype),
        )
        + (block,) * (3 * PORTIONS),
        in_specs=[FAR] * 4,
        out_specs=(WHOLE,) * (4 + 3 * PORTIONS),
        scratch_shapes=[pltpu.VMEM(initial.shape, jnp.float32), pltpu.SemaphoreType.DMA((2 * LOADS + 2,))],
        **settings(initial.shape[0], 43),
    )(initial, gain, first, second)
    states = [
        dict(zip(("current", "four", "sixteen"), made[4 + 3 * k : 7 + 3 * k])) for k in range(PORTIONS)
    ]
    return made[0], made[1:4], states


def round_kernel(jobs, names_in, names_out, *refs):
    given = dict(zip(names_in, refs))
    made = dict(zip(names_out, refs[len(names_in) :]))
    update_ref = refs[-1]
    place = lax.axis_index("layer").astype(jnp.int32)
    made["token"][...] = given["token"][...]

    def among(points):
        mask = 0
        for n in points:
            mask |= 1 << (n - 1)
        if mask >= 2**31:
            mask -= 2**32
        return (lax.shift_right_logical(jnp.int32(mask), place) & 1) == 1

    busy = among([n for points in jobs.values() for n in points])

    @pl.when(busy)
    def compute():
        update_ref[...] = branch(given["arrived"][...], given["gain"], given["first"], given["second"])

    for name, writers in WRITERS.items():
        if name in made and name in given:

            @pl.when(jnp.logical_not(among([n for job in writers for n in jobs.get(job, ())])))
            def keep(name=name):
                made[name][...] = given[name][...]

    if "partner" in given:
        made["sums"][...] = given["sums"][...] + given["partner"][...]
    elif "sums" in given:
        made["sums"][...] = given["sums"][...]
    elif "sums" in made:
        made["sums"][...] = jnp.zeros(made["sums"].shape, jnp.float32)

    for job, points in jobs.items():

        @pl.when(among(points))
        def finish(job=job):
            stepped = given["arrived"][...] + SPACING[job] * update_ref[...]
            if job == FINE:
                made["current"][...] = stepped
            if job == LEVEL:
                made["four"][...] = stepped
                made["current"][...] = stepped + given["coarse"][...]
            if job == GAP_FOUR:
                made["four"][...] = stepped
            if job == GAP_SIXTEEN:
                made["sixteen"][...] = stepped
            if job == COARSEST:
                made["current"][...] = given["current"][...] + (stepped - given["sixteen"][...])
                made["sixteen"][...] = stepped
            if job == RESTRICT:
                gap = stepped - given["current"][...]
                update = update_ref[...]
                made["current"][...] = stepped
                made["coarse"][...] = stepped - given["four"][...]
                shape = made["sums"].shape
                row = lax.broadcasted_iota(jnp.int32, shape, 0)
                here = lax.broadcasted_iota(jnp.int32, shape, 1) == (place + 1) // 4 - 2
                both = jnp.where(row == 0, jnp.sum(gap * gap), jnp.sum(update * update))
                made["sums"][...] += jnp.where(here & (row < 2), both, 0.0)


WRITERS = {
    "current": {FINE, LEVEL, RESTRICT, COARSEST},
    "four": {LEVEL, GAP_FOUR},
    "sixteen": {GAP_SIXTEEN, COARSEST},
    "coarse": {RESTRICT},
}
READERS = {
    "current": {FINE, LEVEL, RESTRICT, COARSEST},
    "four": {RESTRICT, LEVEL, GAP_FOUR},
    "sixteen": {GAP_SIXTEEN, COARSEST},
    "coarse": {LEVEL},
}


def run_round(arrived, state, layer, pairs, token, sums):
    jobs = {}
    for unused, target, job in pairs:
        jobs.setdefault(job, []).append(target)
    kinds = set(jobs)
    names_in = ["arrived", "gain", "first", "second", "token"]
    values = [arrived, *layer, token]
    names_out, shapes = ["token"], [TOKEN]
    block = jax.ShapeDtypeStruct(arrived.shape, jnp.float32)
    for name, writers in WRITERS.items():
        if name in state and kinds & READERS[name]:
            names_in.append(name)
            values.append(state[name])
        if kinds & writers:
            names_out.append(name)
            shapes.append(block)
    names_in += list(sums)
    values += list(sums.values())
    if RESTRICT in kinds or sums:
        names_out.append("sums")
        shapes.append(TOKEN)
    made = pl.pallas_call(
        functools.partial(round_kernel, jobs, names_in, names_out),
        out_shape=tuple(shapes),
        in_specs=[WHOLE] * len(names_in),
        out_specs=(WHOLE,) * len(shapes),
        scratch_shapes=[pltpu.VMEM(arrived.shape, jnp.float32)],
        **settings(arrived.shape[0]),
    )(*values)
    made = dict(zip(names_out, made))
    return made


def finish_kernel(sums_ref, token_ref, *refs):
    given = refs[: 3 * PORTIONS]
    outs = refs[3 * PORTIONS : 3 * PORTIONS + 3]
    ratios_ref, *scratch, sems = refs[3 * PORTIONS + 3 :]
    point = lax.axis_index("layer") + 1
    rows = given[0].shape[0]
    copies = []

    def send(source, target, portion):
        block = target.at[0, pl.ds(portion * rows, rows), :]
        copies.append(pltpu.make_async_copy(source, block, sems.at[len(copies)]))
        copies[-1].start()

    for portion in range(PORTIONS):
        send(given[3 * portion], outs[0], portion)
    for portion in range(PORTIONS):
        current, *coarser = given[3 * portion : 3 * portion + 3]
        mine = pl.ds(portion * rows, rows)
        for ref, made, least, out in zip(coarser, scratch, (4, 16), outs[1:]):
            made[mine, :] = jnp.where(point >= least, current[...] - ref[...], 0.0)
            send(made.at[mine, :], out, portion)
    sums = sums_ref[...]
    ratios_ref[...] = jnp.sqrt(sums[0:1] / (sums[1:2] + epsilon))
    for copy in copies:
        copy.wait()


def finish(states, sums, token):
    rows, width = states[0]["current"].shape
    whole = jax.ShapeDtypeStruct((1, rows * PORTIONS, width), jnp.float32)
    values = [state[name] for state in states for name in ("current", "four", "sixteen")]
    layer_states, defects_four, defects_sixteen, ratios = pl.pallas_call(
        finish_kernel,
        out_shape=(whole, whole, whole, jax.ShapeDtypeStruct((1, 128), jnp.float32)),
        in_specs=[WHOLE] * (2 + len(values)),
        out_specs=(FAR, FAR, FAR, WHOLE),
        scratch_shapes=[pltpu.VMEM((rows * PORTIONS, width), jnp.float32)] * 2
        + [pltpu.SemaphoreType.DMA((3 * PORTIONS,))],
        compiler_params=pltpu.CompilerParams(vmem_limit_bytes=8 * 2**20),
    )(sums, token, *values)
    return layer_states, ratios[0, :7], defects_four, defects_sixteen


def local(initial, norm_gains, first_weights, second_weights):
    layers = lax.axis_size("layer")
    rounds, routes, restricted = plan(layers)
    token, layer, states = first_round(initial, norm_gains, first_weights[0], second_weights[0])
    steps = [("dp", 1 << k) for k in range((lax.axis_size("dp") - 1).bit_length())]
    steps += [("layer", 1 << k) for k in range((layers - 1).bit_length())]
    sums, partner = None, None
    for index, pairs in enumerate(rounds):
        route = [(a - 1, b - 1) for a, b in routes[index]]
        for portion in range(PORTIONS):
            arrived = lax.ppermute(states[portion]["current"], "layer", route)
            adding = {}
            if sums is not None and index == restricted:
                adding = {"sums": sums}
            if partner is not None and portion == PORTIONS - 1:
                adding = {"sums": sums, "partner": partner}
            made = run_round(arrived, states[portion], layer, pairs, token, adding)
            token = made.pop("token")
            sums = made.pop("sums", sums)
            states[portion].update(made)
        if index >= restricted:
            partner = None
            if steps:
                axis, distance = steps.pop(0)
                partner = lax.ppermute(sums, axis, [(i, i ^ distance) for i in range(lax.axis_size(axis))])
    assert not steps and partner is None
    return finish(states, sums, token)


def solution(mesh):
    placed = (P("dp", None), P("layer", None), P("layer", None, None), P("layer", None, None))
    return jax.shard_map(
        local,
        mesh=mesh,
        in_specs=placed,
        out_specs=(P("layer", "dp", None), P(), P("layer", "dp", None), P("layer", "dp", None)),
        check_vma=False,
    )
```

```python
import functools

import jax
import jax.numpy as jnp
from jax import lax
from jax.experimental import pallas as pl
from jax.experimental.pallas import tpu as pltpu
from jax.sharding import PartitionSpec as P

epsilon = 1e-06
PORTIONS = 2
CHUNK = 1024
LOADS = 4

ADD = "add"
FINE, LEVEL, GAP_FOUR, GAP_SIXTEEN, RESTRICT, COARSEST = 1, 2, 3, 4, 5, 6
SPACING = {FINE: 1.0, LEVEL: 4.0, GAP_FOUR: 4.0, GAP_SIXTEEN: 16.0, RESTRICT: 1.0, COARSEST: 16.0}


def plan(layers):
    rounds = []

    def every(residue, shift, job, least=1):
        return [
            (n, n + shift, job)
            for n in range(least, layers - shift + 1)
            if n % 4 == residue
        ]

    rounds.append(every(1, 1, FINE))
    rounds.append(every(2, 1, FINE))
    rounds.append(every(3, 1, FINE))
    rounds.append(every(0, 1, FINE))
    rounds.append(every(0, 4, GAP_FOUR))
    rounds.append(every(1, 1, FINE) + [(16, 32, GAP_SIXTEEN)])
    rounds.append(every(2, 1, FINE))
    rounds.append(every(3, 1, RESTRICT))
    restricted = len(rounds) - 1
    rounds.append([(8, 12, LEVEL), (20, 24, LEVEL)])
    rounds.append([(12, 16, LEVEL), (24, 28, LEVEL)])
    rounds.append([(16, 20, LEVEL), (28, 32, LEVEL)])
    rounds.append([(20, 24, LEVEL), (16, 32, COARSEST)])
    rounds.append([(24, 28, LEVEL)])
    rounds.append([(24, 25, FINE)])
    rounds.append([(28, 29, FINE), (25, 26, FINE)])
    rounds.append([(29, 30, FINE), (26, 27, FINE), (28, 32, GAP_FOUR)])
    rounds.append([(27, 31, GAP_FOUR)])
    rounds.append([(30, 31, FINE)])

    final = {1: -1, 2: 0, 3: 1, 4: 2, 5: 3, 6: 5, 7: 6, 8: 7}
    final.update({12: 8, 16: 9, 20: 10, 24: 11, 28: 12, 32: 11, 25: 13, 26: 14, 27: 15, 29: 14, 30: 15, 31: 17})

    closed = {17}

    def place(source, target, job, not_before=0):
        index = max(final[source] + 1, not_before)
        while index < len(rounds):
            used = rounds[index]
            if index not in closed and all(a != source and b != target for a, b, unused in used):
                used.append((source, target, job))
                return index
            index += 1
        rounds.append([(source, target, job)])
        return index

    for anchor in (8, 12, 16, 20):
        for n in (anchor + 1, anchor + 2, anchor + 3):
            final[n] = place(n - 1, n, FINE, restricted + 1)
    wanted = []
    for n in range(5, layers + 1):
        if n % 4 != 0 and n != 31:
            wanted.append((final[n - 4], n - 4, n, GAP_FOUR))
    for n in range(17, layers):
        wanted.append((final[n - 16], n - 16, n, GAP_SIXTEEN))
    for unused, source, target, job in sorted(wanted):
        place(source, target, job, 4)
    routes = [[(a, b) for a, b, unused in pairs] for pairs in rounds]
    for index, like in ((0, 5), (1, 6), (2, 7), (17, 6)):
        assert set(routes[index]) <= set(routes[like])
        routes[index] = routes[like]
    routes[3] = routes[3] + [(layers, 1)]
    return rounds, routes, restricted


def gathering(routes, planes):
    root = 3

    def within(pairs):
        return [(a - 1, b - 1) for a, b in pairs]

    steps = [
        ((8, 1), "layer", within([(8, 4), (16, 12), (24, 20), (32, 28)]), ADD),
        ((9, 1), "layer", within([(12, 4), (28, 20)]), ADD),
        ((10, 0), "layer", within([(20, 4)]), ADD),
    ]
    for when, distance in (((10, 1), 1), ((11, 0), 2), ((11, 1), 4)):
        pairs = [(root * planes + i, root * planes + (i ^ distance)) for i in range(planes)]
        steps.append((when, ("layer", "dp"), pairs, ADD))
    assert (4, 20) in routes[5]
    steps.append(((12, 1), "layer", within(routes[5]), (20,)))
    steps.append(((14, 0), "layer", within([(4, 12), (20, 28)]), (12, 28)))
    steps.append(((14, 1), "layer", within(routes[4]), (8, 16, 24, 32)))
    steps.append(((15, 1), "layer", within(routes[3]), tuple(range(1, 33, 4))))
    steps.append(((16, 1), "layer", within(routes[5]), tuple(range(2, 33, 4))))
    steps.append((None, "layer", within(routes[6]), tuple(range(3, 33, 4))))
    return steps


def member(points):
    place = lax.axis_index("layer").astype(jnp.int32)
    mask = 0
    for n in points:
        mask |= 1 << (n - 1)
    if mask >= 2**31:
        mask -= 2**32
    return (lax.shift_right_logical(jnp.int32(mask), place) & 1) == 1


def taken(held_ref, arrived_ref, receivers, target_ref):
    if receivers == ADD:
        target_ref[...] = held_ref[...] + arrived_ref[...]
    else:
        here = member(receivers)

        @pl.when(here)
        def replace():
            target_ref[...] = arrived_ref[...]

        @pl.when(jnp.logical_not(here))
        def keep():
            target_ref[...] = held_ref[...]


def normalised(state, gain_ref):
    mean_square = jnp.mean(state * state, axis=-1, keepdims=True)
    return (state * lax.rsqrt(mean_square + epsilon) * gain_ref[...]).astype(jnp.bfloat16)


def chunk_of(normed, first_ref, second_ref, start, width):
    hidden = jax.nn.gelu(
        jnp.dot(normed, first_ref[:, start : start + width], preferred_element_type=jnp.float32),
        approximate=True,
    ).astype(jnp.bfloat16)
    return jnp.dot(hidden, second_ref[start : start + width, :], preferred_element_type=jnp.float32)


def branch(state, gain_ref, first_ref, second_ref):
    normed = normalised(state, gain_ref)
    total = None
    for start in range(0, first_ref.shape[1], CHUNK):
        part = chunk_of(normed, first_ref, second_ref, start, CHUNK)
        total = part if total is None else total + part
    return total


WHOLE = pl.BlockSpec(memory_space=pltpu.VMEM)
FAR = pl.BlockSpec(memory_space=pltpu.HBM)
TOKEN = jax.ShapeDtypeStruct((8, 128), jnp.float32)


def settings(rows, mebibytes=8):
    return dict(
        compiler_params=pltpu.CompilerParams(vmem_limit_bytes=mebibytes * 2**20),
        cost_estimate=pl.CostEstimate(flops=4 * rows * 1024 * 2048 * 4, bytes_accessed=2**20, transcendentals=0),
    )


def first_kernel(state_hbm, gain_hbm, first_hbm, second_hbm, token_ref, gain_ref, first_ref, second_ref, *refs):
    state_ref, sems = refs[-2:]
    small = [
        pltpu.make_async_copy(state_hbm, state_ref, sems.at[2 * LOADS]),
        pltpu.make_async_copy(gain_hbm, gain_ref, sems.at[2 * LOADS + 1]),
    ]
    for copy in small:
        copy.start()
    width = first_hbm.shape[1] // LOADS
    copies = []
    for k in range(LOADS):
        columns = pl.ds(k * width, width)
        copies.append(pltpu.make_async_copy(first_hbm.at[:, columns], first_ref.at[:, columns], sems.at[2 * k]))
        copies.append(pltpu.make_async_copy(second_hbm.at[columns, :], second_ref.at[columns, :], sems.at[2 * k + 1]))
    for copy in copies:
        copy.start()
    token_ref[...] = jnp.zeros(token_ref.shape, jnp.float32)
    for copy in small:
        copy.wait()
    state = state_ref[...]
    normed = normalised(state, gain_ref)
    update = None
    for k in range(LOADS):
        copies[2 * k].wait()
        copies[2 * k + 1].wait()
        part = chunk_of(normed, first_ref, second_ref, k * width, width)
        update = part if update is None else update + part
    rows = state.shape[0] // PORTIONS
    for portion in range(PORTIONS):
        mine = slice(portion * rows, (portion + 1) * rows)
        for k, spacing in enumerate((1.0, 4.0, 16.0)):
            refs[3 * portion + k][...] = state[mine] + spacing * update[mine]


def first_round(initial, gain, first, second):
    rows = initial.shape[0] // PORTIONS
    block = jax.ShapeDtypeStruct((rows, initial.shape[1]), jnp.float32)
    made = pl.pallas_call(
        first_kernel,
        out_shape=(
            TOKEN,
            jax.ShapeDtypeStruct(gain.shape, gain.dtype),
            jax.ShapeDtypeStruct(first.shape, first.dtype),
            jax.ShapeDtypeStruct(second.shape, second.dtype),
        )
        + (block,) * (3 * PORTIONS),
        in_specs=[FAR] * 4,
        out_specs=(WHOLE,) * (4 + 3 * PORTIONS),
        scratch_shapes=[pltpu.VMEM(initial.shape, jnp.float32), pltpu.SemaphoreType.DMA((2 * LOADS + 2,))],
        **settings(initial.shape[0], 43),
    )(initial, gain, first, second)
    states = [
        dict(zip(("current", "four", "sixteen"), made[4 + 3 * k : 7 + 3 * k])) for k in range(PORTIONS)
    ]
    return made[0], made[1:4], states


def round_kernel(jobs, names_in, names_out, receivers, *refs):
    given = dict(zip(names_in, refs))
    made = dict(zip(names_out, refs[len(names_in) :]))
    update_ref = refs[-1]
    place = lax.axis_index("layer").astype(jnp.int32)
    made["token"][...] = given["token"][...]

    among = member
    busy = among([n for points in jobs.values() for n in points])

    @pl.when(busy)
    def compute():
        update_ref[...] = branch(given["arrived"][...], given["gain"], given["first"], given["second"])

    for name, writers in WRITERS.items():
        if name in made and name in given:

            @pl.when(jnp.logical_not(among([n for job in writers for n in jobs.get(job, ())])))
            def keep(name=name):
                made[name][...] = given[name][...]

    if "partner" in given:
        taken(given["sums"], given["partner"], receivers, made["sums"])
    elif "sums" in given:
        made["sums"][...] = given["sums"][...]
    elif "sums" in made:
        made["sums"][...] = jnp.zeros(made["sums"].shape, jnp.float32)

    for job, points in jobs.items():

        @pl.when(among(points))
        def finish(job=job):
            stepped = given["arrived"][...] + SPACING[job] * update_ref[...]
            if job == FINE:
                made["current"][...] = stepped
            if job == LEVEL:
                made["four"][...] = stepped
                made["current"][...] = stepped + given["coarse"][...]
            if job == GAP_FOUR:
                made["four"][...] = stepped
            if job == GAP_SIXTEEN:
                made["sixteen"][...] = stepped
            if job == COARSEST:
                made["current"][...] = given["current"][...] + (stepped - given["sixteen"][...])
                made["sixteen"][...] = stepped
            if job == RESTRICT:
                gap = stepped - given["current"][...]
                update = update_ref[...]
                made["current"][...] = stepped
                made["coarse"][...] = stepped - given["four"][...]
                shape = made["sums"].shape
                row = lax.broadcasted_iota(jnp.int32, shape, 0)
                here = lax.broadcasted_iota(jnp.int32, shape, 1) == (place + 1) // 4 - 2
                both = jnp.where(row == 0, jnp.sum(gap * gap), jnp.sum(update * update))
                made["sums"][...] += jnp.where(here & (row < 2), both, 0.0)


WRITERS = {
    "current": {FINE, LEVEL, RESTRICT, COARSEST},
    "four": {LEVEL, GAP_FOUR},
    "sixteen": {GAP_SIXTEEN, COARSEST},
    "coarse": {RESTRICT},
}
READERS = {
    "current": {FINE, LEVEL, RESTRICT, COARSEST},
    "four": {RESTRICT, LEVEL, GAP_FOUR},
    "sixteen": {GAP_SIXTEEN, COARSEST},
    "coarse": {LEVEL},
}


def run_round(arrived, state, layer, pairs, token, sums, receivers):
    jobs = {}
    for unused, target, job in pairs:
        jobs.setdefault(job, []).append(target)
    kinds = set(jobs)
    names_in = ["arrived", "gain", "first", "second", "token"]
    values = [arrived, *layer, token]
    names_out, shapes = ["token"], [TOKEN]
    block = jax.ShapeDtypeStruct(arrived.shape, jnp.float32)
    for name, writers in WRITERS.items():
        if name in state and kinds & READERS[name]:
            names_in.append(name)
            values.append(state[name])
        if kinds & writers:
            names_out.append(name)
            shapes.append(block)
    names_in += list(sums)
    values += list(sums.values())
    if RESTRICT in kinds or sums:
        names_out.append("sums")
        shapes.append(TOKEN)
    made = pl.pallas_call(
        functools.partial(round_kernel, jobs, names_in, names_out, receivers),
        out_shape=tuple(shapes),
        in_specs=[WHOLE] * len(names_in),
        out_specs=(WHOLE,) * len(shapes),
        scratch_shapes=[pltpu.VMEM(arrived.shape, jnp.float32)],
        **settings(arrived.shape[0]),
    )(*values)
    made = dict(zip(names_out, made))
    return made


def finish_kernel(receivers, sums_ref, partner_ref, token_ref, *refs):
    given = refs[: 3 * PORTIONS]
    outs = refs[3 * PORTIONS : 3 * PORTIONS + 3]
    ratios_ref, *scratch, total_ref, sems = refs[3 * PORTIONS + 3 :]
    point = lax.axis_index("layer") + 1
    rows = given[0].shape[0]
    copies = []

    def send(source, target, portion):
        block = target.at[0, pl.ds(portion * rows, rows), :]
        copies.append(pltpu.make_async_copy(source, block, sems.at[len(copies)]))
        copies[-1].start()

    for portion in range(PORTIONS):
        send(given[3 * portion], outs[0], portion)
    for portion in range(PORTIONS):
        current, *coarser = given[3 * portion : 3 * portion + 3]
        mine = pl.ds(portion * rows, rows)
        for ref, made, least, out in zip(coarser, scratch, (4, 16), outs[1:]):
            made[mine, :] = jnp.where(point >= least, current[...] - ref[...], 0.0)
            send(made.at[mine, :], out, portion)
    taken(sums_ref, partner_ref, receivers, total_ref)
    sums = total_ref[...]
    ratios_ref[...] = jnp.sqrt(sums[0:1] / (sums[1:2] + epsilon))
    for copy in copies:
        copy.wait()


def finish(states, sums, partner, receivers, token):
    rows, width = states[0]["current"].shape
    whole = jax.ShapeDtypeStruct((1, rows * PORTIONS, width), jnp.float32)
    values = [state[name] for state in states for name in ("current", "four", "sixteen")]
    layer_states, defects_four, defects_sixteen, ratios = pl.pallas_call(
        functools.partial(finish_kernel, receivers),
        out_shape=(whole, whole, whole, jax.ShapeDtypeStruct((1, 128), jnp.float32)),
        in_specs=[WHOLE] * (3 + len(values)),
        out_specs=(FAR, FAR, FAR, WHOLE),
        scratch_shapes=[pltpu.VMEM((rows * PORTIONS, width), jnp.float32)] * 2
        + [pltpu.VMEM(TOKEN.shape, jnp.float32), pltpu.SemaphoreType.DMA((3 * PORTIONS,))],
        compiler_params=pltpu.CompilerParams(vmem_limit_bytes=8 * 2**20),
    )(sums, partner, token, *values)
    return layer_states, ratios[0, :7], defects_four, defects_sixteen


def local(initial, norm_gains, first_weights, second_weights):
    layers = lax.axis_size("layer")
    rounds, routes, restricted = plan(layers)
    token, layer, states = first_round(initial, norm_gains, first_weights[0], second_weights[0])
    steps = gathering(routes, lax.axis_size("dp"))
    sums, partner, receivers, due = None, None, None, None
    for index, pairs in enumerate(rounds):
        route = [(a - 1, b - 1) for a, b in routes[index]]
        for portion in range(PORTIONS):
            arrived = lax.ppermute(states[portion]["current"], "layer", route)
            adding, taking = {}, None
            if sums is not None and index == restricted:
                adding = {"sums": sums}
            if due == (index, portion):
                adding, taking = {"sums": sums, "partner": partner}, receivers
            made = run_round(arrived, states[portion], layer, pairs, token, adding, taking)
            token = made.pop("token")
            sums = made.pop("sums", sums)
            states[portion].update(made)
            if due == (index, portion) or (index == restricted and portion == PORTIONS - 1):
                due, axes, ring, receivers = steps.pop(0)
                partner = lax.ppermute(sums, axes, ring)
    assert not steps and due is None
    return finish(states, sums, partner, receivers, token)


def solution(mesh):
    placed = (P("dp", None), P("layer", None), P("layer", None, None), P("layer", None, None))
    return jax.shard_map(
        local,
        mesh=mesh,
        in_specs=placed,
        out_specs=(P("layer", "dp", None), P(), P("layer", "dp", None), P("layer", "dp", None)),
        check_vma=False,
    )
```

```python
import functools

import jax
import jax.numpy as jnp
from jax import lax
from jax.experimental import pallas as pl
from jax.experimental.pallas import tpu as pltpu
from jax.sharding import PartitionSpec as P

epsilon = 1e-06
PORTIONS = 2
CHUNK = 1024
LOADS = 4

ADD = "add"
FINE, LEVEL, GAP_FOUR, GAP_SIXTEEN, RESTRICT, COARSEST = 1, 2, 3, 4, 5, 6
SPACING = {FINE: 1.0, LEVEL: 4.0, GAP_FOUR: 4.0, GAP_SIXTEEN: 16.0, RESTRICT: 1.0, COARSEST: 16.0}


def plan(layers):
    def every(residue, shift, job):
        return [(n, n + shift, job) for n in range(1, layers - shift + 1) if n % 4 == residue]

    hops = {
        (0, 0): every(1, 1, FINE),
        (1, 0): every(2, 1, FINE),
        (2, 0): every(3, 1, FINE),
        (3, 0): every(0, 1, FINE) + [(3, 19, GAP_SIXTEEN)],
        (4, 0): every(0, 4, GAP_FOUR),
        (5, 0): every(1, 1, FINE),
        (6, 0): every(2, 1, FINE) + [(16, 32, GAP_SIXTEEN)],
        (7, 0): every(3, 1, RESTRICT),
        (8, 0): [(8, 12, LEVEL), (20, 24, LEVEL)],
        (9, 0): [(12, 16, LEVEL), (24, 28, LEVEL)],
        (10, 0): [(16, 20, LEVEL), (28, 32, LEVEL)],
        (11, 0): [(20, 24, LEVEL), (16, 32, COARSEST)],
        (12, 0): [(24, 28, LEVEL)],
        (12, 1): [(24, 25, FINE)],
        (13, 0): [(28, 29, FINE), (25, 26, FINE)],
        (14, 0): [(29, 30, FINE), (26, 27, FINE), (28, 32, GAP_FOUR)],
        (15, 0): [(30, 31, FINE)],
        (15, 1): [(27, 31, GAP_FOUR)],
    }
    restricted = 7
    like = {(0, 0): (5, 0), (1, 0): (6, 0), (2, 0): (7, 0), (15, 0): (6, 0), (8, 0): (10, 0)}
    closed = {(n, 0) for n in (0, 1, 2, 3, 5, 7, 15)}

    final = {1: -1, 2: 0, 3: 1, 4: 2, 5: 3, 6: 5, 7: 6, 8: 7}
    final.update({12: 8, 16: 9, 20: 10, 24: 11, 28: 12, 32: 11, 25: 12, 26: 13, 27: 14, 29: 13, 30: 14, 31: 15})

    def place(source, target, job, first):
        for key in sorted(hops):
            group = [key] + [k for k in hops if like.get(k) == key or like.get(key) == k]
            if key[0] < first or key in closed:
                continue
            if any(a == source or b == target for k in group for a, b, unused in hops[k]):
                continue
            if any(b == target for k in hops if k[0] == key[0] for unused, b, held in hops[k]):
                continue
            hops[key].append((source, target, job))
            return key[0]
        raise ValueError((source, target, job))

    for anchor in (8, 12, 16, 20):
        for n in (anchor + 1, anchor + 2, anchor + 3):
            final[n] = place(n - 1, n, FINE, max(final[n - 1], restricted) + 1)
    wanted = []
    for n in range(5, layers + 1):
        if n % 4 != 0 and n != 31:
            wanted.append((final[n - 4], n - 4, n, GAP_FOUR))
    for n in range(17, layers):
        if n != 19:
            wanted.append((final[n - 16], n - 16, n, GAP_SIXTEEN))
    for ready, source, target, job in sorted(wanted, key=lambda want: (-want[0], want)):
        place(source, target, job, max(13 if target == 24 else 4, ready + 1))

    routes = {key: [(a, b) for a, b, unused in pairs] for key, pairs in hops.items()}
    for key, other in like.items():
        routes[other] = routes[other] + [pair for pair in routes[key] if pair not in routes[other]]
    for key, other in like.items():
        routes[key] = routes[other]
    return hops, routes, restricted


def gathering(routes, planes):
    root = 2

    def within(pairs):
        return [(a - 1, b - 1) for a, b in pairs]

    steps = [
        ((8, 0), "layer", within([(n, n - 1) for n in range(8, 33, 4)]), ADD),
        ((8, 1), "layer", within([(7, 3), (15, 11), (23, 19), (31, 27)]), ADD),
        ((9, 0), "layer", within([(11, 3), (27, 19)]), ADD),
        ((9, 1), "layer", within([(19, 3)]), ADD),
    ]
    for when, distance in (((10, 0), 1), ((10, 1), 2), ((11, 0), 4)):
        pairs = [(root * planes + i, root * planes + (i ^ distance)) for i in range(planes)]
        steps.append((when, ("layer", "dp"), pairs, ADD))
    steps.append(((11, 1), "layer", within(routes[3, 0]), (19,)))
    steps.append(((12, 1), "layer", within([(3, 11), (19, 27)]), (11, 27)))
    steps.append(((13, 1), "layer", within([(3, 7), (11, 15), (19, 23), (27, 31)]), (7, 15, 23, 31)))
    steps.append(((14, 1), "layer", within(routes[7, 0]), tuple(range(4, 33, 4))))
    last = [(n, n % 32 + 1) for n in range(4, 33, 4)] + [(n, n - 1) for n in range(3, 33, 4)]
    steps.append((None, "layer", within(last), tuple(n for n in range(1, 33) if n % 4 in (1, 2))))
    return steps


def member(points):
    place = lax.axis_index("layer").astype(jnp.int32)
    mask = 0
    for n in points:
        mask |= 1 << (n - 1)
    if mask >= 2**31:
        mask -= 2**32
    return (lax.shift_right_logical(jnp.int32(mask), place) & 1) == 1


def taken(held_ref, arrived_ref, receivers, target_ref):
    if receivers == ADD:
        target_ref[...] = held_ref[...] + arrived_ref[...]
    else:
        here = member(receivers)

        @pl.when(here)
        def replace():
            target_ref[...] = arrived_ref[...]

        @pl.when(jnp.logical_not(here))
        def keep():
            target_ref[...] = held_ref[...]


def normalised(state, gain_ref):
    mean_square = jnp.mean(state * state, axis=-1, keepdims=True)
    return (state * lax.rsqrt(mean_square + epsilon) * gain_ref[...]).astype(jnp.bfloat16)


def chunk_of(normed, first_ref, second_ref, start, width):
    hidden = jax.nn.gelu(
        jnp.dot(normed, first_ref[:, start : start + width], preferred_element_type=jnp.float32),
        approximate=True,
    ).astype(jnp.bfloat16)
    return jnp.dot(hidden, second_ref[start : start + width, :], preferred_element_type=jnp.float32)


def branch(state, gain_ref, first_ref, second_ref):
    normed = normalised(state, gain_ref)
    total = None
    for start in range(0, first_ref.shape[1], CHUNK):
        part = chunk_of(normed, first_ref, second_ref, start, CHUNK)
        total = part if total is None else total + part
    return total


WHOLE = pl.BlockSpec(memory_space=pltpu.VMEM)
FAR = pl.BlockSpec(memory_space=pltpu.HBM)
TOKEN = jax.ShapeDtypeStruct((8, 128), jnp.float32)


def settings(rows, mebibytes=8):
    return dict(
        compiler_params=pltpu.CompilerParams(vmem_limit_bytes=mebibytes * 2**20),
        cost_estimate=pl.CostEstimate(flops=4 * rows * 1024 * 2048 * 4, bytes_accessed=2**20, transcendentals=0),
    )


def first_kernel(state_hbm, gain_hbm, first_hbm, second_hbm, token_ref, gain_ref, first_ref, second_ref, *refs):
    state_ref, sems = refs[-2:]
    small = [
        pltpu.make_async_copy(state_hbm, state_ref, sems.at[2 * LOADS]),
        pltpu.make_async_copy(gain_hbm, gain_ref, sems.at[2 * LOADS + 1]),
    ]
    for copy in small:
        copy.start()
    width = first_hbm.shape[1] // LOADS
    copies = []
    for k in range(LOADS):
        columns = pl.ds(k * width, width)
        copies.append(pltpu.make_async_copy(first_hbm.at[:, columns], first_ref.at[:, columns], sems.at[2 * k]))
        copies.append(pltpu.make_async_copy(second_hbm.at[columns, :], second_ref.at[columns, :], sems.at[2 * k + 1]))
    for copy in copies:
        copy.start()
    token_ref[...] = jnp.zeros(token_ref.shape, jnp.float32)
    for copy in small:
        copy.wait()
    state = state_ref[...]
    normed = normalised(state, gain_ref)
    update = None
    for k in range(LOADS):
        copies[2 * k].wait()
        copies[2 * k + 1].wait()
        part = chunk_of(normed, first_ref, second_ref, k * width, width)
        update = part if update is None else update + part
    rows = state.shape[0] // PORTIONS
    for portion in range(PORTIONS):
        mine = slice(portion * rows, (portion + 1) * rows)
        for k, spacing in enumerate((1.0, 4.0, 16.0)):
            refs[3 * portion + k][...] = state[mine] + spacing * update[mine]


def first_round(initial, gain, first, second):
    rows = initial.shape[0] // PORTIONS
    block = jax.ShapeDtypeStruct((rows, initial.shape[1]), jnp.float32)
    made = pl.pallas_call(
        first_kernel,
        out_shape=(
            TOKEN,
            jax.ShapeDtypeStruct(gain.shape, gain.dtype),
            jax.ShapeDtypeStruct(first.shape, first.dtype),
            jax.ShapeDtypeStruct(second.shape, second.dtype),
        )
        + (block,) * (3 * PORTIONS),
        in_specs=[FAR] * 4,
        out_specs=(WHOLE,) * (4 + 3 * PORTIONS),
        scratch_shapes=[pltpu.VMEM(initial.shape, jnp.float32), pltpu.SemaphoreType.DMA((2 * LOADS + 2,))],
        **settings(initial.shape[0], 43),
    )(initial, gain, first, second)
    states = [
        dict(zip(("current", "four", "sixteen"), made[4 + 3 * k : 7 + 3 * k])) for k in range(PORTIONS)
    ]
    return made[0], made[1:4], states


def targets(jobs):
    return [n for points in jobs.values() for n in points]


def round_kernel(jobs, more, names_in, names_out, receivers, *refs):
    given = dict(zip(names_in, refs))
    made = dict(zip(names_out, refs[len(names_in) :]))
    picked_ref, update_ref = refs[-2:]
    rows = given["arrived"].shape[0]
    place = lax.axis_index("layer").astype(jnp.int32)
    made["token"][...] = given["token"][...]
    doubled = sorted(set(targets(jobs)) & set(targets(more)))
    layer = (given["gain"], given["first"], given["second"])

    if more:

        @pl.when(member(targets(jobs)))
        def pick():
            picked_ref[:rows, :] = given["arrived"][...]

        @pl.when(member(sorted(set(targets(more)) - set(doubled))))
        def pick_other():
            picked_ref[:rows, :] = given["other"][...]

    busy = sorted((set(targets(jobs)) | set(targets(more))) - set(doubled))

    @pl.when(member(busy))
    def compute():
        state = picked_ref[:rows, :] if more else given["arrived"][...]
        update_ref[:rows, :] = branch(state, *layer)

    if doubled:

        @pl.when(member(doubled))
        def compute_both():
            picked_ref[rows:, :] = given["other"][...]
            update_ref[...] = branch(picked_ref[...], *layer)

    both = {job: sorted(jobs.get(job, []) + more.get(job, [])) for job in set(jobs) | set(more)}
    for name, writers in WRITERS.items():
        if name in made and name in given:

            @pl.when(jnp.logical_not(member([n for job in writers for n in both.get(job, ())])))
            def keep(name=name):
                made[name][...] = given[name][...]

    if "partner" in given:
        taken(given["sums"], given["partner"], receivers, made["sums"])
    elif "sums" in given:
        made["sums"][...] = given["sums"][...]
    elif "sums" in made:
        made["sums"][...] = jnp.zeros(made["sums"].shape, jnp.float32)

    def finish(job, stepped, update):
        if job == FINE:
            made["current"][...] = stepped
        if job == LEVEL:
            made["four"][...] = stepped
            made["current"][...] = stepped + given["coarse"][...]
        if job == GAP_FOUR:
            made["four"][...] = stepped
        if job == GAP_SIXTEEN:
            made["sixteen"][...] = stepped
        if job == COARSEST:
            made["current"][...] = given["current"][...] + (stepped - given["sixteen"][...])
            made["sixteen"][...] = stepped
        if job == RESTRICT:
            gap = stepped - given["current"][...]
            made["current"][...] = stepped
            made["coarse"][...] = stepped - given["four"][...]
            shape = made["sums"].shape
            row = lax.broadcasted_iota(jnp.int32, shape, 0)
            here = lax.broadcasted_iota(jnp.int32, shape, 1) == (place + 1) // 4 - 2
            pair = jnp.where(row == 0, jnp.sum(gap * gap), jnp.sum(update * update))
            made["sums"][...] += jnp.where(here & (row < 2), pair, 0.0)

    for hop, name, start in ((jobs, "arrived", 0), (more, "other", rows)):
        for job, points in hop.items():
            for twice in (False, True):
                mine = [n for n in points if (n in doubled) == twice]
                if mine:

                    @pl.when(member(mine))
                    def done(job=job, name=name, start=start if twice else 0):
                        update = update_ref[start : start + rows, :]
                        finish(job, given[name][...] + SPACING[job] * update, update)


WRITERS = {
    "current": {FINE, LEVEL, RESTRICT, COARSEST},
    "four": {LEVEL, GAP_FOUR},
    "sixteen": {GAP_SIXTEEN, COARSEST},
    "coarse": {RESTRICT},
}
READERS = {
    "current": {FINE, LEVEL, RESTRICT, COARSEST},
    "four": {RESTRICT, LEVEL, GAP_FOUR},
    "sixteen": {GAP_SIXTEEN, COARSEST},
    "coarse": {LEVEL},
}


def by_job(pairs):
    jobs = {}
    for unused, target, job in pairs:
        jobs.setdefault(job, []).append(target)
    return jobs


def run_round(arrivals, state, layer, hops, token, sums, receivers):
    jobs, more = by_job(hops[0]), by_job(hops[1] if len(hops) > 1 else [])
    kinds = set(jobs) | set(more)
    names_in = ["arrived", "other"][: len(arrivals)] + ["gain", "first", "second", "token"]
    values = [*arrivals, *layer, token]
    names_out, shapes = ["token"], [TOKEN]
    rows, width = arrivals[0].shape
    block = jax.ShapeDtypeStruct((rows, width), jnp.float32)
    for name, writers in WRITERS.items():
        if name in state and kinds & READERS[name]:
            names_in.append(name)
            values.append(state[name])
        if kinds & writers:
            names_out.append(name)
            shapes.append(block)
    names_in += list(sums)
    values += list(sums.values())
    if RESTRICT in kinds or sums:
        names_out.append("sums")
        shapes.append(TOKEN)
    scratch = pltpu.VMEM((rows * len(arrivals), width), jnp.float32)
    made = pl.pallas_call(
        functools.partial(round_kernel, jobs, more, names_in, names_out, receivers),
        out_shape=tuple(shapes),
        in_specs=[WHOLE] * len(names_in),
        out_specs=(WHOLE,) * len(shapes),
        scratch_shapes=[scratch, scratch],
        **settings(rows),
    )(*values)
    return dict(zip(names_out, made))


def finish_kernel(receivers, sums_ref, partner_ref, token_ref, *refs):
    given = refs[: 3 * PORTIONS]
    outs = refs[3 * PORTIONS : 3 * PORTIONS + 3]
    ratios_ref, *scratch, total_ref, sems = refs[3 * PORTIONS + 3 :]
    point = lax.axis_index("layer") + 1
    rows = given[0].shape[0]
    copies = []

    def send(source, target, portion):
        block = target.at[0, pl.ds(portion * rows, rows), :]
        copies.append(pltpu.make_async_copy(source, block, sems.at[len(copies)]))
        copies[-1].start()

    for portion in range(PORTIONS):
        send(given[3 * portion], outs[0], portion)
    for portion in range(PORTIONS):
        current, *coarser = given[3 * portion : 3 * portion + 3]
        mine = pl.ds(portion * rows, rows)
        for ref, made, least, out in zip(coarser, scratch, (4, 16), outs[1:]):
            made[mine, :] = jnp.where(point >= least, current[...] - ref[...], 0.0)
            send(made.at[mine, :], out, portion)
    taken(sums_ref, partner_ref, receivers, total_ref)
    sums = total_ref[...]
    ratios_ref[...] = jnp.sqrt(sums[0:1] / (sums[1:2] + epsilon))
    for copy in copies:
        copy.wait()


def finish(states, sums, partner, receivers, token):
    rows, width = states[0]["current"].shape
    whole = jax.ShapeDtypeStruct((1, rows * PORTIONS, width), jnp.float32)
    values = [state[name] for state in states for name in ("current", "four", "sixteen")]
    layer_states, defects_four, defects_sixteen, ratios = pl.pallas_call(
        functools.partial(finish_kernel, receivers),
        out_shape=(whole, whole, whole, jax.ShapeDtypeStruct((1, 128), jnp.float32)),
        in_specs=[WHOLE] * (3 + len(values)),
        out_specs=(FAR, FAR, FAR, WHOLE),
        scratch_shapes=[pltpu.VMEM((rows * PORTIONS, width), jnp.float32)] * 2
        + [pltpu.VMEM(TOKEN.shape, jnp.float32), pltpu.SemaphoreType.DMA((3 * PORTIONS,))],
        compiler_params=pltpu.CompilerParams(vmem_limit_bytes=8 * 2**20),
    )(sums, partner, token, *values)
    return layer_states, ratios[0, :7], defects_four, defects_sixteen


def local(initial, norm_gains, first_weights, second_weights):
    layers = lax.axis_size("layer")
    hops, routes, restricted = plan(layers)
    token, layer, states = first_round(initial, norm_gains, first_weights[0], second_weights[0])
    steps = gathering(routes, lax.axis_size("dp"))
    sums, partner, receivers, due = None, None, None, None
    for index in range(max(hops)[0] + 1):
        keys = sorted(key for key in hops if key[0] == index)
        for portion in range(PORTIONS):
            current = states[portion]["current"]
            arrivals = [lax.ppermute(current, "layer", [(a - 1, b - 1) for a, b in routes[key]]) for key in keys]
            adding, taking = {}, None
            if sums is not None and index == restricted:
                adding = {"sums": sums}
            if due == (index, portion):
                adding, taking = {"sums": sums, "partner": partner}, receivers
            made = run_round(arrivals, states[portion], layer, [hops[key] for key in keys], token, adding, taking)
            token = made.pop("token")
            sums = made.pop("sums", sums)
            states[portion].update(made)
            if due == (index, portion) or (index == restricted and portion == PORTIONS - 1):
                due, axes, ring, receivers = steps.pop(0)
                partner = lax.ppermute(sums, axes, ring)
    assert not steps and due is None
    return finish(states, sums, partner, receivers, token)


def solution(mesh):
    placed = (P("dp", None), P("layer", None), P("layer", None, None), P("layer", None, None))
    return jax.shard_map(
        local,
        mesh=mesh,
        in_specs=placed,
        out_specs=(P("layer", "dp", None), P(), P("layer", "dp", None), P("layer", "dp", None)),
        check_vma=False,
    )
```

```python
import functools

import jax
import jax.numpy as jnp
from jax import lax
from jax.experimental import pallas as pl
from jax.experimental.pallas import tpu as pltpu
from jax.sharding import PartitionSpec as P

epsilon = 1e-06
PORTIONS = 2
CHUNK = 1024
LOADS = 4

ADD = "add"
FINE, LEVEL, GAP_FOUR, GAP_SIXTEEN, RESTRICT, COARSEST = 1, 2, 3, 4, 5, 6
SPACING = {FINE: 1.0, LEVEL: 4.0, GAP_FOUR: 4.0, GAP_SIXTEEN: 16.0, RESTRICT: 1.0, COARSEST: 16.0}


def plan(layers):
    def every(residue, shift, job):
        return [(n, n + shift, job) for n in range(1, layers - shift + 1) if n % 4 == residue]

    hops = {
        (0, 0): every(1, 1, FINE),
        (1, 0): every(2, 1, FINE),
        (2, 0): every(3, 1, FINE),
        (3, 0): every(0, 1, FINE) + [(3, 19, GAP_SIXTEEN)],
        (4, 0): every(0, 4, GAP_FOUR),
        (5, 0): every(1, 1, FINE),
        (6, 0): every(2, 1, FINE) + [(16, 32, GAP_SIXTEEN)],
        (7, 0): every(3, 1, RESTRICT),
        (8, 0): [(8, 12, LEVEL), (20, 24, LEVEL)],
        (9, 0): [(12, 16, LEVEL), (24, 28, LEVEL)],
        (10, 0): [(16, 20, LEVEL), (28, 32, LEVEL)],
        (11, 0): [(20, 24, LEVEL), (16, 32, COARSEST)],
        (12, 0): [(24, 28, LEVEL)],
        (12, 1): [(24, 25, FINE)],
        (13, 0): [(28, 29, FINE), (25, 26, FINE)],
        (14, 0): [(29, 30, FINE), (26, 27, FINE), (28, 32, GAP_FOUR)],
        (15, 0): [(30, 31, FINE)],
        (15, 1): [(27, 31, GAP_FOUR)],
    }
    restricted = 7
    like = {(0, 0): (5, 0), (1, 0): (6, 0), (2, 0): (7, 0), (15, 0): (6, 0), (9, 0): (11, 0)}
    closed = {(n, 0) for n in (0, 1, 2, 3, 5, 7, 15)}

    final = {1: -1, 2: 0, 3: 1, 4: 2, 5: 3, 6: 5, 7: 6, 8: 7}
    final.update({12: 8, 16: 9, 20: 10, 24: 11, 28: 12, 32: 11, 25: 12, 26: 13, 27: 14, 29: 13, 30: 14, 31: 15})

    def place(source, target, job, first):
        for key in sorted(hops):
            group = [key] + [k for k in hops if like.get(k) == key or like.get(key) == k]
            if key[0] < first or key in closed:
                continue
            if any(a == source or b == target for k in group for a, b, unused in hops[k]):
                continue
            if any(b == target for k in hops if k[0] == key[0] for unused, b, held in hops[k]):
                continue
            hops[key].append((source, target, job))
            return key[0]
        raise ValueError((source, target, job))

    for anchor in (8, 12, 16, 20):
        for n in (anchor + 1, anchor + 2, anchor + 3):
            final[n] = place(n - 1, n, FINE, max(final[n - 1], restricted) + 1)
    wanted = []
    for n in range(5, layers + 1):
        if n % 4 != 0 and n != 31:
            wanted.append((final[n - 4], n - 4, n, GAP_FOUR))
    for n in range(17, layers):
        if n != 19:
            wanted.append((final[n - 16], n - 16, n, GAP_SIXTEEN))
    for ready, source, target, job in sorted(wanted, key=lambda want: (-want[0], want)):
        place(source, target, job, max(13 if target == 24 else 4, ready + 1))

    routes = {key: [(a, b) for a, b, unused in pairs] for key, pairs in hops.items()}
    for key, other in like.items():
        routes[other] = routes[other] + [pair for pair in routes[key] if pair not in routes[other]]
    routes[15, 1] = routes[15, 1] + [(3, 11)]
    for key, other in like.items():
        routes[key] = routes[other]
    return hops, routes, restricted


def gathering(routes, planes):
    root = 2

    def within(pairs):
        return [(a - 1, b - 1) for a, b in pairs]

    steps = [
        (8, "layer", within([(n, n - 1) for n in range(8, 33, 4)]), ADD),
        (8, "layer", within([(7, 3), (15, 11), (23, 19), (31, 27)]), ADD),
        (8, "layer", within([(11, 3), (27, 19)]), ADD),
        (9, "layer", within([(19, 3)]), ADD),
    ]
    for follows, distance in ((9, 1), (9, 2), (10, 4)):
        pairs = [(root * planes + i, root * planes + (i ^ distance)) for i in range(planes)]
        steps.append((follows, ("layer", "dp"), pairs, ADD))
    assert (3, 19) in routes[3, 0] and (19, 23) in routes[15, 1]
    steps.append((12, "layer", within(routes[3, 0]), (19,)))
    steps.append((13, "layer", within(routes[15, 1]), (11, 23)))
    steps.append((15, "layer", within([(3, 7), (11, 15), (19, 27), (23, 31)]), (7, 15, 27, 31)))
    steps.append((15, "layer", within(routes[7, 0]), tuple(range(4, 33, 4))))
    last = [(n, n % 32 + 1) for n in range(4, 33, 4)] + [(n, n - 1) for n in range(3, 33, 4)]
    steps.append((16, "layer", within(last), tuple(n for n in range(1, 33) if n % 4 in (1, 2))))
    return steps


def member(points):
    place = lax.axis_index("layer").astype(jnp.int32)
    mask = 0
    for n in points:
        mask |= 1 << (n - 1)
    if mask >= 2**31:
        mask -= 2**32
    return (lax.shift_right_logical(jnp.int32(mask), place) & 1) == 1


def taken(held_ref, arrived_ref, receivers, target_ref):
    if receivers == ADD:
        target_ref[...] = held_ref[...] + arrived_ref[...]
    else:
        here = member(receivers)

        @pl.when(here)
        def replace():
            target_ref[...] = arrived_ref[...]

        @pl.when(jnp.logical_not(here))
        def keep():
            target_ref[...] = held_ref[...]


def normalised(state, gain_ref):
    mean_square = jnp.mean(state * state, axis=-1, keepdims=True)
    return (state * lax.rsqrt(mean_square + epsilon) * gain_ref[...]).astype(jnp.bfloat16)


def chunk_of(normed, first_ref, second_ref, start, width):
    hidden = jax.nn.gelu(
        jnp.dot(normed, first_ref[:, start : start + width], preferred_element_type=jnp.float32),
        approximate=True,
    ).astype(jnp.bfloat16)
    return jnp.dot(hidden, second_ref[start : start + width, :], preferred_element_type=jnp.float32)


def branch(state, gain_ref, first_ref, second_ref):
    normed = normalised(state, gain_ref)
    total = None
    for start in range(0, first_ref.shape[1], CHUNK):
        part = chunk_of(normed, first_ref, second_ref, start, CHUNK)
        total = part if total is None else total + part
    return total


WHOLE = pl.BlockSpec(memory_space=pltpu.VMEM)
FAR = pl.BlockSpec(memory_space=pltpu.HBM)
TOKEN = jax.ShapeDtypeStruct((8, 128), jnp.float32)


def settings(rows, mebibytes=8):
    return dict(
        compiler_params=pltpu.CompilerParams(vmem_limit_bytes=mebibytes * 2**20),
        cost_estimate=pl.CostEstimate(flops=4 * rows * 1024 * 2048 * 4, bytes_accessed=2**20, transcendentals=0),
    )


def first_kernel(state_hbm, gain_hbm, first_hbm, second_hbm, token_ref, gain_ref, first_ref, second_ref, *refs):
    state_ref, sems = refs[-2:]
    small = [
        pltpu.make_async_copy(state_hbm, state_ref, sems.at[2 * LOADS]),
        pltpu.make_async_copy(gain_hbm, gain_ref, sems.at[2 * LOADS + 1]),
    ]
    for copy in small:
        copy.start()
    width = first_hbm.shape[1] // LOADS
    copies = []
    for k in range(LOADS):
        columns = pl.ds(k * width, width)
        copies.append(pltpu.make_async_copy(first_hbm.at[:, columns], first_ref.at[:, columns], sems.at[2 * k]))
        copies.append(pltpu.make_async_copy(second_hbm.at[columns, :], second_ref.at[columns, :], sems.at[2 * k + 1]))
    for copy in copies:
        copy.start()
    token_ref[...] = jnp.zeros(token_ref.shape, jnp.float32)
    for copy in small:
        copy.wait()
    state = state_ref[...]
    normed = normalised(state, gain_ref)
    update = None
    for k in range(LOADS):
        copies[2 * k].wait()
        copies[2 * k + 1].wait()
        part = chunk_of(normed, first_ref, second_ref, k * width, width)
        update = part if update is None else update + part
    rows = state.shape[0] // PORTIONS
    for portion in range(PORTIONS):
        mine = slice(portion * rows, (portion + 1) * rows)
        for k, spacing in enumerate((1.0, 4.0, 16.0)):
            refs[3 * portion + k][...] = state[mine] + spacing * update[mine]


def first_round(initial, gain, first, second):
    rows = initial.shape[0] // PORTIONS
    block = jax.ShapeDtypeStruct((rows, initial.shape[1]), jnp.float32)
    made = pl.pallas_call(
        first_kernel,
        out_shape=(
            TOKEN,
            jax.ShapeDtypeStruct(gain.shape, gain.dtype),
            jax.ShapeDtypeStruct(first.shape, first.dtype),
            jax.ShapeDtypeStruct(second.shape, second.dtype),
        )
        + (block,) * (3 * PORTIONS),
        in_specs=[FAR] * 4,
        out_specs=(WHOLE,) * (4 + 3 * PORTIONS),
        scratch_shapes=[pltpu.VMEM(initial.shape, jnp.float32), pltpu.SemaphoreType.DMA((2 * LOADS + 2,))],
        **settings(initial.shape[0], 43),
    )(initial, gain, first, second)
    states = [
        dict(zip(("current", "four", "sixteen"), made[4 + 3 * k : 7 + 3 * k])) for k in range(PORTIONS)
    ]
    return made[0], made[1:4], states


def targets(jobs):
    return [n for points in jobs.values() for n in points]


def round_kernel(jobs, more, names_in, names_out, *refs):
    given = dict(zip(names_in, refs))
    made = dict(zip(names_out, refs[len(names_in) :]))
    picked_ref, update_ref = refs[-2:]
    rows = given["arrived"].shape[0]
    place = lax.axis_index("layer").astype(jnp.int32)
    made["token"][...] = given["token"][...]
    doubled = sorted(set(targets(jobs)) & set(targets(more)))
    layer = (given["gain"], given["first"], given["second"])

    if more:

        @pl.when(member(targets(jobs)))
        def pick():
            picked_ref[:rows, :] = given["arrived"][...]

        @pl.when(member(sorted(set(targets(more)) - set(doubled))))
        def pick_other():
            picked_ref[:rows, :] = given["other"][...]

    busy = sorted((set(targets(jobs)) | set(targets(more))) - set(doubled))

    @pl.when(member(busy))
    def compute():
        state = picked_ref[:rows, :] if more else given["arrived"][...]
        update_ref[:rows, :] = branch(state, *layer)

    if doubled:

        @pl.when(member(doubled))
        def compute_both():
            picked_ref[rows:, :] = given["other"][...]
            update_ref[...] = branch(picked_ref[...], *layer)

    both = {job: sorted(jobs.get(job, []) + more.get(job, [])) for job in set(jobs) | set(more)}
    for name, writers in WRITERS.items():
        if name in made and name in given:

            @pl.when(jnp.logical_not(member([n for job in writers for n in both.get(job, ())])))
            def keep(name=name):
                made[name][...] = given[name][...]

    if "sums" in given:
        made["sums"][...] = given["sums"][...]
    elif "sums" in made:
        made["sums"][...] = jnp.zeros(made["sums"].shape, jnp.float32)

    def finish(job, stepped, update):
        if job == FINE:
            made["current"][...] = stepped
        if job == LEVEL:
            made["four"][...] = stepped
            made["current"][...] = stepped + given["coarse"][...]
        if job == GAP_FOUR:
            made["four"][...] = stepped
        if job == GAP_SIXTEEN:
            made["sixteen"][...] = stepped
        if job == COARSEST:
            made["current"][...] = given["current"][...] + (stepped - given["sixteen"][...])
            made["sixteen"][...] = stepped
        if job == RESTRICT:
            gap = stepped - given["current"][...]
            made["current"][...] = stepped
            made["coarse"][...] = stepped - given["four"][...]
            shape = made["sums"].shape
            row = lax.broadcasted_iota(jnp.int32, shape, 0)
            here = lax.broadcasted_iota(jnp.int32, shape, 1) == (place + 1) // 4 - 2
            pair = jnp.where(row == 0, jnp.sum(gap * gap), jnp.sum(update * update))
            made["sums"][...] += jnp.where(here & (row < 2), pair, 0.0)

    for hop, name, start in ((jobs, "arrived", 0), (more, "other", rows)):
        for job, points in hop.items():
            for twice in (False, True):
                mine = [n for n in points if (n in doubled) == twice]
                if mine:

                    @pl.when(member(mine))
                    def done(job=job, name=name, start=start if twice else 0):
                        update = update_ref[start : start + rows, :]
                        finish(job, given[name][...] + SPACING[job] * update, update)


WRITERS = {
    "current": {FINE, LEVEL, RESTRICT, COARSEST},
    "four": {LEVEL, GAP_FOUR},
    "sixteen": {GAP_SIXTEEN, COARSEST},
    "coarse": {RESTRICT},
}
READERS = {
    "current": {FINE, LEVEL, RESTRICT, COARSEST},
    "four": {RESTRICT, LEVEL, GAP_FOUR},
    "sixteen": {GAP_SIXTEEN, COARSEST},
    "coarse": {LEVEL},
}


def by_job(pairs):
    jobs = {}
    for unused, target, job in pairs:
        jobs.setdefault(job, []).append(target)
    return jobs


def run_round(arrivals, state, layer, hops, token, sums):
    jobs, more = by_job(hops[0]), by_job(hops[1] if len(hops) > 1 else [])
    kinds = set(jobs) | set(more)
    names_in = ["arrived", "other"][: len(arrivals)] + ["gain", "first", "second", "token"]
    values = [*arrivals, *layer, token]
    names_out, shapes = ["token"], [TOKEN]
    rows, width = arrivals[0].shape
    block = jax.ShapeDtypeStruct((rows, width), jnp.float32)
    for name, writers in WRITERS.items():
        if name in state and kinds & READERS[name]:
            names_in.append(name)
            values.append(state[name])
        if kinds & writers:
            names_out.append(name)
            shapes.append(block)
    if RESTRICT in kinds:
        if sums is not None:
            names_in.append("sums")
            values.append(sums)
        names_out.append("sums")
        shapes.append(TOKEN)
    scratch = pltpu.VMEM((rows * len(arrivals), width), jnp.float32)
    made = pl.pallas_call(
        functools.partial(round_kernel, jobs, more, names_in, names_out),
        out_shape=tuple(shapes),
        in_specs=[WHOLE] * len(names_in),
        out_specs=(WHOLE,) * len(shapes),
        scratch_shapes=[scratch, scratch],
        **settings(rows),
    )(*values)
    return dict(zip(names_out, made))


def take_kernel(receivers, sums_ref, partner_ref, token_ref, made_ref, passed_ref):
    taken(sums_ref, partner_ref, receivers, made_ref)
    passed_ref[...] = token_ref[...]


def take(sums, partner, token, receivers):
    return pl.pallas_call(
        functools.partial(take_kernel, receivers),
        out_shape=(TOKEN, TOKEN),
        in_specs=[WHOLE] * 3,
        out_specs=(WHOLE, WHOLE),
        compiler_params=pltpu.CompilerParams(vmem_limit_bytes=8 * 2**20),
    )(sums, partner, token)


def finish_kernel(receivers, sums_ref, partner_ref, token_ref, *refs):
    given = refs[: 3 * PORTIONS]
    outs = refs[3 * PORTIONS : 3 * PORTIONS + 3]
    ratios_ref, *scratch, total_ref, sems = refs[3 * PORTIONS + 3 :]
    point = lax.axis_index("layer") + 1
    rows = given[0].shape[0]
    copies = []

    def send(source, target, portion):
        block = target.at[0, pl.ds(portion * rows, rows), :]
        copies.append(pltpu.make_async_copy(source, block, sems.at[len(copies)]))
        copies[-1].start()

    for portion in range(PORTIONS):
        send(given[3 * portion], outs[0], portion)
    for portion in range(PORTIONS):
        current, *coarser = given[3 * portion : 3 * portion + 3]
        mine = pl.ds(portion * rows, rows)
        for ref, made, least, out in zip(coarser, scratch, (4, 16), outs[1:]):
            made[mine, :] = jnp.where(point >= least, current[...] - ref[...], 0.0)
            send(made.at[mine, :], out, portion)
    taken(sums_ref, partner_ref, receivers, total_ref)
    sums = total_ref[...]
    ratios_ref[...] = jnp.sqrt(sums[0:1] / (sums[1:2] + epsilon))
    for copy in copies:
        copy.wait()


def finish(states, sums, partner, receivers, token):
    rows, width = states[0]["current"].shape
    whole = jax.ShapeDtypeStruct((1, rows * PORTIONS, width), jnp.float32)
    values = [state[name] for state in states for name in ("current", "four", "sixteen")]
    layer_states, defects_four, defects_sixteen, ratios = pl.pallas_call(
        functools.partial(finish_kernel, receivers),
        out_shape=(whole, whole, whole, jax.ShapeDtypeStruct((1, 128), jnp.float32)),
        in_specs=[WHOLE] * (3 + len(values)),
        out_specs=(FAR, FAR, FAR, WHOLE),
        scratch_shapes=[pltpu.VMEM((rows * PORTIONS, width), jnp.float32)] * 2
        + [pltpu.VMEM(TOKEN.shape, jnp.float32), pltpu.SemaphoreType.DMA((3 * PORTIONS,))],
        compiler_params=pltpu.CompilerParams(vmem_limit_bytes=8 * 2**20),
    )(sums, partner, token, *values)
    return layer_states, ratios[0, :7], defects_four, defects_sixteen


def local(initial, norm_gains, first_weights, second_weights):
    layers = lax.axis_size("layer")
    hops, routes, restricted = plan(layers)
    token, layer, states = first_round(initial, norm_gains, first_weights[0], second_weights[0])
    steps = gathering(routes, lax.axis_size("dp"))
    sums = None
    last = max(hops)[0] + 1
    for index in range(last):
        while index > restricted and steps[0][0] == index:
            unused, axes, pairs, receivers = steps.pop(0)
            sums, token = take(sums, lax.ppermute(sums, axes, pairs), token, receivers)
        keys = sorted(key for key in hops if key[0] == index)
        for portion in range(PORTIONS):
            current = states[portion]["current"]
            arrivals = [lax.ppermute(current, "layer", [(a - 1, b - 1) for a, b in routes[key]]) for key in keys]
            made = run_round(arrivals, states[portion], layer, [hops[key] for key in keys], token, sums)
            token = made.pop("token")
            sums = made.pop("sums", sums)
            states[portion].update(made)
    ((follows, axes, pairs, receivers),) = steps
    assert follows == last
    return finish(states, sums, lax.ppermute(sums, axes, pairs), receivers, token)


def solution(mesh):
    placed = (P("dp", None), P("layer", None), P("layer", None, None), P("layer", None, None))
    return jax.shard_map(
        local,
        mesh=mesh,
        in_specs=placed,
        out_specs=(P("layer", "dp", None), P(), P("layer", "dp", None), P("layer", "dp", None)),
        check_vma=False,
    )
```

```python
import functools

import jax
import jax.numpy as jnp
from jax import lax
from jax.experimental import pallas as pl
from jax.experimental.pallas import tpu as pltpu
from jax.sharding import PartitionSpec as P

epsilon = 1e-06
PORTIONS = 2
CHUNK = 1024
LOADS = 4

ADD = "add"
FINE, LEVEL, GAP_FOUR, GAP_SIXTEEN, RESTRICT, COARSEST = 1, 2, 3, 4, 5, 6
SPACING = {FINE: 1.0, LEVEL: 4.0, GAP_FOUR: 4.0, GAP_SIXTEEN: 16.0, RESTRICT: 1.0, COARSEST: 16.0}


def plan(layers):
    def every(residue, shift, job):
        return [(n, n + shift, job) for n in range(1, layers - shift + 1) if n % 4 == residue]

    hops = {
        (0, 0): every(1, 1, FINE),
        (1, 0): every(2, 1, FINE),
        (2, 0): every(3, 1, FINE),
        (3, 0): every(0, 1, FINE) + [(3, 19, GAP_SIXTEEN)],
        (4, 0): every(0, 4, GAP_FOUR),
        (5, 0): every(1, 1, FINE),
        (6, 0): every(2, 1, FINE) + [(16, 32, GAP_SIXTEEN)],
        (7, 0): every(3, 1, RESTRICT),
        (8, 0): [(8, 12, LEVEL), (20, 24, LEVEL)],
        (9, 0): [(12, 16, LEVEL), (24, 28, LEVEL)],
        (10, 0): [(16, 20, LEVEL), (28, 32, LEVEL)],
        (11, 0): [(20, 24, LEVEL), (16, 32, COARSEST)],
        (12, 0): [(24, 28, LEVEL)],
        (12, 1): [(24, 25, FINE)],
        (13, 0): [(28, 29, FINE), (25, 26, FINE)],
        (14, 0): [(29, 30, FINE), (26, 27, FINE), (28, 32, GAP_FOUR)],
        (15, 0): [(30, 31, FINE)],
        (15, 1): [(27, 31, GAP_FOUR)],
    }
    restricted = 7
    like = {(0, 0): (5, 0), (1, 0): (6, 0), (2, 0): (7, 0), (15, 0): (6, 0), (9, 0): (11, 0)}
    closed = {(n, 0) for n in (0, 1, 2, 3, 5, 15)}

    final = {1: -1, 2: 0, 3: 1, 4: 2, 5: 3, 6: 5, 7: 6, 8: 7}
    final.update({12: 8, 16: 9, 20: 10, 24: 11, 28: 12, 32: 11, 25: 12, 26: 13, 27: 14, 29: 13, 30: 14, 31: 15})

    def place(source, target, job, first):
        for key in sorted(hops):
            group = [key] + [k for k in hops if like.get(k) == key or like.get(key) == k]
            if key[0] < first or key in closed:
                continue
            if any(a == source or b == target for k in group for a, b, unused in hops[k]):
                continue
            if any(b == target for k in hops if k[0] == key[0] for unused, b, held in hops[k]):
                continue
            hops[key].append((source, target, job))
            return key[0]
        raise ValueError((source, target, job))

    for anchor in (8, 12, 16, 20):
        for n in (anchor + 1, anchor + 2, anchor + 3):
            final[n] = place(n - 1, n, FINE, max(final[n - 1], restricted) + 1)
    wanted = []
    for n in range(5, layers + 1):
        if n % 4 != 0 and n != 31:
            wanted.append((final[n - 4], n - 4, n, GAP_FOUR))
    for n in range(17, layers):
        if n != 19:
            wanted.append((final[n - 16], n - 16, n, GAP_SIXTEEN))
    for ready, source, target, job in sorted(wanted, key=lambda want: (-want[0], want)):
        place(source, target, job, max(13 if target == 24 else 4, ready + 1))

    routes = {key: [(a, b) for a, b, unused in pairs] for key, pairs in hops.items()}
    for key, other in like.items():
        routes[other] = routes[other] + [pair for pair in routes[key] if pair not in routes[other]]
    assert not any(a <= 4 for key, pairs in hops.items() if key[0] > 7 for a, b, unused in pairs)
    for key, other in like.items():
        routes[key] = routes[other]
    return hops, routes, restricted


def gathering(layers, planes):
    def within(pairs):
        return "layer", [(a - 1, b - 1) for a, b in pairs]

    start = [within([(8, 1), (16, 2), (12, 3), (20, 4)]), within([(24, 1), (32, 2), (28, 3)])]
    steps = [(8, start, ADD)]
    for follows, distance in ((9, 1), (9, 2)):
        steps.append((follows, [within([(n + 1, (n ^ distance) + 1) for n in range(4)])], ADD))
    for follows, distance in ((10, 1), (10, 2), (11, 4)):
        pairs = [(n * planes + i, n * planes + (i ^ distance)) for n in range(4) for i in range(planes)]
        steps.append((follows, [(("layer", "dp"), pairs)], ADD))
    for follows, known in ((14, 4), (15, 8), (16, 16)):
        steps.append((follows, [within([(n, n + known) for n in range(1, known + 1)])], tuple(range(known + 1, 2 * known + 1))))
    assert 2 * known == layers
    return steps


def member(points):
    place = lax.axis_index("layer").astype(jnp.int32)
    mask = 0
    for n in points:
        mask |= 1 << (n - 1)
    if mask >= 2**31:
        mask -= 2**32
    return (lax.shift_right_logical(jnp.int32(mask), place) & 1) == 1


def taken(held_ref, arrived_refs, receivers, target_ref):
    if receivers == ADD:
        total = held_ref[...]
        for ref in arrived_refs:
            total = total + ref[...]
        target_ref[...] = total
    else:
        here = member(receivers)

        @pl.when(here)
        def replace():
            target_ref[...] = arrived_refs[0][...]

        @pl.when(jnp.logical_not(here))
        def keep():
            target_ref[...] = held_ref[...]


def normalised(state, gain_ref):
    mean_square = jnp.mean(state * state, axis=-1, keepdims=True)
    return (state * lax.rsqrt(mean_square + epsilon) * gain_ref[...]).astype(jnp.bfloat16)


def chunk_of(normed, first_ref, second_ref, start, width):
    hidden = jax.nn.gelu(
        jnp.dot(normed, first_ref[:, start : start + width], preferred_element_type=jnp.float32),
        approximate=True,
    ).astype(jnp.bfloat16)
    return jnp.dot(hidden, second_ref[start : start + width, :], preferred_element_type=jnp.float32)


def branch(state, gain_ref, first_ref, second_ref):
    normed = normalised(state, gain_ref)
    total = None
    for start in range(0, first_ref.shape[1], CHUNK):
        part = chunk_of(normed, first_ref, second_ref, start, CHUNK)
        total = part if total is None else total + part
    return total


WHOLE = pl.BlockSpec(memory_space=pltpu.VMEM)
FAR = pl.BlockSpec(memory_space=pltpu.HBM)
TOKEN = jax.ShapeDtypeStruct((8, 128), jnp.float32)


def settings(rows, mebibytes=8):
    return dict(
        compiler_params=pltpu.CompilerParams(vmem_limit_bytes=mebibytes * 2**20),
        cost_estimate=pl.CostEstimate(flops=4 * rows * 1024 * 2048 * 4, bytes_accessed=2**20, transcendentals=0),
    )


def first_kernel(state_hbm, gain_hbm, first_hbm, second_hbm, token_ref, gain_ref, first_ref, second_ref, *refs):
    state_ref, sems = refs[-2:]
    small = [
        pltpu.make_async_copy(state_hbm, state_ref, sems.at[2 * LOADS]),
        pltpu.make_async_copy(gain_hbm, gain_ref, sems.at[2 * LOADS + 1]),
    ]
    for copy in small:
        copy.start()
    width = first_hbm.shape[1] // LOADS
    copies = []
    for k in range(LOADS):
        columns = pl.ds(k * width, width)
        copies.append(pltpu.make_async_copy(first_hbm.at[:, columns], first_ref.at[:, columns], sems.at[2 * k]))
        copies.append(pltpu.make_async_copy(second_hbm.at[columns, :], second_ref.at[columns, :], sems.at[2 * k + 1]))
    for copy in copies:
        copy.start()
    token_ref[...] = jnp.zeros(token_ref.shape, jnp.float32)
    for copy in small:
        copy.wait()
    state = state_ref[...]
    normed = normalised(state, gain_ref)
    update = None
    for k in range(LOADS):
        copies[2 * k].wait()
        copies[2 * k + 1].wait()
        part = chunk_of(normed, first_ref, second_ref, k * width, width)
        update = part if update is None else update + part
    rows = state.shape[0] // PORTIONS
    for portion in range(PORTIONS):
        mine = slice(portion * rows, (portion + 1) * rows)
        for k, spacing in enumerate((1.0, 4.0, 16.0)):
            refs[3 * portion + k][...] = state[mine] + spacing * update[mine]


def first_round(initial, gain, first, second):
    rows = initial.shape[0] // PORTIONS
    block = jax.ShapeDtypeStruct((rows, initial.shape[1]), jnp.float32)
    made = pl.pallas_call(
        first_kernel,
        out_shape=(
            TOKEN,
            jax.ShapeDtypeStruct(gain.shape, gain.dtype),
            jax.ShapeDtypeStruct(first.shape, first.dtype),
            jax.ShapeDtypeStruct(second.shape, second.dtype),
        )
        + (block,) * (3 * PORTIONS),
        in_specs=[FAR] * 4,
        out_specs=(WHOLE,) * (4 + 3 * PORTIONS),
        scratch_shapes=[pltpu.VMEM(initial.shape, jnp.float32), pltpu.SemaphoreType.DMA((2 * LOADS + 2,))],
        **settings(initial.shape[0], 43),
    )(initial, gain, first, second)
    states = [
        dict(zip(("current", "four", "sixteen"), made[4 + 3 * k : 7 + 3 * k])) for k in range(PORTIONS)
    ]
    return made[0], made[1:4], states


def targets(jobs):
    return [n for points in jobs.values() for n in points]


def round_kernel(jobs, more, names_in, names_out, *refs):
    given = dict(zip(names_in, refs))
    made = dict(zip(names_out, refs[len(names_in) :]))
    picked_ref, update_ref = refs[-2:]
    rows = given["arrived"].shape[0]
    place = lax.axis_index("layer").astype(jnp.int32)
    made["token"][...] = given["token"][...]
    doubled = sorted(set(targets(jobs)) & set(targets(more)))
    layer = (given["gain"], given["first"], given["second"])

    if more:

        @pl.when(member(targets(jobs)))
        def pick():
            picked_ref[:rows, :] = given["arrived"][...]

        @pl.when(member(sorted(set(targets(more)) - set(doubled))))
        def pick_other():
            picked_ref[:rows, :] = given["other"][...]

    busy = sorted((set(targets(jobs)) | set(targets(more))) - set(doubled))

    @pl.when(member(busy))
    def compute():
        state = picked_ref[:rows, :] if more else given["arrived"][...]
        update_ref[:rows, :] = branch(state, *layer)

    if doubled:

        @pl.when(member(doubled))
        def compute_both():
            picked_ref[rows:, :] = given["other"][...]
            update_ref[...] = branch(picked_ref[...], *layer)

    both = {job: sorted(jobs.get(job, []) + more.get(job, [])) for job in set(jobs) | set(more)}
    for name, writers in WRITERS.items():
        if name in made and name in given:

            @pl.when(jnp.logical_not(member([n for job in writers for n in both.get(job, ())])))
            def keep(name=name):
                made[name][...] = given[name][...]

    if "sums" in given:
        made["sums"][...] = given["sums"][...]
    elif "sums" in made:
        made["sums"][...] = jnp.zeros(made["sums"].shape, jnp.float32)

    def finish(job, stepped, update):
        if job == FINE:
            made["current"][...] = stepped
        if job == LEVEL:
            made["four"][...] = stepped
            made["current"][...] = stepped + given["coarse"][...]
        if job == GAP_FOUR:
            made["four"][...] = stepped
        if job == GAP_SIXTEEN:
            made["sixteen"][...] = stepped
        if job == COARSEST:
            made["current"][...] = given["current"][...] + (stepped - given["sixteen"][...])
            made["sixteen"][...] = stepped
        if job == RESTRICT:
            gap = stepped - given["current"][...]
            made["current"][...] = stepped
            made["coarse"][...] = stepped - given["four"][...]
            shape = made["sums"].shape
            row = lax.broadcasted_iota(jnp.int32, shape, 0)
            here = lax.broadcasted_iota(jnp.int32, shape, 1) == (place + 1) // 4 - 2
            pair = jnp.where(row == 0, jnp.sum(gap * gap), jnp.sum(update * update))
            made["sums"][...] += jnp.where(here & (row < 2), pair, 0.0)

    for hop, name, start in ((jobs, "arrived", 0), (more, "other", rows)):
        for job, points in hop.items():
            for twice in (False, True):
                mine = [n for n in points if (n in doubled) == twice]
                if mine:

                    @pl.when(member(mine))
                    def done(job=job, name=name, start=start if twice else 0):
                        update = update_ref[start : start + rows, :]
                        finish(job, given[name][...] + SPACING[job] * update, update)


WRITERS = {
    "current": {FINE, LEVEL, RESTRICT, COARSEST},
    "four": {LEVEL, GAP_FOUR},
    "sixteen": {GAP_SIXTEEN, COARSEST},
    "coarse": {RESTRICT},
}
READERS = {
    "current": {FINE, LEVEL, RESTRICT, COARSEST},
    "four": {RESTRICT, LEVEL, GAP_FOUR},
    "sixteen": {GAP_SIXTEEN, COARSEST},
    "coarse": {LEVEL},
}


def by_job(pairs):
    jobs = {}
    for unused, target, job in pairs:
        jobs.setdefault(job, []).append(target)
    return jobs


def run_round(arrivals, state, layer, hops, token, sums):
    jobs, more = by_job(hops[0]), by_job(hops[1] if len(hops) > 1 else [])
    kinds = set(jobs) | set(more)
    names_in = ["arrived", "other"][: len(arrivals)] + ["gain", "first", "second", "token"]
    values = [*arrivals, *layer, token]
    names_out, shapes = ["token"], [TOKEN]
    rows, width = arrivals[0].shape
    block = jax.ShapeDtypeStruct((rows, width), jnp.float32)
    for name, writers in WRITERS.items():
        if name in state and kinds & READERS[name]:
            names_in.append(name)
            values.append(state[name])
        if kinds & writers:
            names_out.append(name)
            shapes.append(block)
    if RESTRICT in kinds:
        if sums is not None:
            names_in.append("sums")
            values.append(sums)
        names_out.append("sums")
        shapes.append(TOKEN)
    scratch = pltpu.VMEM((rows * len(arrivals), width), jnp.float32)
    made = pl.pallas_call(
        functools.partial(round_kernel, jobs, more, names_in, names_out),
        out_shape=tuple(shapes),
        in_specs=[WHOLE] * len(names_in),
        out_specs=(WHOLE,) * len(shapes),
        scratch_shapes=[scratch, scratch],
        **settings(rows),
    )(*values)
    return dict(zip(names_out, made))


def take_kernel(receivers, sums_ref, token_ref, *refs):
    *partner_refs, made_ref, passed_ref = refs
    taken(sums_ref, partner_refs, receivers, made_ref)
    passed_ref[...] = token_ref[...]


def take(sums, partners, token, receivers):
    return pl.pallas_call(
        functools.partial(take_kernel, receivers),
        out_shape=(TOKEN, TOKEN),
        in_specs=[WHOLE] * (2 + len(partners)),
        out_specs=(WHOLE, WHOLE),
        compiler_params=pltpu.CompilerParams(vmem_limit_bytes=8 * 2**20),
    )(sums, token, *partners)


def finish_kernel(receivers, sums_ref, partner_ref, token_ref, *refs):
    given = refs[: 3 * PORTIONS]
    outs = refs[3 * PORTIONS : 3 * PORTIONS + 3]
    ratios_ref, *scratch, total_ref, sems = refs[3 * PORTIONS + 3 :]
    point = lax.axis_index("layer") + 1
    rows = given[0].shape[0]
    copies = []

    def send(source, target, portion):
        block = target.at[0, pl.ds(portion * rows, rows), :]
        copies.append(pltpu.make_async_copy(source, block, sems.at[len(copies)]))
        copies[-1].start()

    for portion in range(PORTIONS):
        send(given[3 * portion], outs[0], portion)
    for portion in range(PORTIONS):
        current, *coarser = given[3 * portion : 3 * portion + 3]
        mine = pl.ds(portion * rows, rows)
        for ref, made, least, out in zip(coarser, scratch, (4, 16), outs[1:]):
            made[mine, :] = jnp.where(point >= least, current[...] - ref[...], 0.0)
            send(made.at[mine, :], out, portion)
    taken(sums_ref, (partner_ref,), receivers, total_ref)
    sums = total_ref[...]
    ratios_ref[...] = jnp.sqrt(sums[0:1] / (sums[1:2] + epsilon))
    for copy in copies:
        copy.wait()


def finish(states, sums, partner, receivers, token):
    rows, width = states[0]["current"].shape
    whole = jax.ShapeDtypeStruct((1, rows * PORTIONS, width), jnp.float32)
    values = [state[name] for state in states for name in ("current", "four", "sixteen")]
    layer_states, defects_four, defects_sixteen, ratios = pl.pallas_call(
        functools.partial(finish_kernel, receivers),
        out_shape=(whole, whole, whole, jax.ShapeDtypeStruct((1, 128), jnp.float32)),
        in_specs=[WHOLE] * (3 + len(values)),
        out_specs=(FAR, FAR, FAR, WHOLE),
        scratch_shapes=[pltpu.VMEM((rows * PORTIONS, width), jnp.float32)] * 2
        + [pltpu.VMEM(TOKEN.shape, jnp.float32), pltpu.SemaphoreType.DMA((3 * PORTIONS,))],
        compiler_params=pltpu.CompilerParams(vmem_limit_bytes=8 * 2**20),
    )(sums, partner, token, *values)
    return layer_states, ratios[0, :7], defects_four, defects_sixteen


def local(initial, norm_gains, first_weights, second_weights):
    layers = lax.axis_size("layer")
    hops, routes, restricted = plan(layers)
    token, layer, states = first_round(initial, norm_gains, first_weights[0], second_weights[0])
    steps = gathering(layers, lax.axis_size("dp"))
    sums = None
    last = max(hops)[0] + 1
    for index in range(last):
        while index > restricted and steps[0][0] == index:
            unused, ways, receivers = steps.pop(0)
            sums, token = take(sums, [lax.ppermute(sums, axes, pairs) for axes, pairs in ways], token, receivers)
        keys = sorted(key for key in hops if key[0] == index)
        for portion in range(PORTIONS):
            current = states[portion]["current"]
            arrivals = [lax.ppermute(current, "layer", [(a - 1, b - 1) for a, b in routes[key]]) for key in keys]
            made = run_round(arrivals, states[portion], layer, [hops[key] for key in keys], token, sums)
            token = made.pop("token")
            sums = made.pop("sums", sums)
            states[portion].update(made)
    ((follows, ((axes, pairs),), receivers),) = steps
    assert follows == last
    return finish(states, sums, lax.ppermute(sums, axes, pairs), receivers, token)


def solution(mesh):
    placed = (P("dp", None), P("layer", None), P("layer", None, None), P("layer", None, None))
    return jax.shard_map(
        local,
        mesh=mesh,
        in_specs=placed,
        out_specs=(P("layer", "dp", None), P(), P("layer", "dp", None), P("layer", "dp", None)),
        check_vma=False,
    )
```

```python
import functools

import jax
import jax.numpy as jnp
from jax import lax
from jax.experimental import pallas as pl
from jax.experimental.pallas import tpu as pltpu
from jax.sharding import PartitionSpec as P

epsilon = 1e-06
PORTIONS = 2
CHUNK = 1024
LOADS = 4

ADD = "add"
FINE, LEVEL, GAP_FOUR, GAP_SIXTEEN, RESTRICT, COARSEST = 1, 2, 3, 4, 5, 6
SPACING = {FINE: 1.0, LEVEL: 4.0, GAP_FOUR: 4.0, GAP_SIXTEEN: 16.0, RESTRICT: 1.0, COARSEST: 16.0}


def plan(layers):
    def every(residue, shift, job):
        return [(n, n + shift, job) for n in range(1, layers - shift + 1) if n % 4 == residue]

    hops = {
        (0, 0): every(1, 1, FINE),
        (1, 0): every(2, 1, FINE),
        (2, 0): every(3, 1, FINE),
        (3, 0): every(0, 1, FINE) + [(3, 19, GAP_SIXTEEN)],
        (4, 0): every(1, 1, FINE),
        (5, 0): every(0, 4, GAP_FOUR),
        (6, 0): every(2, 1, FINE) + [(16, 32, GAP_SIXTEEN), (4, 20, GAP_SIXTEEN)],
        (7, 0): every(3, 1, RESTRICT),
        (8, 0): [(8, 12, LEVEL), (20, 24, LEVEL)],
        (9, 0): [(12, 16, LEVEL), (24, 28, LEVEL)],
        (10, 0): [(16, 20, LEVEL), (28, 32, LEVEL)],
        (11, 0): [(20, 24, LEVEL), (16, 32, COARSEST)],
        (12, 0): [(24, 28, LEVEL)],
        (12, 1): [(24, 25, FINE)],
        (13, 0): [(28, 29, FINE), (25, 26, FINE)],
        (14, 0): [(29, 30, FINE), (26, 27, FINE), (28, 32, GAP_FOUR)],
        (15, 0): [(30, 31, FINE)],
        (15, 1): [(27, 31, GAP_FOUR)],
    }
    restricted = 7
    like = {(0, 0): (4, 0), (1, 0): (6, 0), (2, 0): (7, 0), (8, 0): (14, 0), (9, 0): (15, 1)}
    closed = {(n, 0) for n in (0, 1, 2, 3, 4, 15)}

    final = {1: -1, 2: 0, 3: 1, 4: 2, 5: 3, 6: 4, 7: 6, 8: 7}
    final.update({12: 8, 16: 9, 20: 10, 24: 11, 28: 12, 32: 11, 25: 12, 26: 13, 27: 14, 29: 13, 30: 14, 31: 15})

    def place(source, target, job, first):
        for key in sorted(hops):
            group = [key] + [k for k in hops if like.get(k) == key or like.get(key) == k]
            if key[0] < first or key in closed:
                continue
            if any(a == source or b == target for k in group for a, b, unused in hops[k]):
                continue
            if any(b == target for k in hops if k[0] == key[0] for unused, b, held in hops[k]):
                continue
            hops[key].append((source, target, job))
            return key[0]
        raise ValueError((source, target, job))

    for anchor in (8, 12, 16, 20):
        for n in (anchor + 1, anchor + 2, anchor + 3):
            final[n] = place(n - 1, n, FINE, max(final[n - 1], restricted) + 1)
    wanted = []
    for n in range(5, layers + 1):
        if n % 4 != 0 and n != 31:
            wanted.append((final[n - 4], n - 4, n, GAP_FOUR))
    for n in range(17, layers):
        if n not in (19, 20):
            wanted.append((final[n - 16], n - 16, n, GAP_SIXTEEN))
    for ready, source, target, job in sorted(wanted, key=lambda want: (-want[0], want)):
        place(source, target, job, max(13 if target == 24 else 4, ready + 1))

    routes = {key: [(a, b) for a, b, unused in pairs] for key, pairs in hops.items()}
    for key, other in like.items():
        routes[other] = routes[other] + [pair for pair in routes[key] if pair not in routes[other]]
    assert not any(a <= 4 for key, pairs in hops.items() if key[0] > 7 for a, b, unused in pairs)
    for key, other in like.items():
        routes[key] = routes[other]
    return hops, routes, restricted


def gathering(layers, planes):
    def within(pairs):
        return "layer", [(a - 1, b - 1) for a, b in pairs]

    start = [within([(8, 1), (16, 2), (12, 3), (20, 4)]), within([(24, 1), (32, 2), (28, 3)])]
    steps = [(8, start, ADD)]
    for follows, distance in ((9, 1), (9, 2)):
        steps.append((follows, [within([(n + 1, (n ^ distance) + 1) for n in range(4)])], ADD))
    for follows, distance in ((10, 1), (10, 2), (11, 4)):
        pairs = [(n * planes + i, n * planes + (i ^ distance)) for n in range(4) for i in range(planes)]
        steps.append((follows, [(("layer", "dp"), pairs)], ADD))
    for follows, known in ((12, 4), (14, 8), (16, 16)):
        steps.append((follows, [within([(n, n + known) for n in range(1, known + 1)])], tuple(range(known + 1, 2 * known + 1))))
    assert 2 * known == layers
    return steps


def member(points):
    place = lax.axis_index("layer").astype(jnp.int32)
    mask = 0
    for n in points:
        mask |= 1 << (n - 1)
    if mask >= 2**31:
        mask -= 2**32
    return (lax.shift_right_logical(jnp.int32(mask), place) & 1) == 1


def taken(held_ref, arrived_refs, receivers, target_ref):
    if receivers == ADD:
        total = held_ref[...]
        for ref in arrived_refs:
            total = total + ref[...]
        target_ref[...] = total
    else:
        here = member(receivers)

        @pl.when(here)
        def replace():
            target_ref[...] = arrived_refs[0][...]

        @pl.when(jnp.logical_not(here))
        def keep():
            target_ref[...] = held_ref[...]


def normalised(state, gain_ref):
    mean_square = jnp.mean(state * state, axis=-1, keepdims=True)
    return (state * lax.rsqrt(mean_square + epsilon) * gain_ref[...]).astype(jnp.bfloat16)


def chunk_of(normed, first_ref, second_ref, start, width):
    hidden = jax.nn.gelu(
        jnp.dot(normed, first_ref[:, start : start + width], preferred_element_type=jnp.float32),
        approximate=True,
    ).astype(jnp.bfloat16)
    return jnp.dot(hidden, second_ref[start : start + width, :], preferred_element_type=jnp.float32)


def branch(state, gain_ref, first_ref, second_ref):
    normed = normalised(state, gain_ref)
    total = None
    for start in range(0, first_ref.shape[1], CHUNK):
        part = chunk_of(normed, first_ref, second_ref, start, CHUNK)
        total = part if total is None else total + part
    return total


WHOLE = pl.BlockSpec(memory_space=pltpu.VMEM)
FAR = pl.BlockSpec(memory_space=pltpu.HBM)
TOKEN = jax.ShapeDtypeStruct((8, 128), jnp.float32)


def settings(rows, mebibytes=8):
    return dict(
        compiler_params=pltpu.CompilerParams(vmem_limit_bytes=mebibytes * 2**20),
        cost_estimate=pl.CostEstimate(flops=4 * rows * 1024 * 2048 * 4, bytes_accessed=2**20, transcendentals=0),
    )


def first_kernel(state_hbm, gain_hbm, first_hbm, second_hbm, token_ref, gain_ref, first_ref, second_ref, *refs):
    state_ref, sems = refs[-2:]
    small = [
        pltpu.make_async_copy(state_hbm, state_ref, sems.at[2 * LOADS]),
        pltpu.make_async_copy(gain_hbm, gain_ref, sems.at[2 * LOADS + 1]),
    ]
    for copy in small:
        copy.start()
    width = first_hbm.shape[1] // LOADS
    copies = []
    for k in range(LOADS):
        columns = pl.ds(k * width, width)
        copies.append(pltpu.make_async_copy(first_hbm.at[:, columns], first_ref.at[:, columns], sems.at[2 * k]))
        copies.append(pltpu.make_async_copy(second_hbm.at[columns, :], second_ref.at[columns, :], sems.at[2 * k + 1]))
    for copy in copies:
        copy.start()
    token_ref[...] = jnp.zeros(token_ref.shape, jnp.float32)
    for copy in small:
        copy.wait()
    state = state_ref[...]
    normed = normalised(state, gain_ref)
    update = None
    for k in range(LOADS):
        copies[2 * k].wait()
        copies[2 * k + 1].wait()
        part = chunk_of(normed, first_ref, second_ref, k * width, width)
        update = part if update is None else update + part
    rows = state.shape[0] // PORTIONS
    for portion in range(PORTIONS):
        mine = slice(portion * rows, (portion + 1) * rows)
        for k, spacing in enumerate((1.0, 4.0, 16.0)):
            refs[3 * portion + k][...] = state[mine] + spacing * update[mine]


def first_round(initial, gain, first, second):
    rows = initial.shape[0] // PORTIONS
    block = jax.ShapeDtypeStruct((rows, initial.shape[1]), jnp.float32)
    made = pl.pallas_call(
        first_kernel,
        out_shape=(
            TOKEN,
            jax.ShapeDtypeStruct(gain.shape, gain.dtype),
            jax.ShapeDtypeStruct(first.shape, first.dtype),
            jax.ShapeDtypeStruct(second.shape, second.dtype),
        )
        + (block,) * (3 * PORTIONS),
        in_specs=[FAR] * 4,
        out_specs=(WHOLE,) * (4 + 3 * PORTIONS),
        scratch_shapes=[pltpu.VMEM(initial.shape, jnp.float32), pltpu.SemaphoreType.DMA((2 * LOADS + 2,))],
        **settings(initial.shape[0], 43),
    )(initial, gain, first, second)
    states = [
        dict(zip(("current", "four", "sixteen"), made[4 + 3 * k : 7 + 3 * k])) for k in range(PORTIONS)
    ]
    return made[0], made[1:4], states


def targets(jobs):
    return [n for points in jobs.values() for n in points]


def round_kernel(jobs, more, names_in, names_out, *refs):
    given = dict(zip(names_in, refs))
    made = dict(zip(names_out, refs[len(names_in) :]))
    picked_ref, update_ref = refs[-2:]
    rows = given["arrived"].shape[0]
    place = lax.axis_index("layer").astype(jnp.int32)
    made["token"][...] = given["token"][...]
    doubled = sorted(set(targets(jobs)) & set(targets(more)))
    layer = (given["gain"], given["first"], given["second"])

    if more:

        @pl.when(member(targets(jobs)))
        def pick():
            picked_ref[:rows, :] = given["arrived"][...]

        @pl.when(member(sorted(set(targets(more)) - set(doubled))))
        def pick_other():
            picked_ref[:rows, :] = given["other"][...]

    busy = sorted((set(targets(jobs)) | set(targets(more))) - set(doubled))

    @pl.when(member(busy))
    def compute():
        state = picked_ref[:rows, :] if more else given["arrived"][...]
        update_ref[:rows, :] = branch(state, *layer)

    if doubled:

        @pl.when(member(doubled))
        def compute_both():
            picked_ref[rows:, :] = given["other"][...]
            update_ref[...] = branch(picked_ref[...], *layer)

    both = {job: sorted(jobs.get(job, []) + more.get(job, [])) for job in set(jobs) | set(more)}
    for name, writers in WRITERS.items():
        if name in made and name in given:

            @pl.when(jnp.logical_not(member([n for job in writers for n in both.get(job, ())])))
            def keep(name=name):
                made[name][...] = given[name][...]

    if "sums" in given:
        made["sums"][...] = given["sums"][...]
    elif "sums" in made:
        made["sums"][...] = jnp.zeros(made["sums"].shape, jnp.float32)

    def finish(job, stepped, update):
        if job == FINE:
            made["current"][...] = stepped
        if job == LEVEL:
            made["four"][...] = stepped
            made["current"][...] = stepped + given["coarse"][...]
        if job == GAP_FOUR:
            made["four"][...] = stepped
        if job == GAP_SIXTEEN:
            made["sixteen"][...] = stepped
        if job == COARSEST:
            made["current"][...] = given["current"][...] + (stepped - given["sixteen"][...])
            made["sixteen"][...] = stepped
        if job == RESTRICT:
            gap = stepped - given["current"][...]
            made["current"][...] = stepped
            made["coarse"][...] = stepped - given["four"][...]
            shape = made["sums"].shape
            row = lax.broadcasted_iota(jnp.int32, shape, 0)
            here = lax.broadcasted_iota(jnp.int32, shape, 1) == (place + 1) // 4 - 2
            pair = jnp.where(row == 0, jnp.sum(gap * gap), jnp.sum(update * update))
            made["sums"][...] += jnp.where(here & (row < 2), pair, 0.0)

    for hop, name, start in ((jobs, "arrived", 0), (more, "other", rows)):
        for job, points in hop.items():
            for twice in (False, True):
                mine = [n for n in points if (n in doubled) == twice]
                if mine:

                    @pl.when(member(mine))
                    def done(job=job, name=name, start=start if twice else 0):
                        update = update_ref[start : start + rows, :]
                        finish(job, given[name][...] + SPACING[job] * update, update)


WRITERS = {
    "current": {FINE, LEVEL, RESTRICT, COARSEST},
    "four": {LEVEL, GAP_FOUR},
    "sixteen": {GAP_SIXTEEN, COARSEST},
    "coarse": {RESTRICT},
}
READERS = {
    "current": {FINE, LEVEL, RESTRICT, COARSEST},
    "four": {RESTRICT, LEVEL, GAP_FOUR},
    "sixteen": {GAP_SIXTEEN, COARSEST},
    "coarse": {LEVEL},
}


def by_job(pairs):
    jobs = {}
    for unused, target, job in pairs:
        jobs.setdefault(job, []).append(target)
    return jobs


def run_round(arrivals, state, layer, hops, token, sums):
    jobs, more = by_job(hops[0]), by_job(hops[1] if len(hops) > 1 else [])
    kinds = set(jobs) | set(more)
    names_in = ["arrived", "other"][: len(arrivals)] + ["gain", "first", "second", "token"]
    values = [*arrivals, *layer, token]
    names_out, shapes = ["token"], [TOKEN]
    rows, width = arrivals[0].shape
    block = jax.ShapeDtypeStruct((rows, width), jnp.float32)
    for name, writers in WRITERS.items():
        if name in state and kinds & READERS[name]:
            names_in.append(name)
            values.append(state[name])
        if kinds & writers:
            names_out.append(name)
            shapes.append(block)
    if RESTRICT in kinds:
        if sums is not None:
            names_in.append("sums")
            values.append(sums)
        names_out.append("sums")
        shapes.append(TOKEN)
    scratch = pltpu.VMEM((rows * len(arrivals), width), jnp.float32)
    made = pl.pallas_call(
        functools.partial(round_kernel, jobs, more, names_in, names_out),
        out_shape=tuple(shapes),
        in_specs=[WHOLE] * len(names_in),
        out_specs=(WHOLE,) * len(shapes),
        scratch_shapes=[scratch, scratch],
        **settings(rows),
    )(*values)
    return dict(zip(names_out, made))


def take_kernel(receivers, sums_ref, token_ref, *refs):
    *partner_refs, made_ref, passed_ref = refs
    taken(sums_ref, partner_refs, receivers, made_ref)
    passed_ref[...] = token_ref[...]


def take(sums, partners, token, receivers):
    return pl.pallas_call(
        functools.partial(take_kernel, receivers),
        out_shape=(TOKEN, TOKEN),
        in_specs=[WHOLE] * (2 + len(partners)),
        out_specs=(WHOLE, WHOLE),
        compiler_params=pltpu.CompilerParams(vmem_limit_bytes=8 * 2**20),
    )(sums, token, *partners)


def finish_kernel(receivers, sums_ref, partner_ref, token_ref, *refs):
    given = refs[: 3 * PORTIONS]
    outs = refs[3 * PORTIONS : 3 * PORTIONS + 3]
    ratios_ref, *scratch, total_ref, sems = refs[3 * PORTIONS + 3 :]
    point = lax.axis_index("layer") + 1
    rows = given[0].shape[0]
    copies = []

    def send(source, target, portion):
        block = target.at[0, pl.ds(portion * rows, rows), :]
        copies.append(pltpu.make_async_copy(source, block, sems.at[len(copies)]))
        copies[-1].start()

    for portion in range(PORTIONS):
        send(given[3 * portion], outs[0], portion)
    for portion in range(PORTIONS):
        current, *coarser = given[3 * portion : 3 * portion + 3]
        mine = pl.ds(portion * rows, rows)
        for ref, made, least, out in zip(coarser, scratch, (4, 16), outs[1:]):
            made[mine, :] = jnp.where(point >= least, current[...] - ref[...], 0.0)
            send(made.at[mine, :], out, portion)
    taken(sums_ref, (partner_ref,), receivers, total_ref)
    sums = total_ref[...]
    ratios_ref[...] = jnp.sqrt(sums[0:1] / (sums[1:2] + epsilon))
    for copy in copies:
        copy.wait()


def finish(states, sums, partner, receivers, token):
    rows, width = states[0]["current"].shape
    whole = jax.ShapeDtypeStruct((1, rows * PORTIONS, width), jnp.float32)
    values = [state[name] for state in states for name in ("current", "four", "sixteen")]
    layer_states, defects_four, defects_sixteen, ratios = pl.pallas_call(
        functools.partial(finish_kernel, receivers),
        out_shape=(whole, whole, whole, jax.ShapeDtypeStruct((1, 128), jnp.float32)),
        in_specs=[WHOLE] * (3 + len(values)),
        out_specs=(FAR, FAR, FAR, WHOLE),
        scratch_shapes=[pltpu.VMEM((rows * PORTIONS, width), jnp.float32)] * 2
        + [pltpu.VMEM(TOKEN.shape, jnp.float32), pltpu.SemaphoreType.DMA((3 * PORTIONS,))],
        compiler_params=pltpu.CompilerParams(vmem_limit_bytes=8 * 2**20),
    )(sums, partner, token, *values)
    return layer_states, ratios[0, :7], defects_four, defects_sixteen


def local(initial, norm_gains, first_weights, second_weights):
    layers = lax.axis_size("layer")
    hops, routes, restricted = plan(layers)
    token, layer, states = first_round(initial, norm_gains, first_weights[0], second_weights[0])
    steps = gathering(layers, lax.axis_size("dp"))
    sums = None
    last = max(hops)[0] + 1
    for index in range(last):
        while index > restricted and steps[0][0] == index:
            unused, ways, receivers = steps.pop(0)
            sums, token = take(sums, [lax.ppermute(sums, axes, pairs) for axes, pairs in ways], token, receivers)
        keys = sorted(key for key in hops if key[0] == index)
        for portion in range(PORTIONS):
            current = states[portion]["current"]
            arrivals = [lax.ppermute(current, "layer", [(a - 1, b - 1) for a, b in routes[key]]) for key in keys]
            made = run_round(arrivals, states[portion], layer, [hops[key] for key in keys], token, sums)
            token = made.pop("token")
            sums = made.pop("sums", sums)
            states[portion].update(made)
    ((follows, ((axes, pairs),), receivers),) = steps
    assert follows == last
    return finish(states, sums, lax.ppermute(sums, axes, pairs), receivers, token)


def solution(mesh):
    placed = (P("dp", None), P("layer", None), P("layer", None, None), P("layer", None, None))
    return jax.shard_map(
        local,
        mesh=mesh,
        in_specs=placed,
        out_specs=(P("layer", "dp", None), P(), P("layer", "dp", None), P("layer", "dp", None)),
        check_vma=False,
    )
```

```python
import functools

import jax
import jax.numpy as jnp
from jax import lax
from jax.experimental import pallas as pl
from jax.experimental.pallas import tpu as pltpu
from jax.sharding import PartitionSpec as P

epsilon = 1e-06
PORTIONS = 2
CHUNK = 1024
LOADS = 4

ADD = "add"
FINE, LEVEL, GAP_FOUR, GAP_SIXTEEN, RESTRICT, COARSEST = 1, 2, 3, 4, 5, 6
SPACING = {FINE: 1.0, LEVEL: 4.0, GAP_FOUR: 4.0, GAP_SIXTEEN: 16.0, RESTRICT: 1.0, COARSEST: 16.0}


def plan(layers):
    def every(residue, shift, job):
        return [(n, n + shift, job) for n in range(1, layers - shift + 1) if n % 4 == residue]

    hops = {
        (0, 0): every(1, 1, FINE),
        (1, 0): every(2, 1, FINE),
        (2, 0): every(3, 1, FINE),
        (3, 0): every(0, 1, FINE) + [(3, 19, GAP_SIXTEEN)],
        (4, 0): every(1, 1, FINE),
        (4, 1): every(0, 4, GAP_FOUR) + [(1, 17, GAP_SIXTEEN), (2, 18, GAP_SIXTEEN)],
        (6, 0): every(2, 1, FINE) + [(16, 32, GAP_SIXTEEN), (4, 20, GAP_SIXTEEN), (1, 5, GAP_FOUR)],
        (7, 0): every(3, 1, RESTRICT) + [(2, 6, GAP_FOUR)],
        (8, 0): [(8, 12, LEVEL), (20, 24, LEVEL), (3, 7, GAP_FOUR)],
        (9, 0): [(12, 16, LEVEL), (24, 28, LEVEL)],
        (10, 0): [(16, 20, LEVEL), (28, 32, LEVEL)],
        (11, 0): [(20, 24, LEVEL), (16, 32, COARSEST)],
        (12, 0): [(24, 28, LEVEL)],
        (12, 1): [(24, 25, FINE)],
        (13, 0): [(28, 29, FINE), (25, 26, FINE)],
        (14, 0): [(29, 30, FINE), (26, 27, FINE), (28, 32, GAP_FOUR)],
        (15, 0): [(30, 31, FINE)],
        (15, 1): [(27, 31, GAP_FOUR)],
    }
    restricted = 7
    like = {(0, 0): (4, 0), (1, 0): (6, 0), (2, 0): (7, 0), (8, 0): (14, 0), (9, 0): (15, 1)}
    closed = {(n, 0) for n in (0, 1, 2, 3, 4, 15)}

    final = {1: -1, 2: 0, 3: 1, 4: 2, 5: 3, 6: 4, 7: 6, 8: 7}
    final.update({12: 8, 16: 9, 20: 10, 24: 11, 28: 12, 32: 11, 25: 12, 26: 13, 27: 14, 29: 13, 30: 14, 31: 15})

    def place(source, target, job, first):
        for key in sorted(hops):
            group = [key] + [k for k in hops if like.get(k) == key or like.get(key) == k]
            if key[0] < first or key in closed or (key == (4, 1) and {source, target} & {5, 6, 7}):
                continue
            if any(a == source or b == target for k in group for a, b, unused in hops[k]):
                continue
            if any(b == target for k in hops if k[0] == key[0] for unused, b, held in hops[k]):
                continue
            hops[key].append((source, target, job))
            return key[0]
        raise ValueError((source, target, job))

    for anchor in (8, 12, 16, 20):
        for n in (anchor + 1, anchor + 2, anchor + 3):
            final[n] = place(n - 1, n, FINE, max(final[n - 1], restricted) + 1)
    wanted = []
    for n in range(5, layers + 1):
        if n % 4 != 0 and n != 31:
            wanted.append((final[n - 4], n - 4, n, GAP_FOUR))
    for n in range(17, layers):
        if n not in (19, 20):
            wanted.append((final[n - 16], n - 16, n, GAP_SIXTEEN))
    fixed = {(a, b) for pairs in hops.values() for a, b, unused in pairs}
    wanted = [want for want in wanted if want[1:3] not in fixed]
    for ready, source, target, job in sorted(wanted, key=lambda want: (-want[0], want)):
        place(source, target, job, max(13 if target in (24, 28) else 4, ready + 1))

    routes = {key: [(a, b) for a, b, unused in pairs] for key, pairs in hops.items()}
    for key, other in like.items():
        routes[other] = routes[other] + [pair for pair in routes[key] if pair not in routes[other]]
    assert not any(a <= 4 and b > 8 for key, pairs in hops.items() if key[0] > 7 for a, b, unused in pairs)
    for key, other in like.items():
        routes[key] = routes[other]
    return hops, routes, restricted


def gathering(layers, planes):
    def within(pairs):
        return "layer", [(a - 1, b - 1) for a, b in pairs]

    start = [within([(8, 3), (16, 2), (12, 1), (20, 4)]), within([(24, 1), (32, 2), (28, 3)])]
    steps = [(8, start, ADD)]
    for follows, distance in ((9, 1), (9, 2)):
        steps.append((follows, [within([(n + 1, (n ^ distance) + 1) for n in range(4)])], ADD))
    for follows, distance in ((10, 1), (10, 2), (11, 4)):
        pairs = [(n * planes + i, n * planes + (i ^ distance)) for n in range(4) for i in range(planes)]
        steps.append((follows, [(("layer", "dp"), pairs)], ADD))
    for follows, known in ((12, 4), (14, 8), (16, 16)):
        steps.append((follows, [within([(n, n + known) for n in range(1, known + 1)])], tuple(range(known + 1, 2 * known + 1))))
    assert 2 * known == layers
    return steps


def member(points):
    place = lax.axis_index("layer").astype(jnp.int32)
    mask = 0
    for n in points:
        mask |= 1 << (n - 1)
    if mask >= 2**31:
        mask -= 2**32
    return (lax.shift_right_logical(jnp.int32(mask), place) & 1) == 1


def taken(held_ref, arrived_refs, receivers, target_ref):
    if receivers == ADD:
        total = held_ref[...]
        for ref in arrived_refs:
            total = total + ref[...]
        target_ref[...] = total
    else:
        here = member(receivers)

        @pl.when(here)
        def replace():
            target_ref[...] = arrived_refs[0][...]

        @pl.when(jnp.logical_not(here))
        def keep():
            target_ref[...] = held_ref[...]


def normalised(state, gain_ref):
    mean_square = jnp.mean(state * state, axis=-1, keepdims=True)
    return (state * lax.rsqrt(mean_square + epsilon) * gain_ref[...]).astype(jnp.bfloat16)


def chunk_of(normed, first_ref, second_ref, start, width):
    hidden = jax.nn.gelu(
        jnp.dot(normed, first_ref[:, start : start + width], preferred_element_type=jnp.float32),
        approximate=True,
    ).astype(jnp.bfloat16)
    return jnp.dot(hidden, second_ref[start : start + width, :], preferred_element_type=jnp.float32)


def branch(state, gain_ref, first_ref, second_ref):
    normed = normalised(state, gain_ref)
    total = None
    for start in range(0, first_ref.shape[1], CHUNK):
        part = chunk_of(normed, first_ref, second_ref, start, CHUNK)
        total = part if total is None else total + part
    return total


WHOLE = pl.BlockSpec(memory_space=pltpu.VMEM)
FAR = pl.BlockSpec(memory_space=pltpu.HBM)
TOKEN = jax.ShapeDtypeStruct((8, 128), jnp.float32)


def settings(rows, mebibytes=8):
    return dict(
        compiler_params=pltpu.CompilerParams(vmem_limit_bytes=mebibytes * 2**20),
        cost_estimate=pl.CostEstimate(flops=4 * rows * 1024 * 2048 * 4, bytes_accessed=2**20, transcendentals=0),
    )


def first_kernel(state_hbm, gain_hbm, first_hbm, second_hbm, token_ref, gain_ref, first_ref, second_ref, *refs):
    state_ref, sems = refs[-2:]
    small = [
        pltpu.make_async_copy(state_hbm, state_ref, sems.at[2 * LOADS]),
        pltpu.make_async_copy(gain_hbm, gain_ref, sems.at[2 * LOADS + 1]),
    ]
    for copy in small:
        copy.start()
    width = first_hbm.shape[1] // LOADS
    copies = []
    for k in range(LOADS):
        columns = pl.ds(k * width, width)
        copies.append(pltpu.make_async_copy(first_hbm.at[:, columns], first_ref.at[:, columns], sems.at[2 * k]))
        copies.append(pltpu.make_async_copy(second_hbm.at[columns, :], second_ref.at[columns, :], sems.at[2 * k + 1]))
    for copy in copies:
        copy.start()
    token_ref[...] = jnp.zeros(token_ref.shape, jnp.float32)
    for copy in small:
        copy.wait()
    state = state_ref[...]
    normed = normalised(state, gain_ref)
    update = None
    for k in range(LOADS):
        copies[2 * k].wait()
        copies[2 * k + 1].wait()
        part = chunk_of(normed, first_ref, second_ref, k * width, width)
        update = part if update is None else update + part
    rows = state.shape[0] // PORTIONS
    for portion in range(PORTIONS):
        mine = slice(portion * rows, (portion + 1) * rows)
        for k, spacing in enumerate((1.0, 4.0, 16.0)):
            refs[3 * portion + k][...] = state[mine] + spacing * update[mine]


def first_round(initial, gain, first, second):
    rows = initial.shape[0] // PORTIONS
    block = jax.ShapeDtypeStruct((rows, initial.shape[1]), jnp.float32)
    made = pl.pallas_call(
        first_kernel,
        out_shape=(
            TOKEN,
            jax.ShapeDtypeStruct(gain.shape, gain.dtype),
            jax.ShapeDtypeStruct(first.shape, first.dtype),
            jax.ShapeDtypeStruct(second.shape, second.dtype),
        )
        + (block,) * (3 * PORTIONS),
        in_specs=[FAR] * 4,
        out_specs=(WHOLE,) * (4 + 3 * PORTIONS),
        scratch_shapes=[pltpu.VMEM(initial.shape, jnp.float32), pltpu.SemaphoreType.DMA((2 * LOADS + 2,))],
        **settings(initial.shape[0], 43),
    )(initial, gain, first, second)
    states = [
        dict(zip(("current", "four", "sixteen"), made[4 + 3 * k : 7 + 3 * k])) for k in range(PORTIONS)
    ]
    return made[0], made[1:4], states


def targets(jobs):
    return [n for points in jobs.values() for n in points]


def round_kernel(jobs, more, names_in, names_out, *refs):
    given = dict(zip(names_in, refs))
    made = dict(zip(names_out, refs[len(names_in) :]))
    picked_ref, update_ref = refs[-2:]
    rows = given["arrived"].shape[0]
    place = lax.axis_index("layer").astype(jnp.int32)
    made["token"][...] = given["token"][...]
    doubled = sorted(set(targets(jobs)) & set(targets(more)))
    layer = (given["gain"], given["first"], given["second"])

    if more:

        @pl.when(member(targets(jobs)))
        def pick():
            picked_ref[:rows, :] = given["arrived"][...]

        @pl.when(member(sorted(set(targets(more)) - set(doubled))))
        def pick_other():
            picked_ref[:rows, :] = given["other"][...]

    busy = sorted((set(targets(jobs)) | set(targets(more))) - set(doubled))

    @pl.when(member(busy))
    def compute():
        state = picked_ref[:rows, :] if more else given["arrived"][...]
        update_ref[:rows, :] = branch(state, *layer)

    if doubled:

        @pl.when(member(doubled))
        def compute_both():
            picked_ref[rows:, :] = given["other"][...]
            update_ref[...] = branch(picked_ref[...], *layer)

    both = {job: sorted(jobs.get(job, []) + more.get(job, [])) for job in set(jobs) | set(more)}
    for name, writers in WRITERS.items():
        if name in made and name in given:

            @pl.when(jnp.logical_not(member([n for job in writers for n in both.get(job, ())])))
            def keep(name=name):
                made[name][...] = given[name][...]

    if "sums" in given:
        made["sums"][...] = given["sums"][...]
    elif "sums" in made:
        made["sums"][...] = jnp.zeros(made["sums"].shape, jnp.float32)

    def finish(job, stepped, update):
        if job == FINE:
            made["current"][...] = stepped
        if job == LEVEL:
            made["four"][...] = stepped
            made["current"][...] = stepped + given["coarse"][...]
        if job == GAP_FOUR:
            made["four"][...] = stepped
        if job == GAP_SIXTEEN:
            made["sixteen"][...] = stepped
        if job == COARSEST:
            made["current"][...] = given["current"][...] + (stepped - given["sixteen"][...])
            made["sixteen"][...] = stepped
        if job == RESTRICT:
            gap = stepped - given["current"][...]
            made["current"][...] = stepped
            made["coarse"][...] = stepped - given["four"][...]
            shape = made["sums"].shape
            row = lax.broadcasted_iota(jnp.int32, shape, 0)
            here = lax.broadcasted_iota(jnp.int32, shape, 1) == (place + 1) // 4 - 2
            pair = jnp.where(row == 0, jnp.sum(gap * gap), jnp.sum(update * update))
            made["sums"][...] += jnp.where(here & (row < 2), pair, 0.0)

    for hop, name, start in ((jobs, "arrived", 0), (more, "other", rows)):
        for job, points in hop.items():
            for twice in (False, True):
                mine = [n for n in points if (n in doubled) == twice]
                if mine:

                    @pl.when(member(mine))
                    def done(job=job, name=name, start=start if twice else 0):
                        update = update_ref[start : start + rows, :]
                        finish(job, given[name][...] + SPACING[job] * update, update)


WRITERS = {
    "current": {FINE, LEVEL, RESTRICT, COARSEST},
    "four": {LEVEL, GAP_FOUR},
    "sixteen": {GAP_SIXTEEN, COARSEST},
    "coarse": {RESTRICT},
}
READERS = {
    "current": {FINE, LEVEL, RESTRICT, COARSEST},
    "four": {RESTRICT, LEVEL, GAP_FOUR},
    "sixteen": {GAP_SIXTEEN, COARSEST},
    "coarse": {LEVEL},
}


def by_job(pairs):
    jobs = {}
    for unused, target, job in pairs:
        jobs.setdefault(job, []).append(target)
    return jobs


def run_round(arrivals, state, layer, hops, token, sums):
    jobs, more = by_job(hops[0]), by_job(hops[1] if len(hops) > 1 else [])
    kinds = set(jobs) | set(more)
    names_in = ["arrived", "other"][: len(arrivals)] + ["gain", "first", "second", "token"]
    values = [*arrivals, *layer, token]
    names_out, shapes = ["token"], [TOKEN]
    rows, width = arrivals[0].shape
    block = jax.ShapeDtypeStruct((rows, width), jnp.float32)
    for name, writers in WRITERS.items():
        if name in state and kinds & READERS[name]:
            names_in.append(name)
            values.append(state[name])
        if kinds & writers:
            names_out.append(name)
            shapes.append(block)
    if RESTRICT in kinds:
        if sums is not None:
            names_in.append("sums")
            values.append(sums)
        names_out.append("sums")
        shapes.append(TOKEN)
    scratch = pltpu.VMEM((rows * len(arrivals), width), jnp.float32)
    made = pl.pallas_call(
        functools.partial(round_kernel, jobs, more, names_in, names_out),
        out_shape=tuple(shapes),
        in_specs=[WHOLE] * len(names_in),
        out_specs=(WHOLE,) * len(shapes),
        scratch_shapes=[scratch, scratch],
        **settings(rows),
    )(*values)
    return dict(zip(names_out, made))


def take_kernel(receivers, sums_ref, token_ref, *refs):
    *partner_refs, made_ref, passed_ref = refs
    taken(sums_ref, partner_refs, receivers, made_ref)
    passed_ref[...] = token_ref[...]


def take(sums, partners, token, receivers):
    return pl.pallas_call(
        functools.partial(take_kernel, receivers),
        out_shape=(TOKEN, TOKEN),
        in_specs=[WHOLE] * (2 + len(partners)),
        out_specs=(WHOLE, WHOLE),
        compiler_params=pltpu.CompilerParams(vmem_limit_bytes=8 * 2**20),
    )(sums, token, *partners)


def finish_kernel(receivers, sums_ref, partner_ref, token_ref, *refs):
    given = refs[: 3 * PORTIONS]
    outs = refs[3 * PORTIONS : 3 * PORTIONS + 3]
    ratios_ref, *scratch, total_ref, sems = refs[3 * PORTIONS + 3 :]
    point = lax.axis_index("layer") + 1
    rows = given[0].shape[0]
    copies = []

    def send(source, target, portion):
        block = target.at[0, pl.ds(portion * rows, rows), :]
        copies.append(pltpu.make_async_copy(source, block, sems.at[len(copies)]))
        copies[-1].start()

    for portion in range(PORTIONS):
        send(given[3 * portion], outs[0], portion)
    for portion in range(PORTIONS):
        current, *coarser = given[3 * portion : 3 * portion + 3]
        mine = pl.ds(portion * rows, rows)
        for ref, made, least, out in zip(coarser, scratch, (4, 16), outs[1:]):
            made[mine, :] = jnp.where(point >= least, current[...] - ref[...], 0.0)
            send(made.at[mine, :], out, portion)
    taken(sums_ref, (partner_ref,), receivers, total_ref)
    sums = total_ref[...]
    ratios_ref[...] = jnp.sqrt(sums[0:1] / (sums[1:2] + epsilon))
    for copy in copies:
        copy.wait()


def finish(states, sums, partner, receivers, token):
    rows, width = states[0]["current"].shape
    whole = jax.ShapeDtypeStruct((1, rows * PORTIONS, width), jnp.float32)
    values = [state[name] for state in states for name in ("current", "four", "sixteen")]
    layer_states, defects_four, defects_sixteen, ratios = pl.pallas_call(
        functools.partial(finish_kernel, receivers),
        out_shape=(whole, whole, whole, jax.ShapeDtypeStruct((1, 128), jnp.float32)),
        in_specs=[WHOLE] * (3 + len(values)),
        out_specs=(FAR, FAR, FAR, WHOLE),
        scratch_shapes=[pltpu.VMEM((rows * PORTIONS, width), jnp.float32)] * 2
        + [pltpu.VMEM(TOKEN.shape, jnp.float32), pltpu.SemaphoreType.DMA((3 * PORTIONS,))],
        compiler_params=pltpu.CompilerParams(vmem_limit_bytes=8 * 2**20),
    )(sums, partner, token, *values)
    return layer_states, ratios[0, :7], defects_four, defects_sixteen


def local(initial, norm_gains, first_weights, second_weights):
    layers = lax.axis_size("layer")
    hops, routes, restricted = plan(layers)
    token, layer, states = first_round(initial, norm_gains, first_weights[0], second_weights[0])
    steps = gathering(layers, lax.axis_size("dp"))
    sums = None
    last = max(hops)[0] + 1
    for index in range(last):
        while index > restricted and steps[0][0] == index:
            unused, ways, receivers = steps.pop(0)
            sums, token = take(sums, [lax.ppermute(sums, axes, pairs) for axes, pairs in ways], token, receivers)
        keys = sorted(key for key in hops if key[0] == index)
        if not keys:
            continue
        for portion in range(PORTIONS):
            current = states[portion]["current"]
            arrivals = [lax.ppermute(current, "layer", [(a - 1, b - 1) for a, b in routes[key]]) for key in keys]
            made = run_round(arrivals, states[portion], layer, [hops[key] for key in keys], token, sums)
            token = made.pop("token")
            sums = made.pop("sums", sums)
            states[portion].update(made)
    ((follows, ((axes, pairs),), receivers),) = steps
    assert follows == last
    return finish(states, sums, lax.ppermute(sums, axes, pairs), receivers, token)


def solution(mesh):
    placed = (P("dp", None), P("layer", None), P("layer", None, None), P("layer", None, None))
    return jax.shard_map(
        local,
        mesh=mesh,
        in_specs=placed,
        out_specs=(P("layer", "dp", None), P(), P("layer", "dp", None), P("layer", "dp", None)),
        check_vma=False,
    )
```

```python
import functools

import jax
import jax.numpy as jnp
from jax import lax
from jax.experimental import pallas as pl
from jax.experimental.pallas import tpu as pltpu
from jax.sharding import PartitionSpec as P

epsilon = 1e-06
PORTIONS = 2
CHUNK = 1024
LOADS = 4

ADD = "add"
FINE, LEVEL, GAP_FOUR, GAP_SIXTEEN, RESTRICT, COARSEST = 1, 2, 3, 4, 5, 6
SPACING = {FINE: 1.0, LEVEL: 4.0, GAP_FOUR: 4.0, GAP_SIXTEEN: 16.0, RESTRICT: 1.0, COARSEST: 16.0}


def plan(layers):
    def every(residue, shift, job):
        return [(n, n + shift, job) for n in range(1, layers - shift + 1) if n % 4 == residue]

    hops = {
        (0, 0): every(1, 1, FINE),
        (1, 0): every(2, 1, FINE),
        (2, 0): every(3, 1, FINE),
        (3, 0): every(0, 1, FINE) + [(3, 19, GAP_SIXTEEN)],
        (4, 0): every(1, 1, FINE),
        (6, 0): every(2, 1, FINE) + [(16, 32, GAP_SIXTEEN), (4, 20, GAP_SIXTEEN), (1, 5, GAP_FOUR)],
        (6, 1): every(0, 4, GAP_FOUR) + [(1, 17, GAP_SIXTEEN), (2, 18, GAP_SIXTEEN)],
        (7, 0): every(3, 1, RESTRICT) + [(2, 6, GAP_FOUR)],
        (8, 0): [(8, 12, LEVEL), (20, 24, LEVEL), (3, 7, GAP_FOUR)],
        (9, 0): [(12, 16, LEVEL), (24, 28, LEVEL)],
        (10, 0): [(16, 20, LEVEL), (28, 32, LEVEL)],
        (11, 0): [(20, 24, LEVEL)],
        (12, 0): [(24, 28, LEVEL)],
        (12, 1): [(24, 25, FINE)],
        (13, 0): [(28, 29, FINE), (25, 26, FINE), (16, 32, COARSEST)],
        (14, 0): [(29, 30, FINE), (26, 27, FINE)],
        (15, 0): [(30, 31, FINE), (28, 32, GAP_FOUR)],
        (15, 1): [(27, 31, GAP_FOUR)],
    }
    restricted = 7
    like = {(0, 0): (4, 0), (1, 0): (6, 0), (2, 0): (7, 0), (8, 0): (14, 0), (9, 0): (15, 1)}
    closed = {(n, 0) for n in (0, 1, 2, 3, 4, 15)}

    final = {1: -1, 2: 0, 3: 1, 4: 2, 5: 3, 6: 4, 7: 6, 8: 7}
    final.update({12: 8, 16: 9, 20: 10, 24: 11, 28: 12, 32: 13, 25: 12, 26: 13, 27: 14, 29: 13, 30: 14, 31: 15})

    def place(source, target, job, first):
        for key in sorted(hops):
            group = [key] + [k for k in hops if like.get(k) == key or like.get(key) == k]
            if key[0] < first or key in closed or (key == (7, 0) and source == 5):
                continue
            if any(a == source or b == target for k in group for a, b, unused in hops[k]):
                continue
            if any(b == target for k in hops if k[0] == key[0] for unused, b, held in hops[k]):
                continue
            hops[key].append((source, target, job))
            return key[0]
        raise ValueError((source, target, job))

    for anchor in (8, 12, 16, 20):
        for n in (anchor + 1, anchor + 2, anchor + 3):
            final[n] = place(n - 1, n, FINE, max(final[n - 1], restricted) + 1)
    wanted = []
    for n in range(5, layers + 1):
        if n % 4 != 0 and n != 31:
            wanted.append((final[n - 4], n - 4, n, GAP_FOUR))
    for n in range(17, layers):
        if n not in (19, 20):
            wanted.append((final[n - 16], n - 16, n, GAP_SIXTEEN))
    fixed = {(a, b) for pairs in hops.values() for a, b, unused in pairs}
    wanted = [want for want in wanted if want[1:3] not in fixed]
    for ready, source, target, job in sorted(wanted, key=lambda want: (-want[0], want)):
        place(source, target, job, max(13 if target in (24, 28) else 4, ready + 1))

    routes = {key: [(a, b) for a, b, unused in pairs] for key, pairs in hops.items()}
    for key, other in like.items():
        routes[other] = routes[other] + [pair for pair in routes[key] if pair not in routes[other]]
    assert not any(a <= 4 and b > 8 for key, pairs in hops.items() if key[0] > 7 for a, b, unused in pairs)
    for key, other in like.items():
        routes[key] = routes[other]
    return hops, routes, restricted


def gathering(layers, planes):
    def within(pairs):
        return "layer", [(a - 1, b - 1) for a, b in pairs]

    start = [within([(8, 3), (16, 2), (12, 1), (20, 4)]), within([(24, 1), (32, 2), (28, 3)])]
    steps = [((8, 0), start, ADD)]
    for follows, distance in (((8, 1), 1), ((9, 0), 2)):
        steps.append((follows, [within([(n + 1, (n ^ distance) + 1) for n in range(4)])], ADD))
    for follows, distance in (((9, 1), 1), ((10, 0), 2), ((10, 1), 4)):
        pairs = [(n * planes + i, n * planes + (i ^ distance)) for n in range(4) for i in range(planes)]
        steps.append((follows, [(("layer", "dp"), pairs)], ADD))
    for follows, known in (((11, 1), 4), ((14, 0), 8), (None, 16)):
        steps.append((follows, [within([(n, n + known) for n in range(1, known + 1)])], tuple(range(known + 1, 2 * known + 1))))
    assert 2 * known == layers
    return steps


def member(points):
    place = lax.axis_index("layer").astype(jnp.int32)
    mask = 0
    for n in points:
        mask |= 1 << (n - 1)
    if mask >= 2**31:
        mask -= 2**32
    return (lax.shift_right_logical(jnp.int32(mask), place) & 1) == 1


def taken(held_ref, arrived_refs, receivers, target_ref):
    if receivers == ADD:
        total = held_ref[...]
        for ref in arrived_refs:
            total = total + ref[...]
        target_ref[...] = total
    else:
        here = member(receivers)

        @pl.when(here)
        def replace():
            target_ref[...] = arrived_refs[0][...]

        @pl.when(jnp.logical_not(here))
        def keep():
            target_ref[...] = held_ref[...]


def normalised(state, gain_ref):
    mean_square = jnp.mean(state * state, axis=-1, keepdims=True)
    return (state * lax.rsqrt(mean_square + epsilon) * gain_ref[...]).astype(jnp.bfloat16)


def chunk_of(normed, first_ref, second_ref, start, width):
    hidden = jax.nn.gelu(
        jnp.dot(normed, first_ref[:, start : start + width], preferred_element_type=jnp.float32),
        approximate=True,
    ).astype(jnp.bfloat16)
    return jnp.dot(hidden, second_ref[start : start + width, :], preferred_element_type=jnp.float32)


def branch(state, gain_ref, first_ref, second_ref):
    normed = normalised(state, gain_ref)
    total = None
    for start in range(0, first_ref.shape[1], CHUNK):
        part = chunk_of(normed, first_ref, second_ref, start, CHUNK)
        total = part if total is None else total + part
    return total


WHOLE = pl.BlockSpec(memory_space=pltpu.VMEM)
FAR = pl.BlockSpec(memory_space=pltpu.HBM)
TOKEN = jax.ShapeDtypeStruct((8, 128), jnp.float32)


def settings(rows, mebibytes=8):
    return dict(
        compiler_params=pltpu.CompilerParams(vmem_limit_bytes=mebibytes * 2**20),
        cost_estimate=pl.CostEstimate(flops=4 * rows * 1024 * 2048 * 4, bytes_accessed=2**20, transcendentals=0),
    )


def first_kernel(state_hbm, gain_hbm, first_hbm, second_hbm, token_ref, gain_ref, first_ref, second_ref, *refs):
    state_ref, sems = refs[-2:]
    small = [
        pltpu.make_async_copy(state_hbm, state_ref, sems.at[2 * LOADS]),
        pltpu.make_async_copy(gain_hbm, gain_ref, sems.at[2 * LOADS + 1]),
    ]
    for copy in small:
        copy.start()
    width = first_hbm.shape[1] // LOADS
    copies = []
    for k in range(LOADS):
        columns = pl.ds(k * width, width)
        copies.append(pltpu.make_async_copy(first_hbm.at[:, columns], first_ref.at[:, columns], sems.at[2 * k]))
        copies.append(pltpu.make_async_copy(second_hbm.at[columns, :], second_ref.at[columns, :], sems.at[2 * k + 1]))
    for copy in copies:
        copy.start()
    token_ref[...] = jnp.zeros(token_ref.shape, jnp.float32)
    for copy in small:
        copy.wait()
    state = state_ref[...]
    normed = normalised(state, gain_ref)
    update = None
    for k in range(LOADS):
        copies[2 * k].wait()
        copies[2 * k + 1].wait()
        part = chunk_of(normed, first_ref, second_ref, k * width, width)
        update = part if update is None else update + part
    rows = state.shape[0] // PORTIONS
    for portion in range(PORTIONS):
        mine = slice(portion * rows, (portion + 1) * rows)
        for k, spacing in enumerate((1.0, 4.0, 16.0)):
            refs[3 * portion + k][...] = state[mine] + spacing * update[mine]


def first_round(initial, gain, first, second):
    rows = initial.shape[0] // PORTIONS
    block = jax.ShapeDtypeStruct((rows, initial.shape[1]), jnp.float32)
    made = pl.pallas_call(
        first_kernel,
        out_shape=(
            TOKEN,
            jax.ShapeDtypeStruct(gain.shape, gain.dtype),
            jax.ShapeDtypeStruct(first.shape, first.dtype),
            jax.ShapeDtypeStruct(second.shape, second.dtype),
        )
        + (block,) * (3 * PORTIONS),
        in_specs=[FAR] * 4,
        out_specs=(WHOLE,) * (4 + 3 * PORTIONS),
        scratch_shapes=[pltpu.VMEM(initial.shape, jnp.float32), pltpu.SemaphoreType.DMA((2 * LOADS + 2,))],
        **settings(initial.shape[0], 43),
    )(initial, gain, first, second)
    states = [
        dict(zip(("current", "four", "sixteen"), made[4 + 3 * k : 7 + 3 * k])) for k in range(PORTIONS)
    ]
    return made[0], made[1:4], states


def targets(jobs):
    return [n for points in jobs.values() for n in points]


def round_kernel(jobs, more, names_in, names_out, *refs):
    given = dict(zip(names_in, refs))
    made = dict(zip(names_out, refs[len(names_in) :]))
    picked_ref, update_ref = refs[-2:]
    rows = given["arrived"].shape[0]
    place = lax.axis_index("layer").astype(jnp.int32)
    made["token"][...] = given["token"][...]
    doubled = sorted(set(targets(jobs)) & set(targets(more)))
    layer = (given["gain"], given["first"], given["second"])

    if more:

        @pl.when(member(targets(jobs)))
        def pick():
            picked_ref[:rows, :] = given["arrived"][...]

        @pl.when(member(sorted(set(targets(more)) - set(doubled))))
        def pick_other():
            picked_ref[:rows, :] = given["other"][...]

    busy = sorted((set(targets(jobs)) | set(targets(more))) - set(doubled))

    @pl.when(member(busy))
    def compute():
        state = picked_ref[:rows, :] if more else given["arrived"][...]
        update_ref[:rows, :] = branch(state, *layer)

    if doubled:

        @pl.when(member(doubled))
        def compute_both():
            picked_ref[rows:, :] = given["other"][...]
            update_ref[...] = branch(picked_ref[...], *layer)

    both = {job: sorted(jobs.get(job, []) + more.get(job, [])) for job in set(jobs) | set(more)}
    for name, writers in WRITERS.items():
        if name in made and name in given:

            @pl.when(jnp.logical_not(member([n for job in writers for n in both.get(job, ())])))
            def keep(name=name):
                made[name][...] = given[name][...]

    if "sums" in given:
        made["sums"][...] = given["sums"][...]
    elif "sums" in made:
        made["sums"][...] = jnp.zeros(made["sums"].shape, jnp.float32)

    def finish(job, stepped, update):
        if job == FINE:
            made["current"][...] = stepped
        if job == LEVEL:
            made["four"][...] = stepped
            made["current"][...] = stepped + given["coarse"][...]
        if job == GAP_FOUR:
            made["four"][...] = stepped
        if job == GAP_SIXTEEN:
            made["sixteen"][...] = stepped
        if job == COARSEST:
            made["current"][...] = given["current"][...] + (stepped - given["sixteen"][...])
            made["sixteen"][...] = stepped
        if job == RESTRICT:
            gap = stepped - given["current"][...]
            made["current"][...] = stepped
            made["coarse"][...] = stepped - given["four"][...]
            shape = made["sums"].shape
            row = lax.broadcasted_iota(jnp.int32, shape, 0)
            here = lax.broadcasted_iota(jnp.int32, shape, 1) == (place + 1) // 4 - 2
            pair = jnp.where(row == 0, jnp.sum(gap * gap), jnp.sum(update * update))
            made["sums"][...] += jnp.where(here & (row < 2), pair, 0.0)

    for hop, name, start in ((jobs, "arrived", 0), (more, "other", rows)):
        for job, points in hop.items():
            for twice in (False, True):
                mine = [n for n in points if (n in doubled) == twice]
                if mine:

                    @pl.when(member(mine))
                    def done(job=job, name=name, start=start if twice else 0):
                        update = update_ref[start : start + rows, :]
                        finish(job, given[name][...] + SPACING[job] * update, update)


WRITERS = {
    "current": {FINE, LEVEL, RESTRICT, COARSEST},
    "four": {LEVEL, GAP_FOUR},
    "sixteen": {GAP_SIXTEEN, COARSEST},
    "coarse": {RESTRICT},
}
READERS = {
    "current": {FINE, LEVEL, RESTRICT, COARSEST},
    "four": {RESTRICT, LEVEL, GAP_FOUR},
    "sixteen": {GAP_SIXTEEN, COARSEST},
    "coarse": {LEVEL},
}


def by_job(pairs):
    jobs = {}
    for unused, target, job in pairs:
        jobs.setdefault(job, []).append(target)
    return jobs


def run_round(arrivals, state, layer, hops, token, sums):
    jobs, more = by_job(hops[0]), by_job(hops[1] if len(hops) > 1 else [])
    kinds = set(jobs) | set(more)
    names_in = ["arrived", "other"][: len(arrivals)] + ["gain", "first", "second", "token"]
    values = [*arrivals, *layer, token]
    names_out, shapes = ["token"], [TOKEN]
    rows, width = arrivals[0].shape
    block = jax.ShapeDtypeStruct((rows, width), jnp.float32)
    for name, writers in WRITERS.items():
        if name in state and kinds & READERS[name]:
            names_in.append(name)
            values.append(state[name])
        if kinds & writers:
            names_out.append(name)
            shapes.append(block)
    if RESTRICT in kinds:
        if sums is not None:
            names_in.append("sums")
            values.append(sums)
        names_out.append("sums")
        shapes.append(TOKEN)
    scratch = pltpu.VMEM((rows * len(arrivals), width), jnp.float32)
    made = pl.pallas_call(
        functools.partial(round_kernel, jobs, more, names_in, names_out),
        out_shape=tuple(shapes),
        in_specs=[WHOLE] * len(names_in),
        out_specs=(WHOLE,) * len(shapes),
        scratch_shapes=[scratch, scratch],
        **settings(rows),
    )(*values)
    return dict(zip(names_out, made))


def take_kernel(receivers, sums_ref, token_ref, *refs):
    *partner_refs, made_ref, passed_ref = refs
    taken(sums_ref, partner_refs, receivers, made_ref)
    passed_ref[...] = token_ref[...]


def take(sums, partners, token, receivers):
    return pl.pallas_call(
        functools.partial(take_kernel, receivers),
        out_shape=(TOKEN, TOKEN),
        in_specs=[WHOLE] * (2 + len(partners)),
        out_specs=(WHOLE, WHOLE),
        compiler_params=pltpu.CompilerParams(vmem_limit_bytes=8 * 2**20),
    )(sums, token, *partners)


def finish_kernel(receivers, sums_ref, partner_ref, token_ref, *refs):
    given = refs[: 3 * PORTIONS]
    outs = refs[3 * PORTIONS : 3 * PORTIONS + 3]
    ratios_ref, *scratch, total_ref, sems = refs[3 * PORTIONS + 3 :]
    point = lax.axis_index("layer") + 1
    rows = given[0].shape[0]
    copies = []

    def send(source, target, portion):
        block = target.at[0, pl.ds(portion * rows, rows), :]
        copies.append(pltpu.make_async_copy(source, block, sems.at[len(copies)]))
        copies[-1].start()

    for portion in range(PORTIONS):
        send(given[3 * portion], outs[0], portion)
    for portion in range(PORTIONS):
        current, *coarser = given[3 * portion : 3 * portion + 3]
        mine = pl.ds(portion * rows, rows)
        for ref, made, least, out in zip(coarser, scratch, (4, 16), outs[1:]):
            made[mine, :] = jnp.where(point >= least, current[...] - ref[...], 0.0)
            send(made.at[mine, :], out, portion)
    taken(sums_ref, (partner_ref,), receivers, total_ref)
    sums = total_ref[...]
    ratios_ref[...] = jnp.sqrt(sums[0:1] / (sums[1:2] + epsilon))
    for copy in copies:
        copy.wait()


def finish(states, sums, partner, receivers, token):
    rows, width = states[0]["current"].shape
    whole = jax.ShapeDtypeStruct((1, rows * PORTIONS, width), jnp.float32)
    values = [state[name] for state in states for name in ("current", "four", "sixteen")]
    layer_states, defects_four, defects_sixteen, ratios = pl.pallas_call(
        functools.partial(finish_kernel, receivers),
        out_shape=(whole, whole, whole, jax.ShapeDtypeStruct((1, 128), jnp.float32)),
        in_specs=[WHOLE] * (3 + len(values)),
        out_specs=(FAR, FAR, FAR, WHOLE),
        scratch_shapes=[pltpu.VMEM((rows * PORTIONS, width), jnp.float32)] * 2
        + [pltpu.VMEM(TOKEN.shape, jnp.float32), pltpu.SemaphoreType.DMA((3 * PORTIONS,))],
        compiler_params=pltpu.CompilerParams(vmem_limit_bytes=8 * 2**20),
    )(sums, partner, token, *values)
    return layer_states, ratios[0, :7], defects_four, defects_sixteen


def local(initial, norm_gains, first_weights, second_weights):
    layers = lax.axis_size("layer")
    hops, routes, restricted = plan(layers)
    token, layer, states = first_round(initial, norm_gains, first_weights[0], second_weights[0])
    steps = gathering(layers, lax.axis_size("dp"))
    sums = None
    for index in range(max(hops)[0] + 1):
        keys = sorted(key for key in hops if key[0] == index)
        if not keys:
            continue
        for portion in range(PORTIONS):
            if steps[0][0] == (index, portion):
                unused, ways, receivers = steps.pop(0)
                sums, token = take(sums, [lax.ppermute(sums, axes, pairs) for axes, pairs in ways], token, receivers)
            current = states[portion]["current"]
            arrivals = [lax.ppermute(current, "layer", [(a - 1, b - 1) for a, b in routes[key]]) for key in keys]
            made = run_round(arrivals, states[portion], layer, [hops[key] for key in keys], token, sums)
            token = made.pop("token")
            sums = made.pop("sums", sums)
            states[portion].update(made)
    ((follows, ((axes, pairs),), receivers),) = steps
    return finish(states, sums, lax.ppermute(sums, axes, pairs), receivers, token)


def solution(mesh):
    placed = (P("dp", None), P("layer", None), P("layer", None, None), P("layer", None, None))
    return jax.shard_map(
        local,
        mesh=mesh,
        in_specs=placed,
        out_specs=(P("layer", "dp", None), P(), P("layer", "dp", None), P("layer", "dp", None)),
        check_vma=False,
    )
```

```python
import functools

import jax
import jax.numpy as jnp
from jax import lax
from jax.experimental import pallas as pl
from jax.experimental.pallas import tpu as pltpu
from jax.sharding import PartitionSpec as P

epsilon = 1e-06
PORTIONS = 2
CHUNK = 1024
LOADS = 4
LAST_ROWS = 8

ADD = "add"
FINE, LEVEL, GAP_FOUR, GAP_SIXTEEN, RESTRICT, COARSEST = 1, 2, 3, 4, 5, 6
SPACING = {FINE: 1.0, LEVEL: 4.0, GAP_FOUR: 4.0, GAP_SIXTEEN: 16.0, RESTRICT: 1.0, COARSEST: 16.0}


def plan(layers):
    def every(residue, shift, job):
        return [(n, n + shift, job) for n in range(1, layers - shift + 1) if n % 4 == residue]

    hops = {
        (0, 0): every(1, 1, FINE),
        (1, 0): every(2, 1, FINE),
        (2, 0): every(3, 1, FINE),
        (3, 0): every(0, 1, FINE) + [(3, 19, GAP_SIXTEEN)],
        (4, 0): every(1, 1, FINE),
        (6, 0): every(2, 1, FINE) + [(16, 32, GAP_SIXTEEN), (4, 20, GAP_SIXTEEN)],
        (6, 1): every(0, 4, GAP_FOUR) + [(2, 18, GAP_SIXTEEN)],
        (7, 0): every(3, 1, RESTRICT),
        (8, 0): [(8, 12, LEVEL), (20, 24, LEVEL), (3, 7, GAP_FOUR), (1, 17, GAP_SIXTEEN)],
        (9, 0): [(12, 16, LEVEL), (24, 28, LEVEL)],
        (10, 0): [(16, 20, LEVEL), (28, 32, LEVEL), (1, 5, GAP_FOUR), (2, 6, GAP_FOUR)],
        (11, 0): [(20, 24, LEVEL)],
        (12, 0): [(24, 28, LEVEL)],
        (12, 1): [(24, 25, FINE)],
        (13, 0): [(28, 29, FINE), (25, 26, FINE), (16, 32, COARSEST)],
        (14, 0): [(29, 30, FINE), (26, 27, FINE)],
        (15, 0): [(30, 31, FINE), (28, 32, GAP_FOUR)],
        (15, 1): [(27, 31, GAP_FOUR), (13, 29, GAP_SIXTEEN)],
    }
    restricted = 7
    like = {(0, 0): (4, 0), (1, 0): (6, 0), (2, 0): (7, 0), (8, 0): (14, 0), (9, 0): (15, 1)}
    closed = {(n, 0) for n in (0, 1, 2, 3, 4, 15)}

    final = {1: -1, 2: 0, 3: 1, 4: 2, 5: 3, 6: 4, 7: 6, 8: 7}
    final.update({12: 8, 16: 9, 20: 10, 24: 11, 28: 12, 32: 13, 25: 12, 26: 13, 27: 14, 29: 13, 30: 14, 31: 15})

    def place(source, target, job, first):
        for key in sorted(hops):
            group = [key] + [k for k in hops if like.get(k) == key or like.get(key) == k]
            if key[0] < first or key in closed or (key == (7, 0) and source == 5):
                continue
            if any(a == source or b == target for k in group for a, b, unused in hops[k]):
                continue
            if any(b == target for k in hops if k[0] == key[0] for unused, b, held in hops[k]):
                continue
            hops[key].append((source, target, job))
            return key[0]
        raise ValueError((source, target, job))

    for anchor in (8, 12, 16, 20):
        for n in (anchor + 1, anchor + 2, anchor + 3):
            final[n] = place(n - 1, n, FINE, max(final[n - 1], restricted) + 1)
    wanted = []
    for n in range(5, layers + 1):
        if n % 4 != 0 and n != 31:
            wanted.append((final[n - 4], n - 4, n, GAP_FOUR))
    for n in range(17, layers):
        if n not in (19, 20):
            wanted.append((final[n - 16], n - 16, n, GAP_SIXTEEN))
    fixed = {(a, b) for pairs in hops.values() for a, b, unused in pairs}
    wanted = [want for want in wanted if want[1:3] not in fixed]
    for ready, source, target, job in sorted(wanted, key=lambda want: (-want[0], want)):
        place(source, target, job, max(13 if target in (24, 28) else 4, ready + 1))

    routes = {key: [(a, b) for a, b, unused in pairs] for key, pairs in hops.items()}
    for key, other in like.items():
        routes[other] = routes[other] + [pair for pair in routes[key] if pair not in routes[other]]
    assert not any(a <= 4 for key, pairs in hops.items() if key[0] > 10 for a, b, unused in pairs)
    for key, other in like.items():
        routes[key] = routes[other]
    return hops, routes, restricted


def gathering(layers, planes):
    def within(pairs):
        return "layer", [(a - 1, b - 1) for a, b in pairs]

    start = [within([(8, 3), (16, 2), (12, 1), (20, 4)]), within([(24, 1), (32, 2), (28, 3)])]
    steps = [((8, 0), start, ADD)]
    for follows, distance in (((8, 1), 1), ((9, 0), 2)):
        steps.append((follows, [within([(n + 1, (n ^ distance) + 1) for n in range(4)])], ADD))
    for follows, distance in (((9, 1), 1), ((10, 0), 2), ((10, 1), 4)):
        pairs = [(n * planes + i, n * planes + (i ^ distance)) for n in range(4) for i in range(planes)]
        steps.append((follows, [(("layer", "dp"), pairs)], ADD))
    for follows, known in (((11, 1), 4), ((14, 0), 8), (None, 16)):
        steps.append((follows, [within([(n, n + known) for n in range(1, known + 1)])], tuple(range(known + 1, 2 * known + 1))))
    assert 2 * known == layers
    return steps


def member(points):
    place = lax.axis_index("layer").astype(jnp.int32)
    mask = 0
    for n in points:
        mask |= 1 << (n - 1)
    if mask >= 2**31:
        mask -= 2**32
    return (lax.shift_right_logical(jnp.int32(mask), place) & 1) == 1


def taken(held_ref, arrived_refs, receivers, target_ref):
    if receivers == ADD:
        total = held_ref[...]
        for ref in arrived_refs:
            total = total + ref[...]
        target_ref[...] = total
    else:
        here = member(receivers)

        @pl.when(here)
        def replace():
            target_ref[...] = arrived_refs[0][...]

        @pl.when(jnp.logical_not(here))
        def keep():
            target_ref[...] = held_ref[...]


def normalised(state, gain_ref):
    mean_square = jnp.mean(state * state, axis=-1, keepdims=True)
    return (state * lax.rsqrt(mean_square + epsilon) * gain_ref[...]).astype(jnp.bfloat16)


def chunk_of(normed, first_ref, second_ref, start, width):
    hidden = jax.nn.gelu(
        jnp.dot(normed, first_ref[:, start : start + width], preferred_element_type=jnp.float32),
        approximate=True,
    ).astype(jnp.bfloat16)
    return jnp.dot(hidden, second_ref[start : start + width, :], preferred_element_type=jnp.float32)


def branch(state, gain_ref, first_ref, second_ref):
    normed = normalised(state, gain_ref)
    total = None
    for start in range(0, first_ref.shape[1], CHUNK):
        part = chunk_of(normed, first_ref, second_ref, start, CHUNK)
        total = part if total is None else total + part
    return total


WHOLE = pl.BlockSpec(memory_space=pltpu.VMEM)
FAR = pl.BlockSpec(memory_space=pltpu.HBM)
TOKEN = jax.ShapeDtypeStruct((8, 128), jnp.float32)


def settings(rows, mebibytes=8):
    return dict(
        compiler_params=pltpu.CompilerParams(vmem_limit_bytes=mebibytes * 2**20),
        cost_estimate=pl.CostEstimate(flops=4 * rows * 1024 * 2048 * 4, bytes_accessed=2**20, transcendentals=0),
    )


def first_kernel(state_hbm, gain_hbm, first_hbm, second_hbm, token_ref, gain_ref, first_ref, second_ref, *refs):
    state_ref, sems = refs[-2:]
    small = [
        pltpu.make_async_copy(state_hbm, state_ref, sems.at[2 * LOADS]),
        pltpu.make_async_copy(gain_hbm, gain_ref, sems.at[2 * LOADS + 1]),
    ]
    for copy in small:
        copy.start()
    width = first_hbm.shape[1] // LOADS
    copies = []
    for k in range(LOADS):
        columns = pl.ds(k * width, width)
        copies.append(pltpu.make_async_copy(first_hbm.at[:, columns], first_ref.at[:, columns], sems.at[2 * k]))
        copies.append(pltpu.make_async_copy(second_hbm.at[columns, :], second_ref.at[columns, :], sems.at[2 * k + 1]))
    for copy in copies:
        copy.start()
    token_ref[...] = jnp.zeros(token_ref.shape, jnp.float32)
    for copy in small:
        copy.wait()
    state = state_ref[...]
    normed = normalised(state, gain_ref)
    update = None
    for k in range(LOADS):
        copies[2 * k].wait()
        copies[2 * k + 1].wait()
        part = chunk_of(normed, first_ref, second_ref, k * width, width)
        update = part if update is None else update + part
    rows = state.shape[0] // PORTIONS
    for portion in range(PORTIONS):
        mine = slice(portion * rows, (portion + 1) * rows)
        for k, spacing in enumerate((1.0, 4.0, 16.0)):
            refs[3 * portion + k][...] = state[mine] + spacing * update[mine]


def first_round(initial, gain, first, second):
    rows = initial.shape[0] // PORTIONS
    block = jax.ShapeDtypeStruct((rows, initial.shape[1]), jnp.float32)
    made = pl.pallas_call(
        first_kernel,
        out_shape=(
            TOKEN,
            jax.ShapeDtypeStruct(gain.shape, gain.dtype),
            jax.ShapeDtypeStruct(first.shape, first.dtype),
            jax.ShapeDtypeStruct(second.shape, second.dtype),
        )
        + (block,) * (3 * PORTIONS),
        in_specs=[FAR] * 4,
        out_specs=(WHOLE,) * (4 + 3 * PORTIONS),
        scratch_shapes=[pltpu.VMEM(initial.shape, jnp.float32), pltpu.SemaphoreType.DMA((2 * LOADS + 2,))],
        **settings(initial.shape[0], 43),
    )(initial, gain, first, second)
    states = [
        dict(zip(("current", "four", "sixteen"), made[4 + 3 * k : 7 + 3 * k])) for k in range(PORTIONS)
    ]
    return made[0], made[1:4], states


def targets(jobs):
    return [n for points in jobs.values() for n in points]


def round_kernel(jobs, more, names_in, names_out, *refs):
    given = dict(zip(names_in, refs))
    made = dict(zip(names_out, refs[len(names_in) :]))
    picked_ref, update_ref = refs[-2:]
    rows = given["arrived"].shape[0]
    place = lax.axis_index("layer").astype(jnp.int32)
    made["token"][...] = given["token"][...]
    doubled = sorted(set(targets(jobs)) & set(targets(more)))
    layer = (given["gain"], given["first"], given["second"])

    if more:

        @pl.when(member(targets(jobs)))
        def pick():
            picked_ref[:rows, :] = given["arrived"][...]

        @pl.when(member(sorted(set(targets(more)) - set(doubled))))
        def pick_other():
            picked_ref[:rows, :] = given["other"][...]

    busy = sorted((set(targets(jobs)) | set(targets(more))) - set(doubled))

    @pl.when(member(busy))
    def compute():
        state = picked_ref[:rows, :] if more else given["arrived"][...]
        update_ref[:rows, :] = branch(state, *layer)

    if doubled:

        @pl.when(member(doubled))
        def compute_both():
            picked_ref[rows:, :] = given["other"][...]
            update_ref[...] = branch(picked_ref[...], *layer)

    both = {job: sorted(jobs.get(job, []) + more.get(job, [])) for job in set(jobs) | set(more)}
    for name, writers in WRITERS.items():
        if name in made and name in given:

            @pl.when(jnp.logical_not(member([n for job in writers for n in both.get(job, ())])))
            def keep(name=name):
                made[name][...] = given[name][...]

    if "sums" in given:
        made["sums"][...] = given["sums"][...]
    elif "sums" in made:
        made["sums"][...] = jnp.zeros(made["sums"].shape, jnp.float32)

    def finish(job, stepped, update):
        if job == FINE:
            made["current"][...] = stepped
        if job == LEVEL:
            made["four"][...] = stepped
            made["current"][...] = stepped + given["coarse"][...]
        if job == GAP_FOUR:
            made["four"][...] = stepped
        if job == GAP_SIXTEEN:
            made["sixteen"][...] = stepped
        if job == COARSEST:
            made["current"][...] = given["current"][...] + (stepped - given["sixteen"][...])
            made["sixteen"][...] = stepped
        if job == RESTRICT:
            gap = stepped - given["current"][...]
            made["current"][...] = stepped
            made["coarse"][...] = stepped - given["four"][...]
            shape = made["sums"].shape
            row = lax.broadcasted_iota(jnp.int32, shape, 0)
            here = lax.broadcasted_iota(jnp.int32, shape, 1) == (place + 1) // 4 - 2
            pair = jnp.where(row == 0, jnp.sum(gap * gap), jnp.sum(update * update))
            made["sums"][...] += jnp.where(here & (row < 2), pair, 0.0)

    for hop, name, start in ((jobs, "arrived", 0), (more, "other", rows)):
        for job, points in hop.items():
            for twice in (False, True):
                mine = [n for n in points if (n in doubled) == twice]
                if mine:

                    @pl.when(member(mine))
                    def done(job=job, name=name, start=start if twice else 0):
                        update = update_ref[start : start + rows, :]
                        finish(job, given[name][...] + SPACING[job] * update, update)


WRITERS = {
    "current": {FINE, LEVEL, RESTRICT, COARSEST},
    "four": {LEVEL, GAP_FOUR},
    "sixteen": {GAP_SIXTEEN, COARSEST},
    "coarse": {RESTRICT},
}
READERS = {
    "current": {FINE, LEVEL, RESTRICT, COARSEST},
    "four": {RESTRICT, LEVEL, GAP_FOUR},
    "sixteen": {GAP_SIXTEEN, COARSEST},
    "coarse": {LEVEL},
}


def by_job(pairs):
    jobs = {}
    for unused, target, job in pairs:
        jobs.setdefault(job, []).append(target)
    return jobs


def run_round(arrivals, state, layer, hops, token, sums):
    jobs, more = by_job(hops[0]), by_job(hops[1] if len(hops) > 1 else [])
    kinds = set(jobs) | set(more)
    names_in = ["arrived", "other"][: len(arrivals)] + ["gain", "first", "second", "token"]
    values = [*arrivals, *layer, token]
    names_out, shapes = ["token"], [TOKEN]
    rows, width = arrivals[0].shape
    block = jax.ShapeDtypeStruct((rows, width), jnp.float32)
    for name, writers in WRITERS.items():
        if name in state and kinds & READERS[name]:
            names_in.append(name)
            values.append(state[name])
        if kinds & writers:
            names_out.append(name)
            shapes.append(block)
    if RESTRICT in kinds:
        if sums is not None:
            names_in.append("sums")
            values.append(sums)
        names_out.append("sums")
        shapes.append(TOKEN)
    scratch = pltpu.VMEM((rows * len(arrivals), width), jnp.float32)
    made = pl.pallas_call(
        functools.partial(round_kernel, jobs, more, names_in, names_out),
        out_shape=tuple(shapes),
        in_specs=[WHOLE] * len(names_in),
        out_specs=(WHOLE,) * len(shapes),
        scratch_shapes=[scratch, scratch],
        **settings(rows),
    )(*values)
    return dict(zip(names_out, made))


def take_kernel(receivers, sums_ref, token_ref, *refs):
    *partner_refs, made_ref, passed_ref = refs
    taken(sums_ref, partner_refs, receivers, made_ref.at[: sums_ref.shape[0], :])
    passed_ref[...] = token_ref[...]


def take(sums, partners, token, receivers, rows):
    return pl.pallas_call(
        functools.partial(take_kernel, receivers),
        out_shape=(jax.ShapeDtypeStruct((rows, sums.shape[1]), jnp.float32), TOKEN),
        in_specs=[WHOLE] * (2 + len(partners)),
        out_specs=(WHOLE, WHOLE),
        compiler_params=pltpu.CompilerParams(vmem_limit_bytes=8 * 2**20),
    )(sums, token, *partners)


def finish_kernel(receivers, sums_ref, partner_ref, token_ref, *refs):
    given = refs[: 3 * PORTIONS]
    outs = refs[3 * PORTIONS : 3 * PORTIONS + 3]
    ratios_ref, *scratch, total_ref, sems = refs[3 * PORTIONS + 3 :]
    point = lax.axis_index("layer") + 1
    rows = given[0].shape[0]
    copies = []

    def send(source, target, portion):
        block = target.at[0, pl.ds(portion * rows, rows), :]
        copies.append(pltpu.make_async_copy(source, block, sems.at[len(copies)]))
        copies[-1].start()

    for portion in range(PORTIONS):
        send(given[3 * portion], outs[0], portion)
    for portion in range(PORTIONS):
        current, *coarser = given[3 * portion : 3 * portion + 3]
        mine = pl.ds(portion * rows, rows)
        for ref, made, least, out in zip(coarser, scratch, (4, 16), outs[1:]):
            made[mine, :] = jnp.where(point >= least, current[...] - ref[...], 0.0)
            send(made.at[mine, :], out, portion)
    taken(sums_ref, (partner_ref,), receivers, total_ref)
    sums = total_ref[0:8, :]
    ratios_ref[...] = jnp.sqrt(sums[0:1] / (sums[1:2] + epsilon))
    for copy in copies:
        copy.wait()


def finish(states, sums, partner, receivers, token):
    rows, width = states[0]["current"].shape
    whole = jax.ShapeDtypeStruct((1, rows * PORTIONS, width), jnp.float32)
    values = [state[name] for state in states for name in ("current", "four", "sixteen")]
    layer_states, defects_four, defects_sixteen, ratios = pl.pallas_call(
        functools.partial(finish_kernel, receivers),
        out_shape=(whole, whole, whole, jax.ShapeDtypeStruct((1, 128), jnp.float32)),
        in_specs=[WHOLE] * (3 + len(values)),
        out_specs=(FAR, FAR, FAR, WHOLE),
        scratch_shapes=[pltpu.VMEM((rows * PORTIONS, width), jnp.float32)] * 2
        + [pltpu.VMEM(sums.shape, jnp.float32), pltpu.SemaphoreType.DMA((3 * PORTIONS,))],
        compiler_params=pltpu.CompilerParams(vmem_limit_bytes=8 * 2**20),
    )(sums, partner, token, *values)
    return layer_states, ratios[0, :7], defects_four, defects_sixteen


def local(initial, norm_gains, first_weights, second_weights):
    layers = lax.axis_size("layer")
    hops, routes, restricted = plan(layers)
    token, layer, states = first_round(initial, norm_gains, first_weights[0], second_weights[0])
    steps = gathering(layers, lax.axis_size("dp"))
    sums = None
    for index in range(max(hops)[0] + 1):
        keys = sorted(key for key in hops if key[0] == index)
        if not keys:
            continue
        for portion in range(PORTIONS):
            if steps and steps[0][0] == (index, portion):
                unused, ways, receivers = steps.pop(0)
                partners = [lax.ppermute(sums, axes, pairs) for axes, pairs in ways]
                sums, token = take(sums, partners, token, receivers, LAST_ROWS if len(steps) == 1 else TOKEN.shape[0])
            current = states[portion]["current"]
            arrivals = [lax.ppermute(current, "layer", [(a - 1, b - 1) for a, b in routes[key]]) for key in keys]
            made = run_round(arrivals, states[portion], layer, [hops[key] for key in keys], token, sums)
            token = made.pop("token")
            sums = made.pop("sums", sums)
            states[portion].update(made)
    ((unused, ((axes, pairs),), receivers),) = steps
    return finish(states, sums, lax.ppermute(sums, axes, pairs), receivers, token)


def solution(mesh):
    placed = (P("dp", None), P("layer", None), P("layer", None, None), P("layer", None, None))
    return jax.shard_map(
        local,
        mesh=mesh,
        in_specs=placed,
        out_specs=(P("layer", "dp", None), P(), P("layer", "dp", None), P("layer", "dp", None)),
        check_vma=False,
    )
```

```python
import functools

import jax
import jax.numpy as jnp
from jax import lax
from jax.experimental import pallas as pl
from jax.experimental.pallas import tpu as pltpu
from jax.sharding import PartitionSpec as P

epsilon = 1e-06
PORTIONS = 2
CHUNK = 1024
LOADS = 4
BUSY = (27, 30)

ADD = "add"
FINE, LEVEL, GAP_FOUR, GAP_SIXTEEN, RESTRICT, COARSEST = 1, 2, 3, 4, 5, 6
SPACING = {FINE: 1.0, LEVEL: 4.0, GAP_FOUR: 4.0, GAP_SIXTEEN: 16.0, RESTRICT: 1.0, COARSEST: 16.0}


def plan(layers):
    def every(residue, shift, job):
        return [(n, n + shift, job) for n in range(1, layers - shift + 1) if n % 4 == residue]

    hops = {
        (0, 0): every(1, 1, FINE),
        (1, 0): every(2, 1, FINE),
        (2, 0): every(3, 1, FINE),
        (3, 0): every(0, 1, FINE) + [(3, 19, GAP_SIXTEEN)],
        (4, 0): every(1, 1, FINE),
        (6, 0): every(2, 1, FINE) + [(16, 32, GAP_SIXTEEN), (4, 20, GAP_SIXTEEN)],
        (6, 1): every(0, 4, GAP_FOUR) + [(2, 18, GAP_SIXTEEN)],
        (7, 0): every(3, 1, RESTRICT),
        (8, 0): [(8, 12, LEVEL), (20, 24, LEVEL), (3, 7, GAP_FOUR), (1, 17, GAP_SIXTEEN)],
        (9, 0): [(12, 16, LEVEL), (24, 28, LEVEL)],
        (10, 0): [(16, 20, LEVEL), (28, 32, LEVEL), (1, 5, GAP_FOUR), (2, 6, GAP_FOUR)],
        (11, 0): [(20, 24, LEVEL)],
        (12, 0): [(24, 28, LEVEL)],
        (12, 1): [(24, 25, FINE)],
        (13, 0): [(28, 29, FINE), (25, 26, FINE), (16, 32, COARSEST)],
        (14, 0): [(29, 30, FINE), (26, 27, FINE)],
        (15, 0): [(30, 31, FINE), (28, 32, GAP_FOUR)],
        (15, 1): [(27, 31, GAP_FOUR), (13, 29, GAP_SIXTEEN)],
    }
    restricted = 7
    like = {(0, 0): (4, 0), (1, 0): (6, 0), (2, 0): (7, 0), (8, 0): (14, 0), (9, 0): (15, 1)}
    closed = {(n, 0) for n in (0, 1, 2, 3, 4, 15)}

    final = {1: -1, 2: 0, 3: 1, 4: 2, 5: 3, 6: 4, 7: 6, 8: 7}
    final.update({12: 8, 16: 9, 20: 10, 24: 11, 28: 12, 32: 13, 25: 12, 26: 13, 27: 14, 29: 13, 30: 14, 31: 15})

    def place(source, target, job, first):
        for key in sorted(hops):
            group = [key] + [k for k in hops if like.get(k) == key or like.get(key) == k]
            if key[0] < first or key in closed or (key == (7, 0) and source == 5):
                continue
            if any(a == source or b == target for k in group for a, b, unused in hops[k]):
                continue
            if any(b == target for k in hops if k[0] == key[0] for unused, b, held in hops[k]):
                continue
            hops[key].append((source, target, job))
            return key[0]
        raise ValueError((source, target, job))

    for anchor in (8, 12, 16, 20):
        for n in (anchor + 1, anchor + 2, anchor + 3):
            final[n] = place(n - 1, n, FINE, max(final[n - 1], restricted) + 1)
    wanted = []
    for n in range(5, layers + 1):
        if n % 4 != 0 and n != 31:
            wanted.append((final[n - 4], n - 4, n, GAP_FOUR))
    for n in range(17, layers):
        if n not in (19, 20):
            wanted.append((final[n - 16], n - 16, n, GAP_SIXTEEN))
    fixed = {(a, b) for pairs in hops.values() for a, b, unused in pairs}
    wanted = [want for want in wanted if want[1:3] not in fixed]
    for ready, source, target, job in sorted(wanted, key=lambda want: (-want[0], want)):
        place(source, target, job, max(13 if target in (24, 28) else 4, ready + 1))

    routes = {key: [(a, b) for a, b, unused in pairs] for key, pairs in hops.items()}
    for key, other in like.items():
        routes[other] = routes[other] + [pair for pair in routes[key] if pair not in routes[other]]
    assert not any(a <= 4 for key, pairs in hops.items() if key[0] > 10 for a, b, unused in pairs)
    for key, other in like.items():
        routes[key] = routes[other]
    return hops, routes, restricted


def gathering(routes, layers, planes):
    def within(pairs):
        return "layer", [(a - 1, b - 1) for a, b in pairs]

    start = [within([(8, 3), (16, 2), (12, 1), (20, 4)]), within([(24, 1), (32, 2), (28, 3)])]
    steps = [((8, 0), start, ADD)]
    for follows, distance in (((8, 1), 1), ((9, 0), 2)):
        steps.append((follows, [within([(n + 1, (n ^ distance) + 1) for n in range(4)])], ADD))
    for follows, distance in (((9, 1), 1), ((10, 0), 2), ((10, 1), 4)):
        pairs = [(n * planes + i, n * planes + (i ^ distance)) for n in range(4) for i in range(planes)]
        steps.append((follows, [(("layer", "dp"), pairs)], ADD))
    for follows, known in (((11, 1), 4), ((13, 1), 8), ((14, 1), 16)):
        pairs = [(n, n + known) for n in range(1, known + 1) if n + known not in BUSY]
        steps.append((follows, [within(pairs)], tuple(b for a, b in pairs)))
    assert 2 * known == layers
    return steps, [("layer", within(routes[key])[1], (n,)) for key, n in (((4, 0), 30), ((6, 0), 27))]


def member(points):
    place = lax.axis_index("layer").astype(jnp.int32)
    mask = 0
    for n in points:
        mask |= 1 << (n - 1)
    if mask >= 2**31:
        mask -= 2**32
    return (lax.shift_right_logical(jnp.int32(mask), place) & 1) == 1


def taken(held_ref, arrived_refs, receivers, target_ref):
    if receivers == ADD:
        total = held_ref[...]
        for ref in arrived_refs:
            total = total + ref[...]
        target_ref[...] = total
    else:
        here = member(receivers)

        @pl.when(here)
        def replace():
            target_ref[...] = arrived_refs[0][...]

        @pl.when(jnp.logical_not(here))
        def keep():
            target_ref[...] = held_ref[...]


def normalised(state, gain_ref):
    mean_square = jnp.mean(state * state, axis=-1, keepdims=True)
    return (state * lax.rsqrt(mean_square + epsilon) * gain_ref[...]).astype(jnp.bfloat16)


def chunk_of(normed, first_ref, second_ref, start, width):
    hidden = jax.nn.gelu(
        jnp.dot(normed, first_ref[:, start : start + width], preferred_element_type=jnp.float32),
        approximate=True,
    ).astype(jnp.bfloat16)
    return jnp.dot(hidden, second_ref[start : start + width, :], preferred_element_type=jnp.float32)


def branch(state, gain_ref, first_ref, second_ref):
    normed = normalised(state, gain_ref)
    total = None
    for start in range(0, first_ref.shape[1], CHUNK):
        part = chunk_of(normed, first_ref, second_ref, start, CHUNK)
        total = part if total is None else total + part
    return total


WHOLE = pl.BlockSpec(memory_space=pltpu.VMEM)
FAR = pl.BlockSpec(memory_space=pltpu.HBM)
TOKEN = jax.ShapeDtypeStruct((8, 128), jnp.float32)


def settings(rows, mebibytes=8):
    return dict(
        compiler_params=pltpu.CompilerParams(vmem_limit_bytes=mebibytes * 2**20),
        cost_estimate=pl.CostEstimate(flops=4 * rows * 1024 * 2048 * 4, bytes_accessed=2**20, transcendentals=0),
    )


def first_kernel(state_hbm, gain_hbm, first_hbm, second_hbm, token_ref, gain_ref, first_ref, second_ref, *refs):
    state_ref, sems = refs[-2:]
    small = [
        pltpu.make_async_copy(state_hbm, state_ref, sems.at[2 * LOADS]),
        pltpu.make_async_copy(gain_hbm, gain_ref, sems.at[2 * LOADS + 1]),
    ]
    for copy in small:
        copy.start()
    width = first_hbm.shape[1] // LOADS
    copies = []
    for k in range(LOADS):
        columns = pl.ds(k * width, width)
        copies.append(pltpu.make_async_copy(first_hbm.at[:, columns], first_ref.at[:, columns], sems.at[2 * k]))
        copies.append(pltpu.make_async_copy(second_hbm.at[columns, :], second_ref.at[columns, :], sems.at[2 * k + 1]))
    for copy in copies:
        copy.start()
    token_ref[...] = jnp.zeros(token_ref.shape, jnp.float32)
    for copy in small:
        copy.wait()
    state = state_ref[...]
    normed = normalised(state, gain_ref)
    update = None
    for k in range(LOADS):
        copies[2 * k].wait()
        copies[2 * k + 1].wait()
        part = chunk_of(normed, first_ref, second_ref, k * width, width)
        update = part if update is None else update + part
    rows = state.shape[0] // PORTIONS
    for portion in range(PORTIONS):
        mine = slice(portion * rows, (portion + 1) * rows)
        for k, spacing in enumerate((1.0, 4.0, 16.0)):
            refs[3 * portion + k][...] = state[mine] + spacing * update[mine]


def first_round(initial, gain, first, second):
    rows = initial.shape[0] // PORTIONS
    block = jax.ShapeDtypeStruct((rows, initial.shape[1]), jnp.float32)
    made = pl.pallas_call(
        first_kernel,
        out_shape=(
            TOKEN,
            jax.ShapeDtypeStruct(gain.shape, gain.dtype),
            jax.ShapeDtypeStruct(first.shape, first.dtype),
            jax.ShapeDtypeStruct(second.shape, second.dtype),
        )
        + (block,) * (3 * PORTIONS),
        in_specs=[FAR] * 4,
        out_specs=(WHOLE,) * (4 + 3 * PORTIONS),
        scratch_shapes=[pltpu.VMEM(initial.shape, jnp.float32), pltpu.SemaphoreType.DMA((2 * LOADS + 2,))],
        **settings(initial.shape[0], 43),
    )(initial, gain, first, second)
    states = [
        dict(zip(("current", "four", "sixteen"), made[4 + 3 * k : 7 + 3 * k])) for k in range(PORTIONS)
    ]
    return made[0], made[1:4], states


def targets(jobs):
    return [n for points in jobs.values() for n in points]


def round_kernel(jobs, more, names_in, names_out, *refs):
    given = dict(zip(names_in, refs))
    made = dict(zip(names_out, refs[len(names_in) :]))
    picked_ref, update_ref = refs[-2:]
    rows = given["arrived"].shape[0]
    place = lax.axis_index("layer").astype(jnp.int32)
    made["token"][...] = given["token"][...]
    doubled = sorted(set(targets(jobs)) & set(targets(more)))
    layer = (given["gain"], given["first"], given["second"])

    if more:

        @pl.when(member(targets(jobs)))
        def pick():
            picked_ref[:rows, :] = given["arrived"][...]

        @pl.when(member(sorted(set(targets(more)) - set(doubled))))
        def pick_other():
            picked_ref[:rows, :] = given["other"][...]

    busy = sorted((set(targets(jobs)) | set(targets(more))) - set(doubled))

    @pl.when(member(busy))
    def compute():
        state = picked_ref[:rows, :] if more else given["arrived"][...]
        update_ref[:rows, :] = branch(state, *layer)

    if doubled:

        @pl.when(member(doubled))
        def compute_both():
            picked_ref[rows:, :] = given["other"][...]
            update_ref[...] = branch(picked_ref[...], *layer)

    both = {job: sorted(jobs.get(job, []) + more.get(job, [])) for job in set(jobs) | set(more)}
    for name, writers in WRITERS.items():
        if name in made and name in given:

            @pl.when(jnp.logical_not(member([n for job in writers for n in both.get(job, ())])))
            def keep(name=name):
                made[name][...] = given[name][...]

    if "sums" in given:
        made["sums"][...] = given["sums"][...]
    elif "sums" in made:
        made["sums"][...] = jnp.zeros(made["sums"].shape, jnp.float32)

    def finish(job, stepped, update):
        if job == FINE:
            made["current"][...] = stepped
        if job == LEVEL:
            made["four"][...] = stepped
            made["current"][...] = stepped + given["coarse"][...]
        if job == GAP_FOUR:
            made["four"][...] = stepped
        if job == GAP_SIXTEEN:
            made["sixteen"][...] = stepped
        if job == COARSEST:
            made["current"][...] = given["current"][...] + (stepped - given["sixteen"][...])
            made["sixteen"][...] = stepped
        if job == RESTRICT:
            gap = stepped - given["current"][...]
            made["current"][...] = stepped
            made["coarse"][...] = stepped - given["four"][...]
            shape = made["sums"].shape
            row = lax.broadcasted_iota(jnp.int32, shape, 0)
            here = lax.broadcasted_iota(jnp.int32, shape, 1) == (place + 1) // 4 - 2
            pair = jnp.where(row == 0, jnp.sum(gap * gap), jnp.sum(update * update))
            made["sums"][...] += jnp.where(here & (row < 2), pair, 0.0)

    for hop, name, start in ((jobs, "arrived", 0), (more, "other", rows)):
        for job, points in hop.items():
            for twice in (False, True):
                mine = [n for n in points if (n in doubled) == twice]
                if mine:

                    @pl.when(member(mine))
                    def done(job=job, name=name, start=start if twice else 0):
                        update = update_ref[start : start + rows, :]
                        finish(job, given[name][...] + SPACING[job] * update, update)


WRITERS = {
    "current": {FINE, LEVEL, RESTRICT, COARSEST},
    "four": {LEVEL, GAP_FOUR},
    "sixteen": {GAP_SIXTEEN, COARSEST},
    "coarse": {RESTRICT},
}
READERS = {
    "current": {FINE, LEVEL, RESTRICT, COARSEST},
    "four": {RESTRICT, LEVEL, GAP_FOUR},
    "sixteen": {GAP_SIXTEEN, COARSEST},
    "coarse": {LEVEL},
}


def by_job(pairs):
    jobs = {}
    for unused, target, job in pairs:
        jobs.setdefault(job, []).append(target)
    return jobs


def run_round(arrivals, state, layer, hops, token, sums):
    jobs, more = by_job(hops[0]), by_job(hops[1] if len(hops) > 1 else [])
    kinds = set(jobs) | set(more)
    names_in = ["arrived", "other"][: len(arrivals)] + ["gain", "first", "second", "token"]
    values = [*arrivals, *layer, token]
    names_out, shapes = ["token"], [TOKEN]
    rows, width = arrivals[0].shape
    block = jax.ShapeDtypeStruct((rows, width), jnp.float32)
    for name, writers in WRITERS.items():
        if name in state and kinds & READERS[name]:
            names_in.append(name)
            values.append(state[name])
        if kinds & writers:
            names_out.append(name)
            shapes.append(block)
    if RESTRICT in kinds:
        if sums is not None:
            names_in.append("sums")
            values.append(sums)
        names_out.append("sums")
        shapes.append(TOKEN)
    scratch = pltpu.VMEM((rows * len(arrivals), width), jnp.float32)
    made = pl.pallas_call(
        functools.partial(round_kernel, jobs, more, names_in, names_out),
        out_shape=tuple(shapes),
        in_specs=[WHOLE] * len(names_in),
        out_specs=(WHOLE,) * len(shapes),
        scratch_shapes=[scratch, scratch],
        **settings(rows),
    )(*values)
    return dict(zip(names_out, made))


def take_kernel(receivers, sums_ref, token_ref, *refs):
    *partner_refs, made_ref, passed_ref = refs
    taken(sums_ref, partner_refs, receivers, made_ref)
    passed_ref[...] = token_ref[...]


def take(sums, partners, token, receivers):
    return pl.pallas_call(
        functools.partial(take_kernel, receivers),
        out_shape=(TOKEN, TOKEN),
        in_specs=[WHOLE] * (2 + len(partners)),
        out_specs=(WHOLE, WHOLE),
        compiler_params=pltpu.CompilerParams(vmem_limit_bytes=8 * 2**20),
    )(sums, token, *partners)


def finish_kernel(receivers, sums_ref, token_ref, *refs):
    partner_refs, refs = refs[: len(receivers)], refs[len(receivers) :]
    given = refs[: 3 * PORTIONS]
    outs = refs[3 * PORTIONS : 3 * PORTIONS + 3]
    ratios_ref, *scratch, total_ref, sems = refs[3 * PORTIONS + 3 :]
    point = lax.axis_index("layer") + 1
    rows = given[0].shape[0]
    copies = []

    def send(source, target, portion):
        block = target.at[0, pl.ds(portion * rows, rows), :]
        copies.append(pltpu.make_async_copy(source, block, sems.at[len(copies)]))
        copies[-1].start()

    for portion in range(PORTIONS):
        send(given[3 * portion], outs[0], portion)
    for portion in range(PORTIONS):
        current, *coarser = given[3 * portion : 3 * portion + 3]
        mine = pl.ds(portion * rows, rows)
        for ref, made, least, out in zip(coarser, scratch, (4, 16), outs[1:]):
            made[mine, :] = jnp.where(point >= least, current[...] - ref[...], 0.0)
            send(made.at[mine, :], out, portion)
    total_ref[...] = sums_ref[...]
    for points, partner_ref in zip(receivers, partner_refs):

        @pl.when(member(points))
        def replace(partner_ref=partner_ref):
            total_ref[...] = partner_ref[...]

    sums = total_ref[0:8, :]
    ratios_ref[...] = jnp.sqrt(sums[0:1] / (sums[1:2] + epsilon))
    for copy in copies:
        copy.wait()


def finish(states, sums, partners, receivers, token):
    rows, width = states[0]["current"].shape
    whole = jax.ShapeDtypeStruct((1, rows * PORTIONS, width), jnp.float32)
    values = [state[name] for state in states for name in ("current", "four", "sixteen")]
    layer_states, defects_four, defects_sixteen, ratios = pl.pallas_call(
        functools.partial(finish_kernel, receivers),
        out_shape=(whole, whole, whole, jax.ShapeDtypeStruct((1, 128), jnp.float32)),
        in_specs=[WHOLE] * (2 + len(partners) + len(values)),
        out_specs=(FAR, FAR, FAR, WHOLE),
        scratch_shapes=[pltpu.VMEM((rows * PORTIONS, width), jnp.float32)] * 2
        + [pltpu.VMEM(sums.shape, jnp.float32), pltpu.SemaphoreType.DMA((3 * PORTIONS,))],
        compiler_params=pltpu.CompilerParams(vmem_limit_bytes=8 * 2**20),
    )(sums, token, *partners, *values)
    return layer_states, ratios[0, :7], defects_four, defects_sixteen


def local(initial, norm_gains, first_weights, second_weights):
    layers = lax.axis_size("layer")
    hops, routes, restricted = plan(layers)
    token, layer, states = first_round(initial, norm_gains, first_weights[0], second_weights[0])
    steps, ends = gathering(routes, layers, lax.axis_size("dp"))
    sums = None
    for index in range(max(hops)[0] + 1):
        keys = sorted(key for key in hops if key[0] == index)
        if not keys:
            continue
        for portion in range(PORTIONS):
            if steps and steps[0][0] == (index, portion):
                unused, ways, receivers = steps.pop(0)
                partners = [lax.ppermute(sums, axes, pairs) for axes, pairs in ways]
                sums, token = take(sums, partners, token, receivers)
            current = states[portion]["current"]
            arrivals = [lax.ppermute(current, "layer", [(a - 1, b - 1) for a, b in routes[key]]) for key in keys]
            made = run_round(arrivals, states[portion], layer, [hops[key] for key in keys], token, sums)
            token = made.pop("token")
            sums = made.pop("sums", sums)
            states[portion].update(made)
    assert not steps
    partners = [lax.ppermute(sums, axes, pairs) for axes, pairs, unused in ends]
    return finish(states, sums, partners, [receivers for unused, pairs, receivers in ends], token)


def solution(mesh):
    placed = (P("dp", None), P("layer", None), P("layer", None, None), P("layer", None, None))
    return jax.shard_map(
        local,
        mesh=mesh,
        in_specs=placed,
        out_specs=(P("layer", "dp", None), P(), P("layer", "dp", None), P("layer", "dp", None)),
        check_vma=False,
    )
```

```python
import functools

import jax
import jax.numpy as jnp
from jax import lax
from jax.experimental import pallas as pl
from jax.experimental.pallas import tpu as pltpu
from jax.sharding import PartitionSpec as P

epsilon = 1e-06
PORTIONS = 2
CHUNK = 1024
LOADS = 4

ADD = "add"
FINE, LEVEL, GAP_FOUR, GAP_SIXTEEN, RESTRICT, COARSEST = 1, 2, 3, 4, 5, 6
SPACING = {FINE: 1.0, LEVEL: 4.0, GAP_FOUR: 4.0, GAP_SIXTEEN: 16.0, RESTRICT: 1.0, COARSEST: 16.0}


def plan(layers):
    def every(residue, shift, job):
        return [(n, n + shift, job) for n in range(1, layers - shift + 1) if n % 4 == residue]

    hops = {
        (0, 0): every(1, 1, FINE),
        (1, 0): every(2, 1, FINE),
        (2, 0): every(3, 1, FINE),
        (3, 0): every(0, 1, FINE) + [(3, 19, GAP_SIXTEEN)],
        (4, 0): every(1, 1, FINE),
        (6, 0): every(2, 1, FINE) + [(16, 32, GAP_SIXTEEN), (4, 20, GAP_SIXTEEN)],
        (6, 1): every(0, 4, GAP_FOUR) + [(2, 18, GAP_SIXTEEN)],
        (7, 0): every(3, 1, RESTRICT),
        (8, 0): [(8, 12, LEVEL), (20, 24, LEVEL), (3, 7, GAP_FOUR), (1, 17, GAP_SIXTEEN)],
        (9, 0): [(12, 16, LEVEL), (24, 28, LEVEL)],
        (10, 0): [(16, 20, LEVEL), (28, 32, LEVEL), (1, 5, GAP_FOUR), (2, 6, GAP_FOUR)],
        (11, 0): [(20, 24, LEVEL)],
        (12, 0): [(24, 28, LEVEL)],
        (12, 1): [(24, 25, FINE)],
        (13, 0): [(28, 29, FINE), (25, 26, FINE), (16, 32, COARSEST)],
        (14, 0): [(29, 30, FINE), (26, 27, FINE), (13, 29, GAP_SIXTEEN)],
        (15, 0): [(30, 31, FINE), (28, 32, GAP_FOUR)],
        (15, 1): [(27, 31, GAP_FOUR), (25, 29, GAP_FOUR), (21, 25, GAP_FOUR)],
    }
    restricted = 7
    like = {(0, 0): (4, 0), (1, 0): (6, 0), (2, 0): (7, 0), (8, 0): (14, 0), (9, 0): (15, 1)}
    closed = {(n, 0) for n in (0, 1, 2, 3, 4, 15)}

    final = {1: -1, 2: 0, 3: 1, 4: 2, 5: 3, 6: 4, 7: 6, 8: 7}
    final.update({12: 8, 16: 9, 20: 10, 24: 11, 28: 12, 32: 13, 25: 12, 26: 13, 27: 14, 29: 13, 30: 14, 31: 15})

    def place(source, target, job, first):
        for key in sorted(hops):
            group = [key] + [k for k in hops if like.get(k) == key or like.get(key) == k]
            if key[0] < first or key in closed or (key == (7, 0) and source == 5):
                continue
            if any(a == source or b == target for k in group for a, b, unused in hops[k]):
                continue
            if any(b == target for k in hops if k[0] == key[0] for unused, b, held in hops[k]):
                continue
            hops[key].append((source, target, job))
            return key[0]
        raise ValueError((source, target, job))

    for anchor in (8, 12, 16, 20):
        for n in (anchor + 1, anchor + 2, anchor + 3):
            final[n] = place(n - 1, n, FINE, max(final[n - 1], restricted) + 1)
    wanted = []
    for n in range(5, layers + 1):
        if n % 4 != 0 and n != 31:
            wanted.append((final[n - 4], n - 4, n, GAP_FOUR))
    for n in range(17, layers):
        if n not in (19, 20):
            wanted.append((final[n - 16], n - 16, n, GAP_SIXTEEN))
    fixed = {(a, b) for pairs in hops.values() for a, b, unused in pairs}
    wanted = [want for want in wanted if want[1:3] not in fixed]
    for ready, source, target, job in sorted(wanted, key=lambda want: (-want[0], want)):
        place(source, target, job, max(13 if target in (24, 28) else 4, ready + 1))

    routes = {key: [(a, b) for a, b, unused in pairs] for key, pairs in hops.items()}
    for key, other in like.items():
        routes[other] = routes[other] + [pair for pair in routes[key] if pair not in routes[other]]
    assert not any(a <= 4 for key, pairs in hops.items() if key[0] > 10 for a, b, unused in pairs)
    for key, other in like.items():
        routes[key] = routes[other]
    return hops, routes, restricted


def gathering(layers, planes):
    def within(pairs):
        return "layer", [(a - 1, b - 1) for a, b in pairs]

    start = [within([(8, 3), (16, 2), (12, 1), (20, 4)]), within([(24, 1), (32, 2), (28, 3)])]
    steps = [((8, 0), start, ADD)]
    for follows, distance in (((8, 1), 1), ((9, 0), 2)):
        steps.append((follows, [within([(n + 1, (n ^ distance) + 1) for n in range(4)])], ADD))
    for follows, distance in (((9, 1), 1), ((10, 0), 2), ((10, 1), 4)):
        pairs = [(n * planes + i, n * planes + (i ^ distance)) for n in range(4) for i in range(planes)]
        steps.append((follows, [(("layer", "dp"), pairs)], ADD))
    for follows, known in (((11, 1), 4), ((14, 0), 8), (None, 16)):
        steps.append((follows, [within([(n, n + known) for n in range(1, known + 1)])], tuple(range(known + 1, 2 * known + 1))))
    assert 2 * known == layers
    return steps


def member(points):
    place = lax.axis_index("layer").astype(jnp.int32)
    mask = 0
    for n in points:
        mask |= 1 << (n - 1)
    if mask >= 2**31:
        mask -= 2**32
    return (lax.shift_right_logical(jnp.int32(mask), place) & 1) == 1


def taken(held_ref, arrived_refs, receivers, target_ref):
    if receivers == ADD:
        total = held_ref[...]
        for ref in arrived_refs:
            total = total + ref[...]
        target_ref[...] = total
    else:
        here = member(receivers)

        @pl.when(here)
        def replace():
            target_ref[...] = arrived_refs[0][...]

        @pl.when(jnp.logical_not(here))
        def keep():
            target_ref[...] = held_ref[...]


def normalised(state, gain_ref):
    mean_square = jnp.mean(state * state, axis=-1, keepdims=True)
    return (state * lax.rsqrt(mean_square + epsilon) * gain_ref[...]).astype(jnp.bfloat16)


def chunk_of(normed, first_ref, second_ref, start, width):
    hidden = jax.nn.gelu(
        jnp.dot(normed, first_ref[:, start : start + width], preferred_element_type=jnp.float32),
        approximate=True,
    ).astype(jnp.bfloat16)
    return jnp.dot(hidden, second_ref[start : start + width, :], preferred_element_type=jnp.float32)


def branch(state, gain_ref, first_ref, second_ref):
    normed = normalised(state, gain_ref)
    total = None
    for start in range(0, first_ref.shape[1], CHUNK):
        part = chunk_of(normed, first_ref, second_ref, start, CHUNK)
        total = part if total is None else total + part
    return total


WHOLE = pl.BlockSpec(memory_space=pltpu.VMEM)
FAR = pl.BlockSpec(memory_space=pltpu.HBM)
TOKEN = jax.ShapeDtypeStruct((8, 128), jnp.float32)


def settings(rows, mebibytes=8):
    return dict(
        compiler_params=pltpu.CompilerParams(vmem_limit_bytes=mebibytes * 2**20),
        cost_estimate=pl.CostEstimate(flops=4 * rows * 1024 * 2048 * 4, bytes_accessed=2**20, transcendentals=0),
    )


def first_kernel(state_hbm, gain_hbm, first_hbm, second_hbm, token_ref, gain_ref, first_ref, second_ref, *refs):
    state_ref, sems = refs[-2:]
    small = [
        pltpu.make_async_copy(state_hbm, state_ref, sems.at[2 * LOADS]),
        pltpu.make_async_copy(gain_hbm, gain_ref, sems.at[2 * LOADS + 1]),
    ]
    for copy in small:
        copy.start()
    width = first_hbm.shape[1] // LOADS
    copies = []
    for k in range(LOADS):
        columns = pl.ds(k * width, width)
        copies.append(pltpu.make_async_copy(first_hbm.at[:, columns], first_ref.at[:, columns], sems.at[2 * k]))
        copies.append(pltpu.make_async_copy(second_hbm.at[columns, :], second_ref.at[columns, :], sems.at[2 * k + 1]))
    for copy in copies:
        copy.start()
    token_ref[...] = jnp.zeros(token_ref.shape, jnp.float32)
    for copy in small:
        copy.wait()
    state = state_ref[...]
    normed = normalised(state, gain_ref)
    update = None
    for k in range(LOADS):
        copies[2 * k].wait()
        copies[2 * k + 1].wait()
        part = chunk_of(normed, first_ref, second_ref, k * width, width)
        update = part if update is None else update + part
    rows = state.shape[0] // PORTIONS
    for portion in range(PORTIONS):
        mine = slice(portion * rows, (portion + 1) * rows)
        for k, spacing in enumerate((1.0, 4.0, 16.0)):
            refs[3 * portion + k][...] = state[mine] + spacing * update[mine]


def first_round(initial, gain, first, second):
    rows = initial.shape[0] // PORTIONS
    block = jax.ShapeDtypeStruct((rows, initial.shape[1]), jnp.float32)
    made = pl.pallas_call(
        first_kernel,
        out_shape=(
            TOKEN,
            jax.ShapeDtypeStruct(gain.shape, gain.dtype),
            jax.ShapeDtypeStruct(first.shape, first.dtype),
            jax.ShapeDtypeStruct(second.shape, second.dtype),
        )
        + (block,) * (3 * PORTIONS),
        in_specs=[FAR] * 4,
        out_specs=(WHOLE,) * (4 + 3 * PORTIONS),
        scratch_shapes=[pltpu.VMEM(initial.shape, jnp.float32), pltpu.SemaphoreType.DMA((2 * LOADS + 2,))],
        **settings(initial.shape[0], 43),
    )(initial, gain, first, second)
    states = [
        dict(zip(("current", "four", "sixteen"), made[4 + 3 * k : 7 + 3 * k])) for k in range(PORTIONS)
    ]
    return made[0], made[1:4], states


def targets(jobs):
    return [n for points in jobs.values() for n in points]


def round_kernel(jobs, more, names_in, names_out, *refs):
    given = dict(zip(names_in, refs))
    made = dict(zip(names_out, refs[len(names_in) :]))
    picked_ref, update_ref = refs[-2:]
    rows = given["arrived"].shape[0]
    place = lax.axis_index("layer").astype(jnp.int32)
    made["token"][...] = given["token"][...]
    doubled = sorted(set(targets(jobs)) & set(targets(more)))
    layer = (given["gain"], given["first"], given["second"])

    if more:

        @pl.when(member(targets(jobs)))
        def pick():
            picked_ref[:rows, :] = given["arrived"][...]

        @pl.when(member(sorted(set(targets(more)) - set(doubled))))
        def pick_other():
            picked_ref[:rows, :] = given["other"][...]

    busy = sorted((set(targets(jobs)) | set(targets(more))) - set(doubled))

    @pl.when(member(busy))
    def compute():
        state = picked_ref[:rows, :] if more else given["arrived"][...]
        update_ref[:rows, :] = branch(state, *layer)

    if doubled:

        @pl.when(member(doubled))
        def compute_both():
            picked_ref[rows:, :] = given["other"][...]
            update_ref[...] = branch(picked_ref[...], *layer)

    both = {job: sorted(jobs.get(job, []) + more.get(job, [])) for job in set(jobs) | set(more)}
    for name, writers in WRITERS.items():
        if name in made and name in given:

            @pl.when(jnp.logical_not(member([n for job in writers for n in both.get(job, ())])))
            def keep(name=name):
                made[name][...] = given[name][...]

    if "sums" in given:
        made["sums"][...] = given["sums"][...]
    elif "sums" in made:
        made["sums"][...] = jnp.zeros(made["sums"].shape, jnp.float32)

    def finish(job, stepped, update):
        if job == FINE:
            made["current"][...] = stepped
        if job == LEVEL:
            made["four"][...] = stepped
            made["current"][...] = stepped + given["coarse"][...]
        if job == GAP_FOUR:
            made["four"][...] = stepped
        if job == GAP_SIXTEEN:
            made["sixteen"][...] = stepped
        if job == COARSEST:
            made["current"][...] = given["current"][...] + (stepped - given["sixteen"][...])
            made["sixteen"][...] = stepped
        if job == RESTRICT:
            gap = stepped - given["current"][...]
            made["current"][...] = stepped
            made["coarse"][...] = stepped - given["four"][...]
            shape = made["sums"].shape
            row = lax.broadcasted_iota(jnp.int32, shape, 0)
            here = lax.broadcasted_iota(jnp.int32, shape, 1) == (place + 1) // 4 - 2
            pair = jnp.where(row == 0, jnp.sum(gap * gap), jnp.sum(update * update))
            made["sums"][...] += jnp.where(here & (row < 2), pair, 0.0)

    for hop, name, start in ((jobs, "arrived", 0), (more, "other", rows)):
        for job, points in hop.items():
            for twice in (False, True):
                mine = [n for n in points if (n in doubled) == twice]
                if mine:

                    @pl.when(member(mine))
                    def done(job=job, name=name, start=start if twice else 0):
                        update = update_ref[start : start + rows, :]
                        finish(job, given[name][...] + SPACING[job] * update, update)


WRITERS = {
    "current": {FINE, LEVEL, RESTRICT, COARSEST},
    "four": {LEVEL, GAP_FOUR},
    "sixteen": {GAP_SIXTEEN, COARSEST},
    "coarse": {RESTRICT},
}
READERS = {
    "current": {FINE, LEVEL, RESTRICT, COARSEST},
    "four": {RESTRICT, LEVEL, GAP_FOUR},
    "sixteen": {GAP_SIXTEEN, COARSEST},
    "coarse": {LEVEL},
}


def by_job(pairs):
    jobs = {}
    for unused, target, job in pairs:
        jobs.setdefault(job, []).append(target)
    return jobs


def run_round(arrivals, state, layer, hops, token, sums):
    jobs, more = by_job(hops[0]), by_job(hops[1] if len(hops) > 1 else [])
    kinds = set(jobs) | set(more)
    names_in = ["arrived", "other"][: len(arrivals)] + ["gain", "first", "second", "token"]
    values = [*arrivals, *layer, token]
    names_out, shapes = ["token"], [TOKEN]
    rows, width = arrivals[0].shape
    block = jax.ShapeDtypeStruct((rows, width), jnp.float32)
    for name, writers in WRITERS.items():
        if name in state and kinds & READERS[name]:
            names_in.append(name)
            values.append(state[name])
        if kinds & writers:
            names_out.append(name)
            shapes.append(block)
    if RESTRICT in kinds:
        if sums is not None:
            names_in.append("sums")
            values.append(sums)
        names_out.append("sums")
        shapes.append(TOKEN)
    scratch = pltpu.VMEM((rows * len(arrivals), width), jnp.float32)
    made = pl.pallas_call(
        functools.partial(round_kernel, jobs, more, names_in, names_out),
        out_shape=tuple(shapes),
        in_specs=[WHOLE] * len(names_in),
        out_specs=(WHOLE,) * len(shapes),
        scratch_shapes=[scratch, scratch],
        **settings(rows),
    )(*values)
    return dict(zip(names_out, made))


def take_kernel(receivers, sums_ref, token_ref, *refs):
    *partner_refs, made_ref, passed_ref = refs
    taken(sums_ref, partner_refs, receivers, made_ref)
    passed_ref[...] = token_ref[...]


def take(sums, partners, token, receivers):
    return pl.pallas_call(
        functools.partial(take_kernel, receivers),
        out_shape=(TOKEN, TOKEN),
        in_specs=[WHOLE] * (2 + len(partners)),
        out_specs=(WHOLE, WHOLE),
        compiler_params=pltpu.CompilerParams(vmem_limit_bytes=8 * 2**20),
    )(sums, token, *partners)


def finish_kernel(receivers, sums_ref, partner_ref, token_ref, *refs):
    given = refs[: 3 * PORTIONS]
    outs = refs[3 * PORTIONS : 3 * PORTIONS + 3]
    ratios_ref, *scratch, total_ref, sems = refs[3 * PORTIONS + 3 :]
    point = lax.axis_index("layer") + 1
    rows = given[0].shape[0]
    copies = []

    def send(source, target, portion):
        block = target.at[0, pl.ds(portion * rows, rows), :]
        copies.append(pltpu.make_async_copy(source, block, sems.at[len(copies)]))
        copies[-1].start()

    for portion in range(PORTIONS):
        send(given[3 * portion], outs[0], portion)
    for portion in range(PORTIONS):
        current, *coarser = given[3 * portion : 3 * portion + 3]
        mine = pl.ds(portion * rows, rows)
        for ref, made, least, out in zip(coarser, scratch, (4, 16), outs[1:]):
            made[mine, :] = jnp.where(point >= least, current[...] - ref[...], 0.0)
            send(made.at[mine, :], out, portion)
    taken(sums_ref, (partner_ref,), receivers, total_ref)
    sums = total_ref[...]
    ratios_ref[...] = jnp.sqrt(sums[0:1] / (sums[1:2] + epsilon))
    for copy in copies:
        copy.wait()


def finish(states, sums, partner, receivers, token):
    rows, width = states[0]["current"].shape
    whole = jax.ShapeDtypeStruct((1, rows * PORTIONS, width), jnp.float32)
    values = [state[name] for state in states for name in ("current", "four", "sixteen")]
    layer_states, defects_four, defects_sixteen, ratios = pl.pallas_call(
        functools.partial(finish_kernel, receivers),
        out_shape=(whole, whole, whole, jax.ShapeDtypeStruct((1, 128), jnp.float32)),
        in_specs=[WHOLE] * (3 + len(values)),
        out_specs=(FAR, FAR, FAR, WHOLE),
        scratch_shapes=[pltpu.VMEM((rows * PORTIONS, width), jnp.float32)] * 2
        + [pltpu.VMEM(sums.shape, jnp.float32), pltpu.SemaphoreType.DMA((3 * PORTIONS,))],
        compiler_params=pltpu.CompilerParams(vmem_limit_bytes=8 * 2**20),
    )(sums, partner, token, *values)
    return layer_states, ratios[0, :7], defects_four, defects_sixteen


def local(initial, norm_gains, first_weights, second_weights):
    layers = lax.axis_size("layer")
    hops, routes, restricted = plan(layers)
    token, layer, states = first_round(initial, norm_gains, first_weights[0], second_weights[0])
    steps = gathering(layers, lax.axis_size("dp"))
    sums = None
    for index in range(max(hops)[0] + 1):
        keys = sorted(key for key in hops if key[0] == index)
        if not keys:
            continue
        for portion in range(PORTIONS):
            if steps and steps[0][0] == (index, portion):
                unused, ways, receivers = steps.pop(0)
                partners = [lax.ppermute(sums, axes, pairs) for axes, pairs in ways]
                sums, token = take(sums, partners, token, receivers)
            current = states[portion]["current"]
            arrivals = [lax.ppermute(current, "layer", [(a - 1, b - 1) for a, b in routes[key]]) for key in keys]
            made = run_round(arrivals, states[portion], layer, [hops[key] for key in keys], token, sums)
            token = made.pop("token")
            sums = made.pop("sums", sums)
            states[portion].update(made)
    ((unused, ((axes, pairs),), receivers),) = steps
    return finish(states, sums, lax.ppermute(sums, axes, pairs), receivers, token)


def solution(mesh):
    placed = (P("dp", None), P("layer", None), P("layer", None, None), P("layer", None, None))
    return jax.shard_map(
        local,
        mesh=mesh,
        in_specs=placed,
        out_specs=(P("layer", "dp", None), P(), P("layer", "dp", None), P("layer", "dp", None)),
        check_vma=False,
    )
```

```python
import functools

import jax
import jax.numpy as jnp
from jax import lax
from jax.experimental import pallas as pl
from jax.experimental.pallas import tpu as pltpu
from jax.sharding import PartitionSpec as P

epsilon = 1e-06
PORTIONS = 2
CHUNK = 1024
LOADS = 4

ADD = "add"
FINE, LEVEL, GAP_FOUR, GAP_SIXTEEN, RESTRICT, COARSEST = 1, 2, 3, 4, 5, 6
SPACING = {FINE: 1.0, LEVEL: 4.0, GAP_FOUR: 4.0, GAP_SIXTEEN: 16.0, RESTRICT: 1.0, COARSEST: 16.0}


def plan(layers):
    def every(residue, shift, job):
        return [(n, n + shift, job) for n in range(1, layers - shift + 1) if n % 4 == residue]

    hops = {
        (0, 0): every(1, 1, FINE),
        (1, 0): every(2, 1, FINE),
        (2, 0): every(3, 1, FINE),
        (3, 0): every(0, 1, FINE) + [(3, 19, GAP_SIXTEEN)],
        (4, 0): every(1, 1, FINE),
        (6, 0): every(2, 1, FINE) + [(16, 32, GAP_SIXTEEN), (4, 20, GAP_SIXTEEN)],
        (6, 1): every(0, 4, GAP_FOUR) + [(2, 18, GAP_SIXTEEN)],
        (7, 0): every(3, 1, RESTRICT),
        (8, 0): [(8, 12, LEVEL), (20, 24, LEVEL), (3, 7, GAP_FOUR), (1, 17, GAP_SIXTEEN)],
        (9, 0): [(12, 16, LEVEL), (24, 28, LEVEL)],
        (10, 0): [(16, 20, LEVEL), (28, 32, LEVEL), (1, 5, GAP_FOUR), (2, 6, GAP_FOUR)],
        (11, 0): [(20, 24, LEVEL)],
        (12, 0): [(24, 28, LEVEL)],
        (12, 1): [(24, 25, FINE)],
        (13, 0): [(28, 29, FINE), (25, 26, FINE), (16, 32, COARSEST)],
        (14, 0): [(29, 30, FINE), (26, 27, FINE)],
        (15, 0): [(30, 31, FINE), (28, 32, GAP_FOUR), (13, 29, GAP_SIXTEEN)],
        (15, 1): [(27, 31, GAP_FOUR), (25, 29, GAP_FOUR), (21, 25, GAP_FOUR)],
    }
    restricted = 7
    like = {(0, 0): (4, 0), (1, 0): (6, 0), (2, 0): (7, 0), (8, 0): (14, 0), (9, 0): (15, 1)}
    closed = {(n, 0) for n in (0, 1, 2, 3, 4, 15)}

    final = {1: -1, 2: 0, 3: 1, 4: 2, 5: 3, 6: 4, 7: 6, 8: 7}
    final.update({12: 8, 16: 9, 20: 10, 24: 11, 28: 12, 32: 13, 25: 12, 26: 13, 27: 14, 29: 13, 30: 14, 31: 15})

    def place(source, target, job, first):
        for key in sorted(hops):
            group = [key] + [k for k in hops if like.get(k) == key or like.get(key) == k]
            if key[0] < first or key in closed or (key == (7, 0) and source == 5):
                continue
            if any(a == source or b == target for k in group for a, b, unused in hops[k]):
                continue
            if any(b == target for k in hops if k[0] == key[0] for unused, b, held in hops[k]):
                continue
            hops[key].append((source, target, job))
            return key[0]
        raise ValueError((source, target, job))

    for anchor in (8, 12, 16, 20):
        for n in (anchor + 1, anchor + 2, anchor + 3):
            final[n] = place(n - 1, n, FINE, max(final[n - 1], restricted) + 1)
    wanted = []
    for n in range(5, layers + 1):
        if n % 4 != 0 and n != 31:
            wanted.append((final[n - 4], n - 4, n, GAP_FOUR))
    for n in range(17, layers):
        if n not in (19, 20):
            wanted.append((final[n - 16], n - 16, n, GAP_SIXTEEN))
    fixed = {(a, b) for pairs in hops.values() for a, b, unused in pairs}
    wanted = [want for want in wanted if want[1:3] not in fixed]
    for ready, source, target, job in sorted(wanted, key=lambda want: (-want[0], want)):
        place(source, target, job, max(13 if target in (24, 28) else 4, ready + 1))

    routes = {key: [(a, b) for a, b, unused in pairs] for key, pairs in hops.items()}
    for key, other in like.items():
        routes[other] = routes[other] + [pair for pair in routes[key] if pair not in routes[other]]
    assert not any(a <= 4 for key, pairs in hops.items() if key[0] > 10 for a, b, unused in pairs)
    for key, other in like.items():
        routes[key] = routes[other]
    return hops, routes, restricted


def gathering(layers, planes):
    def within(pairs):
        return "layer", [(a - 1, b - 1) for a, b in pairs]

    start = [within([(8, 3), (16, 2), (12, 1), (20, 4)]), within([(24, 1), (32, 2), (28, 3)])]
    steps = [((8, 0), start, ADD)]
    for follows, distance in (((8, 1), 1), ((9, 0), 2)):
        steps.append((follows, [within([(n + 1, (n ^ distance) + 1) for n in range(4)])], ADD))
    for follows, distance in (((9, 1), 1), ((10, 0), 2), ((10, 1), 4)):
        pairs = [(n * planes + i, n * planes + (i ^ distance)) for n in range(4) for i in range(planes)]
        steps.append((follows, [(("layer", "dp"), pairs)], ADD))
    for follows, known in (((11, 1), 4), ((14, 0), 8), (None, 16)):
        steps.append((follows, [within([(n, n + known) for n in range(1, known + 1)])], tuple(range(known + 1, 2 * known + 1))))
    assert 2 * known == layers
    return steps


def member(points):
    place = lax.axis_index("layer").astype(jnp.int32)
    mask = 0
    for n in points:
        mask |= 1 << (n - 1)
    if mask >= 2**31:
        mask -= 2**32
    return (lax.shift_right_logical(jnp.int32(mask), place) & 1) == 1


def taken(held_ref, arrived_refs, receivers, target_ref):
    if receivers == ADD:
        total = held_ref[...]
        for ref in arrived_refs:
            total = total + ref[...]
        target_ref[...] = total
    else:
        here = member(receivers)

        @pl.when(here)
        def replace():
            target_ref[...] = arrived_refs[0][...]

        @pl.when(jnp.logical_not(here))
        def keep():
            target_ref[...] = held_ref[...]


def normalised(state, gain_ref):
    mean_square = jnp.mean(state * state, axis=-1, keepdims=True)
    return (state * lax.rsqrt(mean_square + epsilon) * gain_ref[...]).astype(jnp.bfloat16)


def chunk_of(normed, first_ref, second_ref, start, width):
    hidden = jax.nn.gelu(
        jnp.dot(normed, first_ref[:, start : start + width], preferred_element_type=jnp.float32),
        approximate=True,
    ).astype(jnp.bfloat16)
    return jnp.dot(hidden, second_ref[start : start + width, :], preferred_element_type=jnp.float32)


def branch(state, gain_ref, first_ref, second_ref):
    normed = normalised(state, gain_ref)
    total = None
    for start in range(0, first_ref.shape[1], CHUNK):
        part = chunk_of(normed, first_ref, second_ref, start, CHUNK)
        total = part if total is None else total + part
    return total


WHOLE = pl.BlockSpec(memory_space=pltpu.VMEM)
FAR = pl.BlockSpec(memory_space=pltpu.HBM)
TOKEN = jax.ShapeDtypeStruct((8, 128), jnp.float32)


def settings(rows, mebibytes=8):
    return dict(
        compiler_params=pltpu.CompilerParams(vmem_limit_bytes=mebibytes * 2**20),
        cost_estimate=pl.CostEstimate(flops=4 * rows * 1024 * 2048 * 4, bytes_accessed=2**20, transcendentals=0),
    )


def first_kernel(state_hbm, gain_hbm, first_hbm, second_hbm, token_ref, gain_ref, first_ref, second_ref, *refs):
    state_ref, sems = refs[-2:]
    small = [
        pltpu.make_async_copy(state_hbm, state_ref, sems.at[2 * LOADS]),
        pltpu.make_async_copy(gain_hbm, gain_ref, sems.at[2 * LOADS + 1]),
    ]
    for copy in small:
        copy.start()
    width = first_hbm.shape[1] // LOADS
    copies = []
    for k in range(LOADS):
        columns = pl.ds(k * width, width)
        copies.append(pltpu.make_async_copy(first_hbm.at[:, columns], first_ref.at[:, columns], sems.at[2 * k]))
        copies.append(pltpu.make_async_copy(second_hbm.at[columns, :], second_ref.at[columns, :], sems.at[2 * k + 1]))
    for copy in copies:
        copy.start()
    token_ref[...] = jnp.zeros(token_ref.shape, jnp.float32)
    for copy in small:
        copy.wait()
    state = state_ref[...]
    normed = normalised(state, gain_ref)
    update = None
    for k in range(LOADS):
        copies[2 * k].wait()
        copies[2 * k + 1].wait()
        part = chunk_of(normed, first_ref, second_ref, k * width, width)
        update = part if update is None else update + part
    rows = state.shape[0] // PORTIONS
    for portion in range(PORTIONS):
        mine = slice(portion * rows, (portion + 1) * rows)
        for k, spacing in enumerate((1.0, 4.0, 16.0)):
            refs[3 * portion + k][...] = state[mine] + spacing * update[mine]


def first_round(initial, gain, first, second):
    rows = initial.shape[0] // PORTIONS
    block = jax.ShapeDtypeStruct((rows, initial.shape[1]), jnp.float32)
    made = pl.pallas_call(
        first_kernel,
        out_shape=(
            TOKEN,
            jax.ShapeDtypeStruct(gain.shape, gain.dtype),
            jax.ShapeDtypeStruct(first.shape, first.dtype),
            jax.ShapeDtypeStruct(second.shape, second.dtype),
        )
        + (block,) * (3 * PORTIONS),
        in_specs=[FAR] * 4,
        out_specs=(WHOLE,) * (4 + 3 * PORTIONS),
        scratch_shapes=[pltpu.VMEM(initial.shape, jnp.float32), pltpu.SemaphoreType.DMA((2 * LOADS + 2,))],
        **settings(initial.shape[0], 43),
    )(initial, gain, first, second)
    states = [
        dict(zip(("current", "four", "sixteen"), made[4 + 3 * k : 7 + 3 * k])) for k in range(PORTIONS)
    ]
    return made[0], made[1:4], states


def targets(jobs):
    return [n for points in jobs.values() for n in points]


def round_kernel(jobs, more, names_in, names_out, *refs):
    given = dict(zip(names_in, refs))
    made = dict(zip(names_out, refs[len(names_in) :]))
    picked_ref, update_ref = refs[-2:]
    rows = given["arrived"].shape[0]
    place = lax.axis_index("layer").astype(jnp.int32)
    made["token"][...] = given["token"][...]
    doubled = sorted(set(targets(jobs)) & set(targets(more)))
    layer = (given["gain"], given["first"], given["second"])

    if more:

        @pl.when(member(targets(jobs)))
        def pick():
            picked_ref[:rows, :] = given["arrived"][...]

        @pl.when(member(sorted(set(targets(more)) - set(doubled))))
        def pick_other():
            picked_ref[:rows, :] = given["other"][...]

    busy = sorted((set(targets(jobs)) | set(targets(more))) - set(doubled))

    @pl.when(member(busy))
    def compute():
        state = picked_ref[:rows, :] if more else given["arrived"][...]
        update_ref[:rows, :] = branch(state, *layer)

    if doubled:

        @pl.when(member(doubled))
        def compute_both():
            picked_ref[rows:, :] = given["other"][...]
            update_ref[...] = branch(picked_ref[...], *layer)

    both = {job: sorted(jobs.get(job, []) + more.get(job, [])) for job in set(jobs) | set(more)}
    for name, writers in WRITERS.items():
        if name in made and name in given:

            @pl.when(jnp.logical_not(member([n for job in writers for n in both.get(job, ())])))
            def keep(name=name):
                made[name][...] = given[name][...]

    if "sums" in given:
        made["sums"][...] = given["sums"][...]
    elif "sums" in made:
        made["sums"][...] = jnp.zeros(made["sums"].shape, jnp.float32)

    def finish(job, stepped, update):
        if job == FINE:
            made["current"][...] = stepped
        if job == LEVEL:
            made["four"][...] = stepped
            made["current"][...] = stepped + given["coarse"][...]
        if job == GAP_FOUR:
            made["four"][...] = stepped
        if job == GAP_SIXTEEN:
            made["sixteen"][...] = stepped
        if job == COARSEST:
            made["current"][...] = given["current"][...] + (stepped - given["sixteen"][...])
            made["sixteen"][...] = stepped
        if job == RESTRICT:
            gap = stepped - given["current"][...]
            made["current"][...] = stepped
            made["coarse"][...] = stepped - given["four"][...]
            shape = made["sums"].shape
            row = lax.broadcasted_iota(jnp.int32, shape, 0)
            here = lax.broadcasted_iota(jnp.int32, shape, 1) == (place + 1) // 4 - 2
            pair = jnp.where(row == 0, jnp.sum(gap * gap), jnp.sum(update * update))
            made["sums"][...] += jnp.where(here & (row < 2), pair, 0.0)

    for hop, name, start in ((jobs, "arrived", 0), (more, "other", rows)):
        for job, points in hop.items():
            for twice in (False, True):
                mine = [n for n in points if (n in doubled) == twice]
                if mine:

                    @pl.when(member(mine))
                    def done(job=job, name=name, start=start if twice else 0):
                        update = update_ref[start : start + rows, :]
                        finish(job, given[name][...] + SPACING[job] * update, update)


WRITERS = {
    "current": {FINE, LEVEL, RESTRICT, COARSEST},
    "four": {LEVEL, GAP_FOUR},
    "sixteen": {GAP_SIXTEEN, COARSEST},
    "coarse": {RESTRICT},
}
READERS = {
    "current": {FINE, LEVEL, RESTRICT, COARSEST},
    "four": {RESTRICT, LEVEL, GAP_FOUR},
    "sixteen": {GAP_SIXTEEN, COARSEST},
    "coarse": {LEVEL},
}


def by_job(pairs):
    jobs = {}
    for unused, target, job in pairs:
        jobs.setdefault(job, []).append(target)
    return jobs


def run_round(arrivals, state, layer, hops, token, sums):
    jobs, more = by_job(hops[0]), by_job(hops[1] if len(hops) > 1 else [])
    kinds = set(jobs) | set(more)
    names_in = ["arrived", "other"][: len(arrivals)] + ["gain", "first", "second", "token"]
    values = [*arrivals, *layer, token]
    names_out, shapes = ["token"], [TOKEN]
    rows, width = arrivals[0].shape
    block = jax.ShapeDtypeStruct((rows, width), jnp.float32)
    for name, writers in WRITERS.items():
        if name in state and kinds & READERS[name]:
            names_in.append(name)
            values.append(state[name])
        if kinds & writers:
            names_out.append(name)
            shapes.append(block)
    if RESTRICT in kinds:
        if sums is not None:
            names_in.append("sums")
            values.append(sums)
        names_out.append("sums")
        shapes.append(TOKEN)
    scratch = pltpu.VMEM((rows * len(arrivals), width), jnp.float32)
    made = pl.pallas_call(
        functools.partial(round_kernel, jobs, more, names_in, names_out),
        out_shape=tuple(shapes),
        in_specs=[WHOLE] * len(names_in),
        out_specs=(WHOLE,) * len(shapes),
        scratch_shapes=[scratch, scratch],
        **settings(rows),
    )(*values)
    return dict(zip(names_out, made))


def take_kernel(receivers, sums_ref, token_ref, *refs):
    *partner_refs, made_ref, passed_ref = refs
    taken(sums_ref, partner_refs, receivers, made_ref)
    passed_ref[...] = token_ref[...]


def take(sums, partners, token, receivers):
    return pl.pallas_call(
        functools.partial(take_kernel, receivers),
        out_shape=(TOKEN, TOKEN),
        in_specs=[WHOLE] * (2 + len(partners)),
        out_specs=(WHOLE, WHOLE),
        compiler_params=pltpu.CompilerParams(vmem_limit_bytes=8 * 2**20),
    )(sums, token, *partners)


def finish_kernel(receivers, sums_ref, partner_ref, token_ref, *refs):
    given = refs[: 3 * PORTIONS]
    outs = refs[3 * PORTIONS : 3 * PORTIONS + 3]
    ratios_ref, *scratch, total_ref, sems = refs[3 * PORTIONS + 3 :]
    point = lax.axis_index("layer") + 1
    rows = given[0].shape[0]
    copies = []

    def send(source, target, portion):
        block = target.at[0, pl.ds(portion * rows, rows), :]
        copies.append(pltpu.make_async_copy(source, block, sems.at[len(copies)]))
        copies[-1].start()

    for portion in range(PORTIONS):
        send(given[3 * portion], outs[0], portion)
    for portion in range(PORTIONS):
        current, *coarser = given[3 * portion : 3 * portion + 3]
        mine = pl.ds(portion * rows, rows)
        for ref, made, least, out in zip(coarser, scratch, (4, 16), outs[1:]):
            made[mine, :] = jnp.where(point >= least, current[...] - ref[...], 0.0)
            send(made.at[mine, :], out, portion)
    taken(sums_ref, (partner_ref,), receivers, total_ref)
    sums = total_ref[...]
    ratios_ref[...] = jnp.sqrt(sums[0:1] / (sums[1:2] + epsilon))
    for copy in copies:
        copy.wait()


def finish(states, sums, partner, receivers, token):
    rows, width = states[0]["current"].shape
    whole = jax.ShapeDtypeStruct((1, rows * PORTIONS, width), jnp.float32)
    values = [state[name] for state in states for name in ("current", "four", "sixteen")]
    layer_states, defects_four, defects_sixteen, ratios = pl.pallas_call(
        functools.partial(finish_kernel, receivers),
        out_shape=(whole, whole, whole, jax.ShapeDtypeStruct((1, 128), jnp.float32)),
        in_specs=[WHOLE] * (3 + len(values)),
        out_specs=(FAR, FAR, FAR, WHOLE),
        scratch_shapes=[pltpu.VMEM((rows * PORTIONS, width), jnp.float32)] * 2
        + [pltpu.VMEM(sums.shape, jnp.float32), pltpu.SemaphoreType.DMA((3 * PORTIONS,))],
        compiler_params=pltpu.CompilerParams(vmem_limit_bytes=8 * 2**20),
    )(sums, partner, token, *values)
    return layer_states, ratios[0, :7], defects_four, defects_sixteen


def local(initial, norm_gains, first_weights, second_weights):
    layers = lax.axis_size("layer")
    hops, routes, restricted = plan(layers)
    token, layer, states = first_round(initial, norm_gains, first_weights[0], second_weights[0])
    steps = gathering(layers, lax.axis_size("dp"))
    sums = None
    for index in range(max(hops)[0] + 1):
        keys = sorted(key for key in hops if key[0] == index)
        if not keys:
            continue
        for portion in range(PORTIONS):
            if steps and steps[0][0] == (index, portion):
                unused, ways, receivers = steps.pop(0)
                partners = [lax.ppermute(sums, axes, pairs) for axes, pairs in ways]
                sums, token = take(sums, partners, token, receivers)
            current = states[portion]["current"]
            arrivals = [lax.ppermute(current, "layer", [(a - 1, b - 1) for a, b in routes[key]]) for key in keys]
            made = run_round(arrivals, states[portion], layer, [hops[key] for key in keys], token, sums)
            token = made.pop("token")
            sums = made.pop("sums", sums)
            states[portion].update(made)
    ((unused, ((axes, pairs),), receivers),) = steps
    return finish(states, sums, lax.ppermute(sums, axes, pairs), receivers, token)


def solution(mesh):
    placed = (P("dp", None), P("layer", None), P("layer", None, None), P("layer", None, None))
    return jax.shard_map(
        local,
        mesh=mesh,
        in_specs=placed,
        out_specs=(P("layer", "dp", None), P(), P("layer", "dp", None), P("layer", "dp", None)),
        check_vma=False,
    )
```

```python
import functools

import jax
import jax.numpy as jnp
from jax import lax
from jax.experimental import pallas as pl
from jax.experimental.pallas import tpu as pltpu
from jax.sharding import PartitionSpec as P

epsilon = 1e-06
PORTIONS = 2
CHUNK = 1024
LOADS = 4

ADD = "add"
FINE, LEVEL, GAP_FOUR, GAP_SIXTEEN, RESTRICT, COARSEST = 1, 2, 3, 4, 5, 6
SPACING = {FINE: 1.0, LEVEL: 4.0, GAP_FOUR: 4.0, GAP_SIXTEEN: 16.0, RESTRICT: 1.0, COARSEST: 16.0}


def plan(layers):
    def every(residue, shift, job):
        return [(n, n + shift, job) for n in range(1, layers - shift + 1) if n % 4 == residue]

    hops = {
        (0, 0): every(1, 1, FINE),
        (1, 0): every(2, 1, FINE),
        (2, 0): every(3, 1, FINE),
        (3, 0): every(0, 1, FINE) + [(3, 19, GAP_SIXTEEN)],
        (4, 0): every(1, 1, FINE),
        (6, 0): every(2, 1, FINE) + [(16, 32, GAP_SIXTEEN), (4, 20, GAP_SIXTEEN)],
        (6, 1): every(0, 4, GAP_FOUR) + [(2, 18, GAP_SIXTEEN)],
        (7, 0): every(3, 1, RESTRICT),
        (8, 0): [(8, 12, LEVEL), (20, 24, LEVEL), (3, 7, GAP_FOUR), (1, 17, GAP_SIXTEEN)],
        (9, 0): [(12, 16, LEVEL), (24, 28, LEVEL)],
        (10, 0): [(16, 20, LEVEL), (28, 32, LEVEL), (1, 5, GAP_FOUR), (2, 6, GAP_FOUR), (8, 24, GAP_SIXTEEN)],
        (11, 0): [(20, 24, LEVEL)],
        (12, 0): [(24, 28, LEVEL)],
        (12, 1): [(24, 25, FINE)],
        (13, 0): [(28, 29, FINE), (25, 26, FINE), (16, 32, COARSEST)],
        (14, 0): [(29, 30, FINE), (26, 27, FINE)],
        (15, 0): [(30, 31, FINE), (28, 32, GAP_FOUR), (13, 29, GAP_SIXTEEN)],
        (15, 1): [(27, 31, GAP_FOUR), (25, 29, GAP_FOUR), (21, 25, GAP_FOUR)],
    }
    restricted = 7
    like = {(0, 0): (4, 0), (1, 0): (6, 0), (2, 0): (7, 0), (8, 0): (14, 0), (9, 0): (15, 1)}
    closed = {(n, 0) for n in (0, 1, 2, 3, 4, 15)}

    final = {1: -1, 2: 0, 3: 1, 4: 2, 5: 3, 6: 4, 7: 6, 8: 7}
    final.update({12: 8, 16: 9, 20: 10, 24: 11, 28: 12, 32: 13, 25: 12, 26: 13, 27: 14, 29: 13, 30: 14, 31: 15})

    def place(source, target, job, first):
        for key in sorted(hops):
            group = [key] + [k for k in hops if like.get(k) == key or like.get(key) == k]
            if key[0] < first or key in closed or (key == (7, 0) and source == 5):
                continue
            if any(a == source or b == target for k in group for a, b, unused in hops[k]):
                continue
            if any(b == target for k in hops if k[0] == key[0] for unused, b, held in hops[k]):
                continue
            hops[key].append((source, target, job))
            return key[0]
        raise ValueError((source, target, job))

    for anchor in (8, 12, 16, 20):
        for n in (anchor + 1, anchor + 2, anchor + 3):
            final[n] = place(n - 1, n, FINE, max(final[n - 1], restricted) + 1)
    wanted = []
    for n in range(5, layers + 1):
        if n % 4 != 0 and n != 31:
            wanted.append((final[n - 4], n - 4, n, GAP_FOUR))
    for n in range(17, layers):
        if n not in (19, 20):
            wanted.append((final[n - 16], n - 16, n, GAP_SIXTEEN))
    fixed = {(a, b) for pairs in hops.values() for a, b, unused in pairs}
    wanted = [want for want in wanted if want[1:3] not in fixed]
    for ready, source, target, job in sorted(wanted, key=lambda want: (-want[0], want)):
        place(source, target, job, max(13 if target in (24, 28) else 4, ready + 1))

    routes = {key: [(a, b) for a, b, unused in pairs] for key, pairs in hops.items()}
    for key, other in like.items():
        routes[other] = routes[other] + [pair for pair in routes[key] if pair not in routes[other]]
    assert not any(a <= 4 for key, pairs in hops.items() if key[0] > 10 for a, b, unused in pairs)
    for key, other in like.items():
        routes[key] = routes[other]
    return hops, routes, restricted


def gathering(layers, planes):
    def within(pairs):
        return "layer", [(a - 1, b - 1) for a, b in pairs]

    start = [within([(8, 3), (16, 2), (12, 1), (20, 4)]), within([(24, 1), (32, 2), (28, 3)])]
    steps = [((8, 0), start, ADD)]
    for follows, distance in (((8, 1), 1), ((9, 0), 2)):
        steps.append((follows, [within([(n + 1, (n ^ distance) + 1) for n in range(4)])], ADD))
    for follows, distance in (((9, 1), 1), ((10, 0), 2), ((10, 1), 4)):
        pairs = [(n * planes + i, n * planes + (i ^ distance)) for n in range(4) for i in range(planes)]
        steps.append((follows, [(("layer", "dp"), pairs)], ADD))
    for follows, known in (((11, 1), 4), ((14, 0), 8), (None, 16)):
        steps.append((follows, [within([(n, n + known) for n in range(1, known + 1)])], tuple(range(known + 1, 2 * known + 1))))
    assert 2 * known == layers
    return steps


def member(points):
    place = lax.axis_index("layer").astype(jnp.int32)
    mask = 0
    for n in points:
        mask |= 1 << (n - 1)
    if mask >= 2**31:
        mask -= 2**32
    return (lax.shift_right_logical(jnp.int32(mask), place) & 1) == 1


def taken(held_ref, arrived_refs, receivers, target_ref):
    if receivers == ADD:
        total = held_ref[...]
        for ref in arrived_refs:
            total = total + ref[...]
        target_ref[...] = total
    else:
        here = member(receivers)

        @pl.when(here)
        def replace():
            target_ref[...] = arrived_refs[0][...]

        @pl.when(jnp.logical_not(here))
        def keep():
            target_ref[...] = held_ref[...]


def normalised(state, gain_ref):
    mean_square = jnp.mean(state * state, axis=-1, keepdims=True)
    return (state * lax.rsqrt(mean_square + epsilon) * gain_ref[...]).astype(jnp.bfloat16)


def chunk_of(normed, first_ref, second_ref, start, width):
    hidden = jax.nn.gelu(
        jnp.dot(normed, first_ref[:, start : start + width], preferred_element_type=jnp.float32),
        approximate=True,
    ).astype(jnp.bfloat16)
    return jnp.dot(hidden, second_ref[start : start + width, :], preferred_element_type=jnp.float32)


def branch(state, gain_ref, first_ref, second_ref):
    normed = normalised(state, gain_ref)
    total = None
    for start in range(0, first_ref.shape[1], CHUNK):
        part = chunk_of(normed, first_ref, second_ref, start, CHUNK)
        total = part if total is None else total + part
    return total


WHOLE = pl.BlockSpec(memory_space=pltpu.VMEM)
FAR = pl.BlockSpec(memory_space=pltpu.HBM)
TOKEN = jax.ShapeDtypeStruct((8, 128), jnp.float32)


def settings(rows, mebibytes=8):
    return dict(
        compiler_params=pltpu.CompilerParams(vmem_limit_bytes=mebibytes * 2**20),
        cost_estimate=pl.CostEstimate(flops=4 * rows * 1024 * 2048 * 4, bytes_accessed=2**20, transcendentals=0),
    )


def first_kernel(state_hbm, gain_hbm, first_hbm, second_hbm, token_ref, gain_ref, first_ref, second_ref, *refs):
    state_ref, sems = refs[-2:]
    small = [
        pltpu.make_async_copy(state_hbm, state_ref, sems.at[2 * LOADS]),
        pltpu.make_async_copy(gain_hbm, gain_ref, sems.at[2 * LOADS + 1]),
    ]
    for copy in small:
        copy.start()
    width = first_hbm.shape[1] // LOADS
    copies = []
    for k in range(LOADS):
        columns = pl.ds(k * width, width)
        copies.append(pltpu.make_async_copy(first_hbm.at[:, columns], first_ref.at[:, columns], sems.at[2 * k]))
        copies.append(pltpu.make_async_copy(second_hbm.at[columns, :], second_ref.at[columns, :], sems.at[2 * k + 1]))
    for copy in copies:
        copy.start()
    token_ref[...] = jnp.zeros(token_ref.shape, jnp.float32)
    for copy in small:
        copy.wait()
    state = state_ref[...]
    normed = normalised(state, gain_ref)
    update = None
    for k in range(LOADS):
        copies[2 * k].wait()
        copies[2 * k + 1].wait()
        part = chunk_of(normed, first_ref, second_ref, k * width, width)
        update = part if update is None else update + part
    rows = state.shape[0] // PORTIONS
    for portion in range(PORTIONS):
        mine = slice(portion * rows, (portion + 1) * rows)
        for k, spacing in enumerate((1.0, 4.0, 16.0)):
            refs[3 * portion + k][...] = state[mine] + spacing * update[mine]


def first_round(initial, gain, first, second):
    rows = initial.shape[0] // PORTIONS
    block = jax.ShapeDtypeStruct((rows, initial.shape[1]), jnp.float32)
    made = pl.pallas_call(
        first_kernel,
        out_shape=(
            TOKEN,
            jax.ShapeDtypeStruct(gain.shape, gain.dtype),
            jax.ShapeDtypeStruct(first.shape, first.dtype),
            jax.ShapeDtypeStruct(second.shape, second.dtype),
        )
        + (block,) * (3 * PORTIONS),
        in_specs=[FAR] * 4,
        out_specs=(WHOLE,) * (4 + 3 * PORTIONS),
        scratch_shapes=[pltpu.VMEM(initial.shape, jnp.float32), pltpu.SemaphoreType.DMA((2 * LOADS + 2,))],
        **settings(initial.shape[0], 43),
    )(initial, gain, first, second)
    states = [
        dict(zip(("current", "four", "sixteen"), made[4 + 3 * k : 7 + 3 * k])) for k in range(PORTIONS)
    ]
    return made[0], made[1:4], states


def targets(jobs):
    return [n for points in jobs.values() for n in points]


def round_kernel(jobs, more, names_in, names_out, *refs):
    given = dict(zip(names_in, refs))
    made = dict(zip(names_out, refs[len(names_in) :]))
    picked_ref, update_ref = refs[-2:]
    rows = given["arrived"].shape[0]
    place = lax.axis_index("layer").astype(jnp.int32)
    made["token"][...] = given["token"][...]
    doubled = sorted(set(targets(jobs)) & set(targets(more)))
    layer = (given["gain"], given["first"], given["second"])

    if more:

        @pl.when(member(targets(jobs)))
        def pick():
            picked_ref[:rows, :] = given["arrived"][...]

        @pl.when(member(sorted(set(targets(more)) - set(doubled))))
        def pick_other():
            picked_ref[:rows, :] = given["other"][...]

    busy = sorted((set(targets(jobs)) | set(targets(more))) - set(doubled))

    @pl.when(member(busy))
    def compute():
        state = picked_ref[:rows, :] if more else given["arrived"][...]
        update_ref[:rows, :] = branch(state, *layer)

    if doubled:

        @pl.when(member(doubled))
        def compute_both():
            picked_ref[rows:, :] = given["other"][...]
            update_ref[...] = branch(picked_ref[...], *layer)

    both = {job: sorted(jobs.get(job, []) + more.get(job, [])) for job in set(jobs) | set(more)}
    for name, writers in WRITERS.items():
        if name in made and name in given:

            @pl.when(jnp.logical_not(member([n for job in writers for n in both.get(job, ())])))
            def keep(name=name):
                made[name][...] = given[name][...]

    if "sums" in given:
        made["sums"][...] = given["sums"][...]
    elif "sums" in made:
        made["sums"][...] = jnp.zeros(made["sums"].shape, jnp.float32)

    def finish(job, stepped, update):
        if job == FINE:
            made["current"][...] = stepped
        if job == LEVEL:
            made["four"][...] = stepped
            made["current"][...] = stepped + given["coarse"][...]
        if job == GAP_FOUR:
            made["four"][...] = stepped
        if job == GAP_SIXTEEN:
            made["sixteen"][...] = stepped
        if job == COARSEST:
            made["current"][...] = given["current"][...] + (stepped - given["sixteen"][...])
            made["sixteen"][...] = stepped
        if job == RESTRICT:
            gap = stepped - given["current"][...]
            made["current"][...] = stepped
            made["coarse"][...] = stepped - given["four"][...]
            shape = made["sums"].shape
            row = lax.broadcasted_iota(jnp.int32, shape, 0)
            here = lax.broadcasted_iota(jnp.int32, shape, 1) == (place + 1) // 4 - 2
            pair = jnp.where(row == 0, jnp.sum(gap * gap), jnp.sum(update * update))
            made["sums"][...] += jnp.where(here & (row < 2), pair, 0.0)

    for hop, name, start in ((jobs, "arrived", 0), (more, "other", rows)):
        for job, points in hop.items():
            for twice in (False, True):
                mine = [n for n in points if (n in doubled) == twice]
                if mine:

                    @pl.when(member(mine))
                    def done(job=job, name=name, start=start if twice else 0):
                        update = update_ref[start : start + rows, :]
                        finish(job, given[name][...] + SPACING[job] * update, update)


WRITERS = {
    "current": {FINE, LEVEL, RESTRICT, COARSEST},
    "four": {LEVEL, GAP_FOUR},
    "sixteen": {GAP_SIXTEEN, COARSEST},
    "coarse": {RESTRICT},
}
READERS = {
    "current": {FINE, LEVEL, RESTRICT, COARSEST},
    "four": {RESTRICT, LEVEL, GAP_FOUR},
    "sixteen": {GAP_SIXTEEN, COARSEST},
    "coarse": {LEVEL},
}


def by_job(pairs):
    jobs = {}
    for unused, target, job in pairs:
        jobs.setdefault(job, []).append(target)
    return jobs


def run_round(arrivals, state, layer, hops, token, sums):
    jobs, more = by_job(hops[0]), by_job(hops[1] if len(hops) > 1 else [])
    kinds = set(jobs) | set(more)
    names_in = ["arrived", "other"][: len(arrivals)] + ["gain", "first", "second", "token"]
    values = [*arrivals, *layer, token]
    names_out, shapes = ["token"], [TOKEN]
    rows, width = arrivals[0].shape
    block = jax.ShapeDtypeStruct((rows, width), jnp.float32)
    for name, writers in WRITERS.items():
        if name in state and kinds & READERS[name]:
            names_in.append(name)
            values.append(state[name])
        if kinds & writers:
            names_out.append(name)
            shapes.append(block)
    if RESTRICT in kinds:
        if sums is not None:
            names_in.append("sums")
            values.append(sums)
        names_out.append("sums")
        shapes.append(TOKEN)
    scratch = pltpu.VMEM((rows * len(arrivals), width), jnp.float32)
    made = pl.pallas_call(
        functools.partial(round_kernel, jobs, more, names_in, names_out),
        out_shape=tuple(shapes),
        in_specs=[WHOLE] * len(names_in),
        out_specs=(WHOLE,) * len(shapes),
        scratch_shapes=[scratch, scratch],
        **settings(rows),
    )(*values)
    return dict(zip(names_out, made))


def take_kernel(receivers, sums_ref, token_ref, *refs):
    *partner_refs, made_ref, passed_ref = refs
    taken(sums_ref, partner_refs, receivers, made_ref)
    passed_ref[...] = token_ref[...]


def take(sums, partners, token, receivers):
    return pl.pallas_call(
        functools.partial(take_kernel, receivers),
        out_shape=(TOKEN, TOKEN),
        in_specs=[WHOLE] * (2 + len(partners)),
        out_specs=(WHOLE, WHOLE),
        compiler_params=pltpu.CompilerParams(vmem_limit_bytes=8 * 2**20),
    )(sums, token, *partners)


def finish_kernel(receivers, sums_ref, partner_ref, token_ref, *refs):
    given = refs[: 3 * PORTIONS]
    outs = refs[3 * PORTIONS : 3 * PORTIONS + 3]
    ratios_ref, *scratch, total_ref, sems = refs[3 * PORTIONS + 3 :]
    point = lax.axis_index("layer") + 1
    rows = given[0].shape[0]
    copies = []

    def send(source, target, portion):
        block = target.at[0, pl.ds(portion * rows, rows), :]
        copies.append(pltpu.make_async_copy(source, block, sems.at[len(copies)]))
        copies[-1].start()

    for portion in range(PORTIONS):
        send(given[3 * portion], outs[0], portion)
    for portion in range(PORTIONS):
        current, *coarser = given[3 * portion : 3 * portion + 3]
        mine = pl.ds(portion * rows, rows)
        for ref, made, least, out in zip(coarser, scratch, (4, 16), outs[1:]):
            made[mine, :] = jnp.where(point >= least, current[...] - ref[...], 0.0)
            send(made.at[mine, :], out, portion)
    taken(sums_ref, (partner_ref,), receivers, total_ref)
    sums = total_ref[...]
    ratios_ref[...] = jnp.sqrt(sums[0:1] / (sums[1:2] + epsilon))
    for copy in copies:
        copy.wait()


def finish(states, sums, partner, receivers, token):
    rows, width = states[0]["current"].shape
    whole = jax.ShapeDtypeStruct((1, rows * PORTIONS, width), jnp.float32)
    values = [state[name] for state in states for name in ("current", "four", "sixteen")]
    layer_states, defects_four, defects_sixteen, ratios = pl.pallas_call(
        functools.partial(finish_kernel, receivers),
        out_shape=(whole, whole, whole, jax.ShapeDtypeStruct((1, 128), jnp.float32)),
        in_specs=[WHOLE] * (3 + len(values)),
        out_specs=(FAR, FAR, FAR, WHOLE),
        scratch_shapes=[pltpu.VMEM((rows * PORTIONS, width), jnp.float32)] * 2
        + [pltpu.VMEM(sums.shape, jnp.float32), pltpu.SemaphoreType.DMA((3 * PORTIONS,))],
        compiler_params=pltpu.CompilerParams(vmem_limit_bytes=8 * 2**20),
    )(sums, partner, token, *values)
    return layer_states, ratios[0, :7], defects_four, defects_sixteen


def local(initial, norm_gains, first_weights, second_weights):
    layers = lax.axis_size("layer")
    hops, routes, restricted = plan(layers)
    token, layer, states = first_round(initial, norm_gains, first_weights[0], second_weights[0])
    steps = gathering(layers, lax.axis_size("dp"))
    sums = None
    for index in range(max(hops)[0] + 1):
        keys = sorted(key for key in hops if key[0] == index)
        if not keys:
            continue
        for portion in range(PORTIONS):
            if steps and steps[0][0] == (index, portion):
                unused, ways, receivers = steps.pop(0)
                partners = [lax.ppermute(sums, axes, pairs) for axes, pairs in ways]
                sums, token = take(sums, partners, token, receivers)
            current = states[portion]["current"]
            arrivals = [lax.ppermute(current, "layer", [(a - 1, b - 1) for a, b in routes[key]]) for key in keys]
            made = run_round(arrivals, states[portion], layer, [hops[key] for key in keys], token, sums)
            token = made.pop("token")
            sums = made.pop("sums", sums)
            states[portion].update(made)
    ((unused, ((axes, pairs),), receivers),) = steps
    return finish(states, sums, lax.ppermute(sums, axes, pairs), receivers, token)


def solution(mesh):
    placed = (P("dp", None), P("layer", None), P("layer", None, None), P("layer", None, None))
    return jax.shard_map(
        local,
        mesh=mesh,
        in_specs=placed,
        out_specs=(P("layer", "dp", None), P(), P("layer", "dp", None), P("layer", "dp", None)),
        check_vma=False,
    )
```
